32 devices in a mesh: section: 2 (over y), dp: 16 (over z, x, core).
Axes of the slice: x: 2, y: 2, z: 4, core: 2. Of those that a mesh axis runs over, the one named last changes fastest.
Arguments:
- tokens: bfloat16 [16384, 768], P('dp'), may hold values from -6 to 6
- cotangent: bfloat16 [16384, 768], P('dp'), may hold values from -6 to 6
- segment_ids: int32 [32, 512], P('dp'), may hold values from 0 to 3, as said below
- valid_mask: int32 [32, 512], P('dp'), may hold values from 0 to 1, as said below
- cluster_perm: int32 [2, 32, 12, 512], P('section', 'dp'), may hold values from 0 to 511, as said below
- query_weight: bfloat16 [2, 768, 768], P('section'), may hold values from -0.21875 to 0.21875
- query_bias: bfloat16 [2, 768], P('section'), may hold values from -3 to 3
- key_weight: bfloat16 [2, 768, 768], P('section'), may hold values from -0.21875 to 0.21875
- value_weight: bfloat16 [2, 768, 768], P('section'), may hold values from -0.21875 to 0.21875
- value_bias: bfloat16 [2, 768], P('section'), may hold values from -1.75 to 1.75
- output_weight: bfloat16 [2, 768, 768], P('section'), may hold values from -0.625 to 0.625
- output_bias: bfloat16 [2, 768], P('section'), may hold values from -1.75 to 1.75
- attention_gain: bfloat16 [2, 768], P('section'), may hold values from 0.5 to 1.5
- attention_shift: bfloat16 [2, 768], P('section'), may hold values from -1.75 to 1.75
- up_weight: bfloat16 [2, 768, 3072], P('section'), may hold values from -0.21875 to 0.21875
- up_bias: bfloat16 [2, 3072], P('section'), may hold values from -1.75 to 1.75
- down_weight: bfloat16 [2, 3072, 768], P('section'), may hold values from -0.109375 to 0.109375
- down_bias: bfloat16 [2, 768], P('section'), may hold values from -1.75 to 1.75
- final_gain: bfloat16 [2, 768], P('section'), may hold values from 0.5 to 1.5
- final_shift: bfloat16 [2, 768], P('section'), may hold values from -1.75 to 1.75
Outputs:
- block_output: bfloat16 [16384, 768], P('dp', 'section')
- input_gradient: bfloat16 [16384, 768], P('dp', 'section')
- query_weight_gradient: float32 [2, 768, 768], P('section', 'dp')
- query_bias_gradient: float32 [2, 768], P('section', 'dp')
- key_weight_gradient: float32 [2, 768, 768], P('section', 'dp')
- value_weight_gradient: float32 [2, 768, 768], P('section', 'dp')
- value_bias_gradient: float32 [2, 768], P('section', 'dp')
- output_weight_gradient: float32 [2, 768, 768], P('section', 'dp')
- output_bias_gradient: float32 [2, 768], P('section', 'dp')
- attention_gain_gradient: float32 [2, 768], P('section', 'dp')
- attention_shift_gradient: float32 [2, 768], P('section', 'dp')
- up_weight_gradient: float32 [2, 768, 3072], P('section', 'dp')
- up_bias_gradient: float32 [2, 3072], P('section', 'dp')
- down_weight_gradient: float32 [2, 3072, 768], P('section', 'dp')
- down_bias_gradient: float32 [2, 768], P('section', 'dp')
- final_gain_gradient: float32 [2, 768], P('section', 'dp')
- final_shift_gradient: float32 [2, 768], P('section', 'dp')
- root_means: float32 [2, 3], P('section')
The draws below stay inside these ranges and needn't reach their ends.
Inputs may be any that keep to these rules, and one draw needn't show every extreme that they name: `segment_ids`: along each row the ids start at 0 and never fall, rising by at most one from a position to the next; equal ids mark one document, and every row holds exactly 4 documents. `valid_mask`: in each row the valid tokens are a prefix of 170 tokens or more. `cluster_perm`: for each layer, row and head, a permutation of the row's 512 positions.
All inputs are finite; a program needn't handle non-finite values.
Results may differ from the reference program's by a relative error of at most 0.025.
Values may be sent and summed in bfloat16 or wider, within the bound.
No kernel may reach another device: no remote copies, remote signals or barrier semaphores. Data moves between devices by JAX's collectives and lax.ppermute only.
A program may use at most 448 MiB of HBM per device.

```python
import math
import jax
import jax.numpy as jnp
from jax import lax

D = 768
FF = 3072
HEADS = 12
HEAD_DIM = 64
CLUSTER = 128
SEQ = 512
LAYERS = 2
ROWS = 32
TOKENS = 16384


def draw_segment_ids(key, part):
    key = jax.random.fold_in(key, 11)
    noise = jax.random.randint(key, (ROWS, SEQ - 1), 0, 1048576)
    ranking = noise * SEQ + jnp.arange(SEQ - 1, dtype=jnp.int32)[None, :]
    chosen = jnp.argsort(ranking, axis=1)[:, :3].astype(jnp.int32) + 1
    column = jnp.arange(SEQ, dtype=jnp.int32)
    starts = jnp.any(column[None, None, :] == chosen[:, :, None], axis=1)
    return jnp.cumsum(starts.astype(jnp.int32), axis=1).astype(jnp.int32)


def draw_valid_mask(key, part):
    key = jax.random.fold_in(key, 12)
    row_index = jnp.arange(ROWS, dtype=jnp.int32)
    least = SEQ // 3
    rising = least + (SEQ - least) * row_index // max(ROWS - 1, 1)
    jitter = jax.random.randint(key, (ROWS,), 0, SEQ // 16 + 1)
    length = jnp.maximum(rising - jitter, least)
    column = jnp.arange(SEQ, dtype=jnp.int32)[None, :]
    return (column < length[:, None]).astype(jnp.int32)


def draw_cluster_perm(key, part):
    key = jax.random.fold_in(key, 13)
    noise = jax.random.randint(key, (LAYERS, ROWS, HEADS, SEQ), 0, 1048576)
    ranking = noise * SEQ + jnp.arange(SEQ, dtype=jnp.int32)
    return jnp.argsort(ranking, axis=-1).astype(jnp.int32)


def raised(drawn, stream_key, source, target, parts, factor):
    owner, partner = [(jnp.arange(drawn.shape[axis_at]) // (drawn.shape[axis_at] // parts)).reshape([-1 if axis == axis_at else 1 for axis in range(drawn.ndim)]) for axis_at in (source, target)]
    chosen = jax.random.permutation(stream_key, parts)[partner]
    strong = (owner == chosen) | (owner == (partner + parts // 2) % parts)
    return jnp.where(strong, factor * drawn, drawn)


def levels(own_key, shape, split, smallest, top_value):
    loudness = 1.0
    for position, parts in split:
        steps = jax.random.uniform(jax.random.fold_in(jax.random.fold_in(own_key, 6), position), (parts,), jnp.float32, smallest / len(split), top_value / len(split))
        loudness = loudness * jnp.repeat(jnp.exp(steps), shape[position] // parts).reshape((-1,) + (1,) * (len(shape) - 1 - position))
    return loudness


def gaussian(own_key, shape, scale, most, pieces=(), kind=jnp.bfloat16):
    loudness = levels(own_key, shape, pieces, -0.22, 0.18) if pieces else 1.0
    values = jax.random.normal(own_key, shape, jnp.float32) * scale * loudness
    return jnp.minimum(jnp.maximum(values, -most), most).astype(kind)


def gaussian_with(rng, shape, deviation, reach, pieces, heavy, kind=jnp.bfloat16):
    array = deviation * jax.random.normal(rng, shape, jnp.float32)
    if pieces:
        array = array * levels(rng, shape, pieces, -0.22, 0.18)
    return jnp.clip(raised(array, jax.random.fold_in(rng, 3), *heavy), -reach, reach).astype(kind)


def setup_inputs(seed: int = 0) -> dict:
    arg_keys = jax.random.split(jax.random.key(seed), 21)
    tokens = gaussian(arg_keys[0], (TOKENS, D), 1.0, 6.0, ((0, 16),))
    cotangent = gaussian_with(arg_keys[1], (TOKENS, D), 1.0, 6.0, ((0, 16),), (0, 1, 16, 2.0))
    segment_ids = draw_segment_ids(jax.random.fold_in(arg_keys[20], 71), 0)
    valid_mask = draw_valid_mask(jax.random.fold_in(arg_keys[20], 71), 0)
    cluster_perm = draw_cluster_perm(jax.random.fold_in(arg_keys[20], 71), 0)
    query_weight = gaussian(arg_keys[5], (LAYERS, D, D), D ** -0.5, 0.21875, ((0, 2),))
    query_bias = gaussian(arg_keys[6], (LAYERS, D), 0.5, 3.0, ((0, 2),))
    key_weight = gaussian(arg_keys[7], (LAYERS, D, D), D ** -0.5, 0.21875, ((0, 2),))
    value_weight = gaussian(arg_keys[8], (LAYERS, D, D), D ** -0.5, 0.21875, ((0, 2),))
    value_bias = gaussian(arg_keys[9], (LAYERS, D), 0.3, 1.75, ((0, 2),))
    output_weight = gaussian(arg_keys[10], (LAYERS, D, D), (D // 8) ** -0.5, 0.625, ((0, 2),))
    output_bias = gaussian(arg_keys[11], (LAYERS, D), 0.3, 1.75, ((0, 2),))
    attention_gain = jnp.clip(1.0 + 0.1 * jax.random.normal(arg_keys[12], (LAYERS, D), jnp.float32), 0.5, 1.5).astype(jnp.bfloat16)
    attention_shift = gaussian(arg_keys[13], (LAYERS, D), 0.3, 1.75, ((0, 2),))
    up_weight = gaussian(arg_keys[14], (LAYERS, D, FF), D ** -0.5, 0.21875, ((0, 2),))
    up_bias = gaussian(arg_keys[15], (LAYERS, FF), 0.3, 1.75, ((0, 2),))
    down_weight = gaussian(arg_keys[16], (LAYERS, FF, D), FF ** -0.5, 0.109375, ((0, 2),))
    down_bias = gaussian(arg_keys[17], (LAYERS, D), 0.3, 1.75, ((0, 2),))
    final_gain = jnp.clip(1.0 + 0.1 * jax.random.normal(arg_keys[18], (LAYERS, D), jnp.float32), 0.5, 1.5).astype(jnp.bfloat16)
    final_shift = gaussian(arg_keys[19], (LAYERS, D), 0.3, 1.75, ((0, 2),))
    return dict(tokens=tokens, cotangent=cotangent, segment_ids=segment_ids, valid_mask=valid_mask, cluster_perm=cluster_perm, query_weight=query_weight, query_bias=query_bias, key_weight=key_weight, value_weight=value_weight, value_bias=value_bias, output_weight=output_weight, output_bias=output_bias, attention_gain=attention_gain, attention_shift=attention_shift, up_weight=up_weight, up_bias=up_bias, down_weight=down_weight, down_bias=down_bias, final_gain=final_gain, final_shift=final_shift)


@jax.custom_vjp
def low(v):
    return lax.optimization_barrier(v.astype(jnp.bfloat16)).astype(jnp.float32)

@jax.custom_vjp
def low_back(v):
    return v

def low_keep(v):
    return (low(v), None)

def low_pass(kept, grad):
    return (grad,)

def back_keep(v):
    return (v, None)

def back_low(kept, grad):
    return (low(grad),)
low.defvjp(low_keep, low_pass)
low_back.defvjp(back_keep, back_low)

def product(left, right):
    return jnp.dot(left, right, precision=lax.Precision.HIGHEST)

def layer_norm(residual, norm_gain, norm_shift):
    centre = residual - lax.optimization_barrier(jnp.mean(residual, axis=-1, keepdims=True))
    spread = lax.optimization_barrier(jnp.mean(centre * centre, axis=-1, keepdims=True))
    return centre * lax.rsqrt(spread + 1e-05) * norm_gain + norm_shift

def heads_of(field):
    row_count = field.shape[0]
    return field.reshape(row_count, SEQ, HEADS, HEAD_DIM).transpose(0, 2, 1, 3)

def attend(queries, key_rows, value_rows, orders, segment, valid):
    row_count = queries.shape[0]
    blocks = SEQ // CLUSTER
    index = orders[..., None]

    def arrange(field):
        picked = jnp.take_along_axis(heads_of(field), index, axis=2)
        return picked.reshape(row_count, HEADS, blocks, CLUSTER, HEAD_DIM)
    sorted_query = arrange(queries)
    sorted_key = arrange(key_rows)
    sorted_value = arrange(value_rows)
    mask_shape = (row_count, HEADS, blocks, CLUSTER)
    seg_sorted = jnp.take_along_axis(jnp.broadcast_to(segment[:, None, :], orders.shape), orders, axis=2).reshape(mask_shape)
    live_sorted = jnp.take_along_axis(jnp.broadcast_to(valid[:, None, :], orders.shape), orders, axis=2).reshape(mask_shape)
    same_doc = seg_sorted[..., :, None] == seg_sorted[..., None, :]
    allowed = same_doc & (live_sorted[..., None, :] == 1) | jnp.eye(CLUSTER, dtype=bool)
    scores = low_back(jnp.einsum('rhcqd,rhckd->rhcqk', sorted_query, sorted_key, precision=lax.Precision.HIGHEST) * HEAD_DIM ** (-0.5))
    probabilities = jax.nn.softmax(jnp.where(allowed, scores, -1000000000.0), axis=-1)
    mixed_values = jnp.einsum('rhcqk,rhckd->rhcqd', low(probabilities), sorted_value, precision=lax.Precision.HIGHEST)
    mixed_values = mixed_values.reshape(row_count, HEADS, SEQ, HEAD_DIM)
    inverse = jnp.argsort(orders, axis=-1).astype(jnp.int32)
    back_order = jnp.take_along_axis(mixed_values, inverse[..., None], axis=2)
    return back_order.transpose(0, 2, 1, 3).reshape(row_count, SEQ, HEADS * HEAD_DIM)

def one_layer(inputs, params, orders, segment, valid):
    w_query, b_query, w_key, w_value, b_value, w_output, b_output, gain_one, shift_one, w_upper, b_upper, w_lower, b_lower, gain_two, shift_two = params
    queries = low(low_back(product(inputs, w_query) + b_query))
    key_rows = low(low_back(product(inputs, w_key)))
    value_rows = low(low_back(product(inputs, w_value) + b_value))
    context = low(low_back(attend(queries, key_rows, value_rows, orders, segment, valid)))
    branch = low_back(product(context, w_output) + b_output)
    hidden = layer_norm(inputs + branch, gain_one, shift_one)
    upper = low_back(product(low(hidden), w_upper) + b_upper)
    active = low(jax.nn.gelu(upper, approximate=False))
    feed = low_back(product(active, w_lower) + b_lower)
    result = layer_norm(hidden + feed, gain_two, shift_two)
    live = valid.astype(jnp.float32)[..., None]
    stats = jnp.stack([jnp.sum(live * branch * branch), jnp.sum(live * feed * feed), jnp.sum(live * result * result)])
    return (result, stats)

def two_layers(inputs, params, orders, segment, valid):
    first_params = tuple((tensor[0] for tensor in params))
    second_params = tuple((tensor[1] for tensor in params))
    middle, stats_first = one_layer(inputs, first_params, orders[0], segment, valid)
    result, stats_second = one_layer(low(low_back(middle)), second_params, orders[1], segment, valid)
    return (result, jnp.stack([stats_first, stats_second]))

def reference(tokens, cotangent, segment_ids, valid_mask, cluster_perm, query_weight, query_bias, key_weight, value_weight, value_bias, output_weight, output_bias, attention_gain, attention_shift, up_weight, up_bias, down_weight, down_bias, final_gain, final_shift):
    params = tuple((tensor.astype(jnp.float32) for tensor in (query_weight, query_bias, key_weight, value_weight, value_bias, output_weight, output_bias, attention_gain, attention_shift, up_weight, up_bias, down_weight, down_bias, final_gain, final_shift)))
    group_rows = math.gcd(ROWS, 8)
    group_count = ROWS // group_rows
    inputs = tokens.astype(jnp.float32).reshape(group_count, group_rows, SEQ, D)
    seeds = cotangent.astype(jnp.float32).reshape(group_count, group_rows, SEQ, D)
    segments = segment_ids.reshape(group_count, group_rows, SEQ)
    valids = valid_mask.reshape(group_count, group_rows, SEQ)
    orders = cluster_perm.reshape(LAYERS, group_count, group_rows, HEADS, SEQ).transpose(1, 0, 2, 3, 4)

    def group_step(carry, item):
        grads, sums = carry
        group_in, group_seed, group_seg, group_valid, group_order = item

        def forward(inside, weights):
            return two_layers(inside, weights, group_order, group_seg, group_valid)
        result, pull_back, stats = jax.vjp(forward, group_in, params, has_aux=True)
        d_inputs, d_params = pull_back(group_seed)
        grads = jax.tree.map(jnp.add, grads, d_params)
        return ((grads, sums + stats), (result, d_inputs))
    start = (jax.tree.map(jnp.zeros_like, params), jnp.zeros((LAYERS, 3), jnp.float32))
    (grads, sums), (results, d_all) = lax.scan(group_step, start, (inputs, seeds, segments, valids, orders))
    count = jnp.sum(valid_mask.astype(jnp.float32))
    root_means = jnp.sqrt(sums / (count * D))
    block_output = results.reshape(TOKENS, D).astype(jnp.bfloat16)
    input_gradient = d_all.reshape(TOKENS, D).astype(jnp.bfloat16)
    return (block_output, input_gradient, grads[0], grads[1], grads[2], grads[3], grads[4], grads[5], grads[6], grads[7], grads[8], grads[9], grads[10], grads[11], grads[12], grads[13], grads[14], root_means)
```

```python
from functools import partial

import jax
import jax.numpy as jnp
from jax import lax
from jax.experimental import pallas as pl
from jax.experimental.pallas import tpu as pltpu
from jax.sharding import PartitionSpec as P

HEAD_DIM = 64
CLUSTER = 128
SEQ = 512
LANES = 128
MIB = 1024 * 1024

BF16 = jnp.bfloat16
F32 = jnp.float32
LOG2E = 1.4426950408889634
SCALE = HEAD_DIM**-0.5
SCORE_SCALE = SCALE * LOG2E

NN = ((1,), (0,))
NT = ((1,), (1,))
TN = ((0,), (0,))

ANY = pl.BlockSpec(memory_space=pl.ANY)
WHOLE = pl.BlockSpec(memory_space=pltpu.VMEM)


def mm(left, right, dims):
    return lax.dot_general(left, right, (dims, ((), ())), preferred_element_type=F32)


class Copies:
    def __init__(self, sems):
        self.sems = sems
        self.used = 0

    def start(self, source, target):
        copy = pltpu.make_async_copy(source, target, self.sems.at[self.used])
        copy.start()
        self.used += 1
        return copy


def vec(ref):
    return ref[0:1, :].astype(F32)


SAVED = ("x", "qkv", "ctx", "lse", "kid", "qid", "n1", "r1", "hid", "act", "gp", "n2", "r2")


def saved_shapes(width, inner):
    return dict(
        x=((SEQ, width), BF16),
        qkv=((SEQ, 3 * width), BF16),
        ctx=((SEQ, width), BF16),
        lse=((16, SEQ), F32),
        kid=((SEQ, LANES), F32),
        qid=((16, SEQ), F32),
        n1=((SEQ, width), BF16),
        r1=((SEQ, LANES), F32),
        hid=((SEQ, width), BF16),
        act=((SEQ, inner), BF16),
        gp=((SEQ, inner), BF16),
        n2=((SEQ, width), BF16),
        r2=((SEQ, LANES), F32),
    )


def token_ids(row, heads, perm_ref, seg_ref, valid_ref):
    token = lax.broadcasted_iota(jnp.int32, (SEQ, LANES), 0)
    lane = lax.broadcasted_iota(jnp.int32, (SEQ, LANES), 1)
    clusters = jnp.zeros((SEQ, LANES), F32)
    for h in range(heads):
        places = perm_ref[0, row, h : h + 1, :]
        mine = jnp.zeros((SEQ, LANES), F32)
        for c in range(1, SEQ // CLUSTER):
            part = places[:, c * CLUSTER : (c + 1) * CLUSTER]
            mine = jnp.where(token == part, float(c), mine)
        column = jnp.sum(mine, axis=1, keepdims=True)
        clusters = jnp.where(lane == h, column, clusters)
    seg_row = seg_ref[row : row + 1, :].astype(F32)
    valid_row = valid_ref[row : row + 1, :].astype(F32)
    at = lax.broadcasted_iota(jnp.int32, (LANES, SEQ), 0)
    both = jnp.where(at == 0, seg_row, jnp.where(at == 1, valid_row, 0.0)).T
    live = both[:, 1:2]
    qid = clusters * 4.0 + both[:, 0:1]
    kid = jnp.where(live > 0.5, qid, -1.0)
    return kid, qid.T[0:16, :], live


def allowed_pairs(kid_column, qid_row):
    key = lax.broadcasted_iota(jnp.int32, (SEQ, SEQ), 0)
    query = lax.broadcasted_iota(jnp.int32, (SEQ, SEQ), 1)
    return (kid_column == qid_row) | (key == query)


def low_lanes():
    return lax.broadcasted_iota(jnp.int32, (SEQ, LANES), 1) < HEAD_DIM


def attend_pair(j, width, qkv, kid, qid, lse, ctx):
    low = low_lanes()
    lanes = slice(j * LANES, (j + 1) * LANES)
    query = qkv[:, j * LANES : (j + 1) * LANES]
    key = qkv[:, width + j * LANES : width + (j + 1) * LANES]
    value = qkv[:, 2 * width + j * LANES : 2 * width + (j + 1) * LANES]
    mixed = []
    for half in (0, 1):
        h = 2 * j + half
        own = low if half == 0 else ~low
        own_query = jnp.where(own, query, jnp.zeros_like(query))
        value_ones = jnp.where(own, value, jnp.ones_like(value))
        ok = allowed_pairs(kid[:, h : h + 1], qid[h : h + 1, :])
        scores = jnp.where(ok, mm(key, own_query, NT) * SCORE_SCALE, -1e30)
        top = jnp.max(scores, axis=0, keepdims=True)
        weights = jnp.exp2(scores - top)
        total = jnp.sum(weights, axis=0, keepdims=True)
        lse[h : h + 1, :] = top + jnp.log2(total)
        mixed.append(mm(weights.astype(BF16), value_ones, TN))
    sums = [pltpu.roll(part, HEAD_DIM, 1) for part in mixed]
    ctx[:, lanes] = (
        jnp.where(low, mixed[0], mixed[1]) / jnp.where(low, sums[0], sums[1])
    ).astype(BF16)


def normed(total):
    centre = total - jnp.mean(total, axis=-1, keepdims=True)
    spread = jnp.mean(centre * centre, axis=-1, keepdims=True)
    rate = lax.rsqrt(spread + 1e-05)
    return centre * rate, rate


ROW_BLOCK = 64


def over_rows(step):
    def body(i, carry):
        step(pl.ds(pl.multiple_of(i * ROW_BLOCK, ROW_BLOCK), ROW_BLOCK))
        return carry

    lax.fori_loop(0, SEQ // ROW_BLOCK, body, 0)


def over_tiles(size, tile, step):
    def body(i, carry):
        step(pl.ds(pl.multiple_of(i * tile, tile), tile))
        return carry

    lax.fori_loop(0, size // tile, body, 0)


def fold8(block):
    return jnp.sum(block.reshape(-1, 8, block.shape[-1]), axis=0)


def forward_kernel(section, row, x_row, n_alias, heads, *refs):
    (
        x_hbm,
        perm_ref,
        seg_ref,
        valid_ref,
        wq_hbm,
        bq_ref,
        wk_hbm,
        wv_hbm,
        bv_ref,
        wo_hbm,
        bo_ref,
        g1_ref,
        s1_ref,
        wu_hbm,
        bu_ref,
        wd_hbm,
        bd_ref,
        g2_ref,
        s2_ref,
    ) = refs[:19]
    refs = refs[19 + n_alias :]
    out = dict(zip(SAVED, refs[: len(SAVED)]))
    y_hbm, stats_hbm = refs[len(SAVED) : len(SAVED) + 2]
    refs = refs[len(SAVED) + 2 :]
    here = dict(zip(SAVED, refs[: len(SAVED)]))
    wqkv, wo, wu, wd, wide, feed, y_ref, stats, live_ref, sems = refs[len(SAVED) :]
    width = wo.shape[0]
    inner = wu.shape[1]

    @pl.when(lax.axis_index("section") == section)
    def _():
        copies = Copies(sems)
        get_x = copies.start(x_hbm.at[pl.ds(x_row * SEQ, SEQ), :], here["x"])
        get_qkv = [
            copies.start(w.at[0], wqkv.at[:, pl.ds(i * width, width)])
            for i, w in enumerate((wq_hbm, wk_hbm, wv_hbm))
        ]
        get_o = copies.start(wo_hbm.at[0], wo)
        get_u = copies.start(wu_hbm.at[0], wu)
        get_d = copies.start(wd_hbm.at[0], wd)
        puts = []

        def save(name):
            puts.append(copies.start(here[name], out[name]))

        kid, qid, live = token_ids(row, heads, perm_ref, seg_ref, valid_ref)
        here["kid"][...] = kid
        here["qid"][...] = qid
        live_ref[...] = jnp.broadcast_to(live, (SEQ, LANES))
        here["lse"][...] = jnp.zeros((16, SEQ), F32)
        stats[...] = jnp.zeros(stats.shape, F32)
        save("kid")
        save("qid")
        get_x.wait()
        save("x")
        xs = here["x"]
        qkv = here["qkv"]
        for i, bias in enumerate((bq_ref, None, bv_ref)):
            get_qkv[i].wait()
            part = pl.ds(i * width, width)
            value = mm(xs[...], wqkv[:, i * width : (i + 1) * width], NN)
            if bias is not None:
                value = value + vec(bias)
            qkv[:, part] = value.astype(BF16)
        save("qkv")
        for j in range(heads // 2):
            attend_pair(j, width, qkv, here["kid"], here["qid"], here["lse"], here["ctx"])
        save("lse")
        save("ctx")
        get_o.wait()
        wide[...] = mm(here["ctx"][...], wo[...], NN)

        def first_norm(rows):
            branch = wide[rows, :] + vec(bo_ref)
            alive = live_ref[rows, 0:1]
            stats[0:8, :] += fold8(branch * branch * alive)
            unit, rate = normed(xs[rows, :].astype(F32) + branch)
            hidden = unit * vec(g1_ref) + vec(s1_ref)
            here["n1"][rows, :] = unit.astype(BF16)
            here["r1"][rows, :] = jnp.broadcast_to(rate, (ROW_BLOCK, LANES))
            here["hid"][rows, :] = hidden.astype(BF16)
            wide[rows, :] = hidden

        over_rows(first_norm)
        save("n1")
        save("r1")
        save("hid")
        get_u.wait()

        def up(part):
            upper = mm(here["hid"][...], wu[:, part], NN) + bu_ref[0:1, part].astype(F32)
            half = 0.5 + 0.5 * lax.erf(upper * 0.5**0.5)
            bell = jnp.exp2(upper * upper * (-0.5 * LOG2E)) * 0.3989422804014327
            here["act"][:, part] = (upper * half).astype(BF16)
            here["gp"][:, part] = (half + upper * bell).astype(BF16)

        over_tiles(inner, inner // 4, up)
        save("act")
        save("gp")
        get_d.wait()
        feed[...] = mm(here["act"][...], wd[...], NN)

        def second_norm(rows):
            ffn = feed[rows, :] + vec(bd_ref)
            alive = live_ref[rows, 0:1]
            stats[8:16, :] += fold8(ffn * ffn * alive)
            unit, rate = normed(wide[rows, :] + ffn)
            result = unit * vec(g2_ref) + vec(s2_ref)
            stats[16:24, :] += fold8(result * result * alive)
            here["n2"][rows, :] = unit.astype(BF16)
            here["r2"][rows, :] = jnp.broadcast_to(rate, (ROW_BLOCK, LANES))
            y_ref[rows, :] = result.astype(BF16)

        over_rows(second_norm)
        puts.append(copies.start(y_ref, y_hbm))
        puts.append(copies.start(stats, stats_hbm))
        save("n2")
        save("r2")
        for put in puts:
            put.wait()


def forward(section, row, x, x_row, ids, params, saved):
    width = x.shape[1]
    inner = params[9].shape[2]
    heads = ids[0].shape[2]
    shapes = saved_shapes(width, inner)
    out_shape = [jax.ShapeDtypeStruct(*shapes[name]) for name in SAVED]
    out_shape += [
        jax.ShapeDtypeStruct((SEQ, width), BF16),
        jax.ShapeDtypeStruct((24, width), F32),
    ]
    param_specs = [ANY if p.ndim == 3 else WHOLE for p in params]
    old = [] if saved is None else list(saved)
    n_in = 4 + len(params)
    result = pl.pallas_call(
        partial(forward_kernel, section, row, x_row, len(old), heads),
        out_shape=out_shape,
        in_specs=[ANY, WHOLE, WHOLE, WHOLE] + param_specs + [ANY] * len(old),
        out_specs=[ANY] * len(out_shape),
        input_output_aliases={n_in + i: i for i in range(len(old))},
        scratch_shapes=[pltpu.VMEM(*shapes[name]) for name in SAVED]
        + [
            pltpu.VMEM((width, 3 * width), BF16),
            pltpu.VMEM((width, width), BF16),
            pltpu.VMEM((width, inner), BF16),
            pltpu.VMEM((inner, width), BF16),
            pltpu.VMEM((SEQ, width), F32),
            pltpu.VMEM((SEQ, width), F32),
            pltpu.VMEM((SEQ, width), BF16),
            pltpu.VMEM((24, width), F32),
            pltpu.VMEM((SEQ, LANES), F32),
            pltpu.SemaphoreType.DMA((24,)),
        ],
        compiler_params=pltpu.CompilerParams(vmem_limit_bytes=56 * MIB),
        cost_estimate=pl.CostEstimate(
            flops=2 * SEQ * (4 * width * width + 2 * width * inner) * 2,
            bytes_accessed=30 * MIB,
            transcendentals=0,
        ),
        name="layer_forward",
    )(x, *ids, *params, *old)
    return tuple(result[: len(SAVED)]), result[-2], result[-1]


GRADS = ("dffn", "dup", "dbr", "dqkv", "sums")
FROM_FORWARD = ("qkv", "ctx", "lse", "kid", "qid", "n1", "r1", "gp", "n2", "r2")
SUM_ROWS = ("gain2", "shift2", "bdown", "gain1", "shift1", "bout", "bq", "bv", "bup")


def grad_shapes(width, inner):
    return dict(
        dffn=((SEQ, width), BF16),
        dup=((SEQ, inner), BF16),
        dbr=((SEQ, width), BF16),
        dqkv=((SEQ, 3 * width), BF16),
        sums=((8 * len(SUM_ROWS), inner), F32),
    )


def attend_pair_back(j, width, qkv, dctx, kid, qid, lse, delta, dqkv):
    low = low_lanes()
    lanes = [slice(i * width + j * LANES, i * width + (j + 1) * LANES) for i in range(3)]
    query, key, value = (qkv[:, part] for part in lanes)
    d_out = dctx[:, lanes[0]]
    d_query, d_key, d_value = [], [], []
    for half in (0, 1):
        h = 2 * j + half
        own = low if half == 0 else ~low
        own_query = jnp.where(own, query, jnp.zeros_like(query))
        own_out = jnp.where(own, d_out, jnp.zeros_like(d_out))
        ok = allowed_pairs(kid[:, h : h + 1], qid[h : h + 1, :])
        scores = mm(key, own_query, NT) * SCORE_SCALE - lse[h : h + 1, :]
        weights = jnp.exp2(jnp.where(ok, scores, -1e30))
        d_weights = mm(value, own_out, NT)
        d_scores = (weights * (d_weights - delta[h : h + 1, :])).astype(BF16)
        d_value.append(mm(weights.astype(BF16), own_out, NN))
        d_key.append(mm(d_scores, own_query, NN))
        d_query.append(mm(d_scores, key, TN))
    dqkv[:, lanes[0]] = (jnp.where(low, d_query[0], d_query[1]) * SCALE).astype(BF16)
    dqkv[:, lanes[1]] = ((d_key[0] + d_key[1]) * SCALE).astype(BF16)
    dqkv[:, lanes[2]] = (d_value[0] + d_value[1]).astype(BF16)


def norm_back(grad, unit, rate, gain):
    scaled = grad * gain
    mean = jnp.mean(scaled, axis=-1, keepdims=True)
    along = jnp.mean(scaled * unit, axis=-1, keepdims=True)
    return (scaled - mean - unit * along) * rate


def backward_kernel(section, g_row, n_alias, heads, *refs):
    g_hbm = refs[0]
    wq_hbm, wk_hbm, wv_hbm, wo_hbm, wu_hbm, wd_hbm, g1_ref, g2_ref = refs[1:9]
    given = dict(zip(FROM_FORWARD, refs[9 : 9 + len(FROM_FORWARD)]))
    refs = refs[9 + len(FROM_FORWARD) + n_alias :]
    out = dict(zip(GRADS, refs[: len(GRADS)]))
    dx_hbm = refs[len(GRADS)]
    refs = refs[len(GRADS) + 1 :]
    here = dict(zip(FROM_FORWARD, refs[: len(FROM_FORWARD)]))
    refs = refs[len(FROM_FORWARD) :]
    made = dict(zip(GRADS, refs[: len(GRADS)]))
    wqkv, wo, wu, wd, g_ref, wide, dctx, delta, dx_ref, sems = refs[len(GRADS) :]
    width = wo.shape[0]
    inner = wu.shape[1]
    sums = made["sums"]

    def add_sum(name, value):
        at = 8 * SUM_ROWS.index(name)
        sums[at : at + 8, 0:width] += fold8(value)

    @pl.when(lax.axis_index("section") == section)
    def _():
        copies = Copies(sems)
        get_g = copies.start(g_hbm.at[pl.ds(g_row * SEQ, SEQ), :], g_ref)
        got = {}
        for name in ("n2", "r2"):
            got[name] = copies.start(given[name], here[name])
        get_d = copies.start(wd_hbm.at[0], wd)
        got["gp"] = copies.start(given["gp"], here["gp"])
        get_u = copies.start(wu_hbm.at[0], wu)
        for name in ("n1", "r1"):
            got[name] = copies.start(given[name], here[name])
        get_o = copies.start(wo_hbm.at[0], wo)
        for name in ("ctx", "lse", "kid", "qid", "qkv"):
            got[name] = copies.start(given[name], here[name])
        get_qkv = [
            copies.start(w.at[0], wqkv.at[:, pl.ds(i * width, width)])
            for i, w in enumerate((wq_hbm, wk_hbm, wv_hbm))
        ]
        puts = []

        def save(name):
            puts.append(copies.start(made[name], out[name]))

        sums[...] = jnp.zeros(sums.shape, F32)
        get_g.wait()
        got["n2"].wait()
        got["r2"].wait()

        def second_back(rows):
            grad = g_ref[rows, :].astype(F32)
            unit = here["n2"][rows, :].astype(F32)
            add_sum("gain2", grad * unit)
            add_sum("shift2", grad)
            d_second = norm_back(grad, unit, here["r2"][rows, 0:1], vec(g2_ref))
            wide[rows, :] = d_second
            low = d_second.astype(BF16)
            made["dffn"][rows, :] = low
            add_sum("bdown", low.astype(F32))

        over_rows(second_back)
        save("dffn")
        get_d.wait()
        got["gp"].wait()

        def up_back(part):
            d_act = mm(made["dffn"][...], wd[part, :], NT)
            low = (d_act * here["gp"][:, part].astype(F32)).astype(BF16)
            made["dup"][:, part] = low
            at = 8 * SUM_ROWS.index("bup")
            sums[at : at + 8, part] += fold8(low.astype(F32))

        over_tiles(inner, inner // 4, up_back)
        save("dup")
        get_u.wait()
        wide[...] += mm(made["dup"][...], wu[...], NT)
        got["n1"].wait()
        got["r1"].wait()

        def first_back(rows):
            grad = wide[rows, :]
            unit = here["n1"][rows, :].astype(F32)
            add_sum("gain1", grad * unit)
            add_sum("shift1", grad)
            d_first = norm_back(grad, unit, here["r1"][rows, 0:1], vec(g1_ref))
            wide[rows, :] = d_first
            low = d_first.astype(BF16)
            made["dbr"][rows, :] = low
            add_sum("bout", low.astype(F32))

        over_rows(first_back)
        save("dbr")
        get_o.wait()
        dctx[...] = mm(made["dbr"][...], wo[...], NT).astype(BF16)
        got["ctx"].wait()
        product = dctx[...].astype(F32) * here["ctx"][...].astype(F32)
        high = product.astype(BF16)
        rest = (product - high.astype(F32)).astype(BF16)
        of_head = (
            lax.broadcasted_iota(jnp.int32, (16, width), 1) // HEAD_DIM
            == lax.broadcasted_iota(jnp.int32, (16, width), 0)
        )
        pick = jnp.where(of_head, 1.0, 0.0).astype(BF16)
        delta[...] = mm(pick, high, NT) + mm(pick, rest, NT)
        for name in ("lse", "kid", "qid", "qkv"):
            got[name].wait()
        for j in range(heads // 2):
            attend_pair_back(
                j,
                width,
                here["qkv"],
                dctx,
                here["kid"],
                here["qid"],
                here["lse"],
                delta,
                made["dqkv"],
            )
        save("dqkv")
        for get in get_qkv:
            get.wait()

        def bias_sums(rows):
            add_sum("bq", made["dqkv"][rows, 0:width].astype(F32))
            add_sum("bv", made["dqkv"][rows, 2 * width : 3 * width].astype(F32))

        over_rows(bias_sums)
        save("sums")
        dx_ref[...] = (wide[...] + mm(made["dqkv"][...], wqkv[...], NT)).astype(BF16)
        puts.append(copies.start(dx_ref, dx_hbm))
        for put in puts:
            put.wait()


def backward(section, g, g_row, params, saved, grads):
    width = g.shape[1]
    inner = params[9].shape[2]
    heads = width // HEAD_DIM
    kept = dict(zip(SAVED, saved))
    shapes = saved_shapes(width, inner)
    out = grad_shapes(width, inner)
    wq, _, wk, wv, _, wo, _, g1, _, wu, _, wd, _, g2, _ = params
    out_shape = [jax.ShapeDtypeStruct(*out[name]) for name in GRADS]
    out_shape.append(jax.ShapeDtypeStruct((SEQ, width), BF16))
    old = [] if grads is None else list(grads)
    n_in = 9 + len(FROM_FORWARD)
    result = pl.pallas_call(
        partial(backward_kernel, section, g_row, len(old), heads),
        out_shape=out_shape,
        in_specs=[ANY] * 7 + [WHOLE] * 2 + [ANY] * (len(FROM_FORWARD) + len(old)),
        out_specs=[ANY] * len(out_shape),
        input_output_aliases={n_in + i: i for i in range(len(old))},
        scratch_shapes=[pltpu.VMEM(*shapes[name]) for name in FROM_FORWARD]
        + [pltpu.VMEM(*out[name]) for name in GRADS]
        + [
            pltpu.VMEM((width, 3 * width), BF16),
            pltpu.VMEM((width, width), BF16),
            pltpu.VMEM((width, inner), BF16),
            pltpu.VMEM((inner, width), BF16),
            pltpu.VMEM((SEQ, width), BF16),
            pltpu.VMEM((SEQ, width), F32),
            pltpu.VMEM((SEQ, width), BF16),
            pltpu.VMEM((16, SEQ), F32),
            pltpu.VMEM((SEQ, width), BF16),
            pltpu.SemaphoreType.DMA((24,)),
        ],
        compiler_params=pltpu.CompilerParams(vmem_limit_bytes=56 * MIB),
        cost_estimate=pl.CostEstimate(
            flops=2 * SEQ * (4 * width * width + 2 * width * inner) * 2,
            bytes_accessed=40 * MIB,
            transcendentals=0,
        ),
        name="layer_backward",
    )(g, wq, wk, wv, wo, wu, wd, g1, g2, *(kept[name] for name in FROM_FORWARD), *old)
    return tuple(result[: len(GRADS)]), result[-1]


def outer_kernel(n_rows, tile, split_left, *refs):
    lefts = refs[:n_rows]
    rights = refs[n_rows : 2 * n_rows]
    out_hbm = refs[2 * n_rows]
    left, right, out, sems = refs[2 * n_rows + 1 :]
    copies = Copies(sems)
    gets = [
        copies.start(ref, buf.at[pl.ds(i * SEQ, SEQ), :])
        for i in range(n_rows)
        for ref, buf in ((lefts[i], left), (rights[i], right))
    ]
    for get in gets:
        get.wait()

    size = left.shape[1] if split_left else right.shape[1]

    def body(i, carry):
        part = pl.ds(pl.multiple_of(i * tile, tile), tile)
        if split_left:
            out[part, :] = mm(left[:, part], right[...], TN).astype(BF16)
        else:
            out[:, part] = mm(left[...], right[:, part], TN).astype(BF16)
        return carry

    lax.fori_loop(0, size // tile, body, 0)
    put = copies.start(out, out_hbm)
    put.wait()


def outer(lefts, rights, tile, split_left):
    n_rows = len(lefts)
    rows, columns = lefts[0].shape[1], rights[0].shape[1]
    return pl.pallas_call(
        partial(outer_kernel, n_rows, tile, split_left),
        out_shape=jax.ShapeDtypeStruct((rows, columns), BF16),
        in_specs=[ANY] * (2 * n_rows),
        out_specs=ANY,
        scratch_shapes=[
            pltpu.VMEM((n_rows * SEQ, rows), BF16),
            pltpu.VMEM((n_rows * SEQ, columns), BF16),
            pltpu.VMEM((rows, columns), BF16),
            pltpu.SemaphoreType.DMA((2 * n_rows + 1,)),
        ],
        compiler_params=pltpu.CompilerParams(vmem_limit_bytes=48 * MIB),
        cost_estimate=pl.CostEstimate(
            flops=2 * n_rows * SEQ * rows * columns,
            bytes_accessed=2 * (n_rows * SEQ * (rows + columns) + rows * columns),
            transcendentals=0,
        ),
        name="weight_gradient",
    )(*lefts, *rights)


def scatter_sum(partial_sum):
    count = lax.axis_size("dp")
    if count != 16:
        total = lax.psum_scatter(partial_sum, "dp", scatter_dimension=0, tiled=True)
        return total.astype(F32)
    me = lax.axis_index("dp")
    core, x, z = me % 2, (me // 2) % 2, me // 4
    rows, columns = partial_sum.shape
    block = rows // count

    def pick(array, index):
        return lax.dynamic_index_in_dim(array, index, 1, keepdims=False)

    def halve(array, own, stride):
        pairs = [(d, d ^ stride) for d in range(count)]
        arrived = lax.ppermute(pick(array, 1 - own), "dp", pairs)
        return (pick(array, own).astype(F32) + arrived.astype(F32)).astype(BF16)

    held = halve(partial_sum.reshape(8, 2, block, columns), core, 1)
    held = halve(held.reshape(4, 2, block, columns), x, 2)

    def at(index):
        return lax.dynamic_index_in_dim(held, jnp.clip(index, 0, 3), 0, keepdims=False)

    rising = falling = None
    for step in range(3):
        up_pairs = [(d, d + 4) for d in range(12) if d // 4 <= step]
        down_pairs = [(d, d - 4) for d in range(4, 16) if 3 - d // 4 <= step]
        up = at(3 + z - step)
        down = at(step - 3 + z)
        if rising is not None:
            up = (up.astype(F32) + rising.astype(F32)).astype(BF16)
            down = (down.astype(F32) + falling.astype(F32)).astype(BF16)
        rising = lax.ppermute(up, "dp", up_pairs)
        falling = lax.ppermute(down, "dp", down_pairs)
    return at(z).astype(F32) + rising.astype(F32) + falling.astype(F32)


def on_device(
    tokens,
    cotangent,
    segment_ids,
    valid_mask,
    cluster_perm,
    *params,
):
    section = lax.axis_index("section")
    width = tokens.shape[1]
    inner = params[9].shape[2]
    ids = (cluster_perm, segment_ids, valid_mask)

    def hop(array, source, target):
        return lax.ppermute(array, "section", [(source, target)])

    def then(first, array):
        return lax.optimization_barrier((array, first))[0]

    kept0, y0, stats00 = forward(0, 0, tokens, 0, ids, params, None)
    in0 = hop(y0, 0, 1)
    kept1, y1, stats01 = forward(0, 1, tokens, 1, ids, params, None)
    in1 = hop(y1, 0, 1)
    kept0, out0, stats10 = forward(1, 0, in0, 0, ids, params, kept0)
    grads0, dx0 = backward(1, cotangent, 0, params, kept0, None)
    g0 = hop(dx0, 1, 0)
    kept1, out1, stats11 = forward(1, 1, in1, 0, ids, params, kept1)
    grads1, dx1 = backward(1, cotangent, 1, params, kept1, None)
    g1 = hop(dx1, 1, 0)
    grads0, dx0 = backward(0, g0, 0, params, kept0, grads0)
    grads1, dx1 = backward(0, g1, 0, params, kept1, grads1)

    a, b = dict(zip(SAVED, kept0)), dict(zip(SAVED, kept1))
    c, d = dict(zip(GRADS, grads0)), dict(zip(GRADS, grads1))

    def both(left, right, tile, split_left):
        return outer((a[left], b[left]), (c[right], d[right]), tile, split_left)

    w_down = scatter_sum(both("act", "dffn", width, True))
    w_up = scatter_sum(both("hid", "dup", width, False))
    w_out = scatter_sum(both("ctx", "dbr", width, False))
    w_qkv = scatter_sum(both("x", "dqkv", width, False))

    sums = (c["sums"] + d["sums"]).reshape(len(SUM_ROWS), 8, inner).sum(axis=1)
    first = section == 0
    stats = jnp.where(first, stats00 + stats01, stats10 + stats11)
    stats = stats.reshape(3, 8 * width).sum(axis=1)
    count = jnp.sum(valid_mask.astype(F32))
    small = jnp.concatenate(
        [sums[:8, :width].reshape(-1), sums[8], stats, jnp.broadcast_to(count, (1,))]
    )
    small = lax.psum(small, "dp")
    shares = lax.axis_size("dp")
    me = lax.axis_index("dp")

    def small_part(name):
        i = SUM_ROWS.index(name)
        size = inner if name == "bup" else width
        own = size // shares
        return lax.dynamic_slice_in_dim(small, i * width + me * own, own, 0)[None]

    base = 8 * width + inner
    root_means = jnp.sqrt(small[base : base + 3] / (small[base + 3] * width))[None, :]

    half = width // 2
    outputs = jnp.concatenate([out0, out1])
    input_grads = jnp.concatenate([dx0, dx1])
    outgoing = jnp.where(first, input_grads[:, half:], outputs[:, :half])
    arrived = lax.ppermute(outgoing, "section", [(0, 1), (1, 0)])
    block_part = jnp.where(first, arrived, outputs[:, half:])
    grad_part = jnp.where(first, input_grads[:, :half], arrived)
    return (
        block_part,
        grad_part,
        w_qkv[None, :, :width],
        small_part("bq"),
        w_qkv[None, :, width : 2 * width],
        w_qkv[None, :, 2 * width :],
        small_part("bv"),
        w_out[None],
        small_part("bout"),
        small_part("gain1"),
        small_part("shift1"),
        w_up[None],
        small_part("bup"),
        w_down[None],
        small_part("bdown"),
        small_part("gain2"),
        small_part("shift2"),
        root_means,
    )


def solution(mesh):
    by_layer = P("section", None)
    matrix = P("section", None, None)
    share = P("section", "dp")
    matrix_share = P("section", "dp", None)
    return jax.shard_map(
        on_device,
        mesh=mesh,
        in_specs=(
            P("dp", None),
            P("dp", None),
            P("dp", None),
            P("dp", None),
            P("section", "dp", None, None),
            matrix,
            by_layer,
            matrix,
            matrix,
            by_layer,
            matrix,
            by_layer,
            by_layer,
            by_layer,
            matrix,
            by_layer,
            matrix,
            by_layer,
            by_layer,
            by_layer,
        ),
        out_specs=(
            P("dp", "section"),
            P("dp", "section"),
            matrix_share,
            share,
            matrix_share,
            matrix_share,
            share,
            matrix_share,
            share,
            share,
            share,
            matrix_share,
            share,
            matrix_share,
            share,
            share,
            share,
            P("section", None),
        ),
        check_vma=False,
    )
```

```python
from functools import partial

import jax
import jax.numpy as jnp
from jax import lax
from jax.experimental import pallas as pl
from jax.experimental.pallas import tpu as pltpu
from jax.sharding import PartitionSpec as P

HEAD_DIM = 64
CLUSTER = 128
SEQ = 512
LANES = 128
MIB = 1024 * 1024

BF16 = jnp.bfloat16
F32 = jnp.float32
LOG2E = 1.4426950408889634
SCALE = HEAD_DIM**-0.5
SCORE_SCALE = SCALE * LOG2E

NN = ((1,), (0,))
NT = ((1,), (1,))
TN = ((0,), (0,))

ANY = pl.BlockSpec(memory_space=pltpu.HBM)
SHORT = pl.CostEstimate(flops=1, bytes_accessed=1, transcendentals=0)
WHOLE = pl.BlockSpec(memory_space=pltpu.VMEM)


def mm(left, right, dims):
    return lax.dot_general(left, right, (dims, ((), ())), preferred_element_type=F32)


class Copies:
    def __init__(self, sems):
        self.sems = sems
        self.used = 0

    def start(self, source, target):
        copy = pltpu.make_async_copy(source, target, self.sems.at[self.used])
        copy.start()
        self.used += 1
        return copy


def vec(ref):
    return ref[0:1, :].astype(F32)


SAVED = ("x", "qkv", "ctx", "lse", "kid", "qid", "n1", "r1", "hid", "act", "gp", "n2", "r2")


def saved_shapes(width, inner):
    return dict(
        x=((SEQ, width), BF16),
        qkv=((SEQ, 3 * width), BF16),
        ctx=((SEQ, width), BF16),
        lse=((16, SEQ), F32),
        kid=((SEQ, width), F32),
        qid=((16, SEQ), F32),
        n1=((SEQ, width), BF16),
        r1=((SEQ, LANES), F32),
        hid=((SEQ, width), BF16),
        act=((SEQ, inner), BF16),
        gp=((SEQ, inner), BF16),
        n2=((SEQ, width), BF16),
        r2=((SEQ, LANES), F32),
    )


def token_ids(row, heads, perm_ref, seg_ref, valid_ref, kid_ref, qid_ref):
    token = lax.broadcasted_iota(jnp.int32, (SEQ, LANES), 0)
    lane = lax.broadcasted_iota(jnp.int32, (SEQ, LANES), 1)
    seg_row = seg_ref[row : row + 1, :].astype(F32)
    valid_row = valid_ref[row : row + 1, :].astype(F32)
    at = lax.broadcasted_iota(jnp.int32, (LANES, SEQ), 0)
    both = jnp.where(at == 0, seg_row, jnp.where(at == 1, valid_row, 0.0)).T
    segment, live = both[:, 0:1], both[:, 1:2]

    def column(h):
        places = perm_ref[0, row, pl.ds(h, 1), :]
        mine = jnp.zeros((SEQ, LANES), F32)
        for c in range(1, SEQ // CLUSTER):
            part = places[:, c * CLUSTER : (c + 1) * CLUSTER]
            mine = jnp.where(token == part, float(c), mine)
        return jnp.sum(mine, axis=1, keepdims=True) * 4.0 + segment

    def pair(j, ids):
        left, right = column(2 * j), column(2 * j + 1)
        own = jnp.where(lane < HEAD_DIM, left, right)
        kid_ref[:, lanes_at(j * LANES)] = jnp.where(live > 0.5, own, -1.0)
        ids = jnp.where(lane == 2 * j, left, ids)
        return jnp.where(lane == 2 * j + 1, right, ids)

    qid = lax.fori_loop(0, heads // 2, pair, jnp.zeros((SEQ, LANES), F32))
    qid_ref[...] = qid.T[0:16, :]
    return live


def allowed_pairs(kid_column, qid_row):
    key = lax.broadcasted_iota(jnp.int32, (SEQ, SEQ), 0)
    query = lax.broadcasted_iota(jnp.int32, (SEQ, SEQ), 1)
    return (kid_column == qid_row) | (key == query)


def low_lanes():
    return lax.broadcasted_iota(jnp.int32, (SEQ, LANES), 1) < HEAD_DIM


def lanes_at(start):
    return pl.ds(pl.multiple_of(start, LANES), LANES)


def attend_pair(j, width, qkv, kid, qid, lse, ctx):
    low = low_lanes()
    lanes = lanes_at(j * LANES)
    query = qkv[:, lanes]
    key = qkv[:, lanes_at(width + j * LANES)]
    value = qkv[:, lanes_at(2 * width + j * LANES)]
    kid_pair = kid[:, lanes]
    mixed = []
    for half in (0, 1):
        h = pl.ds(2 * j + half, 1)
        own = low if half == 0 else ~low
        own_query = jnp.where(own, query, jnp.zeros_like(query))
        value_ones = jnp.where(own, value, jnp.ones_like(value))
        kid_column = kid_pair[:, half * HEAD_DIM : half * HEAD_DIM + 1]
        ok = allowed_pairs(kid_column, qid[h, :])
        scores = jnp.where(ok, mm(key, own_query, NT) * SCORE_SCALE, -1e30)
        top = jnp.max(scores, axis=0, keepdims=True)
        weights = jnp.exp2(scores - top)
        total = jnp.sum(weights, axis=0, keepdims=True)
        lse[h, :] = top + jnp.log2(total)
        mixed.append(mm(weights.astype(BF16), value_ones, TN))
    sums = [pltpu.roll(part, HEAD_DIM, 1) for part in mixed]
    ctx[:, lanes] = (
        jnp.where(low, mixed[0], mixed[1]) / jnp.where(low, sums[0], sums[1])
    ).astype(BF16)


def normed(total):
    centre = total - jnp.mean(total, axis=-1, keepdims=True)
    spread = jnp.mean(centre * centre, axis=-1, keepdims=True)
    rate = lax.rsqrt(spread + 1e-05)
    return centre * rate, rate


ROW_BLOCK = 64


def over_rows(step):
    def body(i, carry):
        step(pl.ds(pl.multiple_of(i * ROW_BLOCK, ROW_BLOCK), ROW_BLOCK))
        return carry

    lax.fori_loop(0, SEQ // ROW_BLOCK, body, 0)


def over_tiles(size, tile, step):
    def body(i, carry):
        step(pl.ds(pl.multiple_of(i * tile, tile), tile))
        return carry

    lax.fori_loop(0, size // tile, body, 0)


def fold8(block):
    return jnp.sum(block.reshape(-1, 8, block.shape[-1]), axis=0)


def forward_kernel(section, row, x_row, n_alias, heads, *refs):
    (
        x_hbm,
        perm_ref,
        seg_ref,
        valid_ref,
        wq_hbm,
        bq_ref,
        wk_hbm,
        wv_hbm,
        bv_ref,
        wo_hbm,
        bo_ref,
        g1_ref,
        s1_ref,
        wu_hbm,
        bu_ref,
        wd_hbm,
        bd_ref,
        g2_ref,
        s2_ref,
    ) = refs[:19]
    refs = refs[19 + n_alias :]
    out = dict(zip(SAVED, refs[: len(SAVED)]))
    y_hbm, stats_hbm = refs[len(SAVED) : len(SAVED) + 2]
    refs = refs[len(SAVED) + 2 :]
    here = dict(zip(SAVED, refs[: len(SAVED)]))
    wqkv, wo, wu, wd, wide, feed, y_ref, stats, live_ref, bias, sems = refs[len(SAVED) :]
    width = wo.shape[0]
    inner = wu.shape[1]

    @pl.when(lax.axis_index("section") == section)
    def _():
        copies = Copies(sems)
        get_x = copies.start(x_hbm.at[pl.ds(x_row * SEQ, SEQ), :], here["x"])
        get_qkv = [
            copies.start(w.at[0], wqkv.at[:, pl.ds(i * width, width)])
            for i, w in enumerate((wq_hbm, wk_hbm, wv_hbm))
        ]
        get_o = copies.start(wo_hbm.at[0], wo)
        get_u = copies.start(wu_hbm.at[0], wu)
        get_d = copies.start(wd_hbm.at[0], wd)
        puts = []

        def save(name):
            puts.append(copies.start(here[name], out[name]))

        live = token_ids(row, heads, perm_ref, seg_ref, valid_ref, here["kid"], here["qid"])
        live_ref[...] = jnp.broadcast_to(live, (SEQ, LANES))
        here["lse"][...] = jnp.zeros((16, SEQ), F32)
        stats[...] = jnp.zeros(stats.shape, F32)
        save("kid")
        save("qid")
        get_x.wait()
        save("x")
        xs = here["x"]
        qkv = here["qkv"]
        bias[0:1, :] = vec(bq_ref)
        bias[1:2, :] = jnp.zeros((1, width), F32)
        bias[2:3, :] = vec(bv_ref)
        for get in get_qkv:
            get.wait()

        def to_qkv(i, carry):
            part = pl.ds(pl.multiple_of(i * width, LANES), width)
            qkv[:, part] = (mm(xs[...], wqkv[:, part], NN) + bias[pl.ds(i, 1), :]).astype(BF16)
            return carry

        lax.fori_loop(0, 3, to_qkv, 0)
        save("qkv")

        def attend(j, carry):
            attend_pair(j, width, qkv, here["kid"], here["qid"], here["lse"], here["ctx"])
            return carry

        lax.fori_loop(0, heads // 2, attend, 0)
        save("lse")
        save("ctx")
        get_o.wait()
        wide[...] = mm(here["ctx"][...], wo[...], NN)

        def first_norm(rows):
            branch = wide[rows, :] + vec(bo_ref)
            alive = live_ref[rows, 0:1]
            stats[0:8, :] += fold8(branch * branch * alive)
            unit, rate = normed(xs[rows, :].astype(F32) + branch)
            hidden = unit * vec(g1_ref) + vec(s1_ref)
            here["n1"][rows, :] = unit.astype(BF16)
            here["r1"][rows, :] = jnp.broadcast_to(rate, (ROW_BLOCK, LANES))
            here["hid"][rows, :] = hidden.astype(BF16)
            wide[rows, :] = hidden

        over_rows(first_norm)
        save("n1")
        save("r1")
        save("hid")
        get_u.wait()

        def up(part):
            upper = mm(here["hid"][...], wu[:, part], NN) + bu_ref[0:1, part].astype(F32)
            half = 0.5 + 0.5 * lax.erf(upper * 0.5**0.5)
            bell = jnp.exp2(upper * upper * (-0.5 * LOG2E)) * 0.3989422804014327
            here["act"][:, part] = (upper * half).astype(BF16)
            here["gp"][:, part] = (half + upper * bell).astype(BF16)

        over_tiles(inner, inner // 4, up)
        save("act")
        save("gp")
        get_d.wait()
        feed[...] = mm(here["act"][...], wd[...], NN)

        def second_norm(rows):
            ffn = feed[rows, :] + vec(bd_ref)
            alive = live_ref[rows, 0:1]
            stats[8:16, :] += fold8(ffn * ffn * alive)
            unit, rate = normed(wide[rows, :] + ffn)
            result = unit * vec(g2_ref) + vec(s2_ref)
            stats[16:24, :] += fold8(result * result * alive)
            here["n2"][rows, :] = unit.astype(BF16)
            here["r2"][rows, :] = jnp.broadcast_to(rate, (ROW_BLOCK, LANES))
            y_ref[rows, :] = result.astype(BF16)

        over_rows(second_norm)
        puts.append(copies.start(y_ref, y_hbm))
        puts.append(copies.start(stats, stats_hbm))
        save("n2")
        save("r2")
        for put in puts:
            put.wait()


def forward(section, row, x, x_row, ids, params, saved):
    width = x.shape[1]
    inner = params[9].shape[2]
    heads = ids[0].shape[2]
    shapes = saved_shapes(width, inner)
    out_shape = [jax.ShapeDtypeStruct(*shapes[name]) for name in SAVED]
    out_shape += [
        jax.ShapeDtypeStruct((SEQ, width), BF16),
        jax.ShapeDtypeStruct((24, width), F32),
    ]
    param_specs = [ANY if p.ndim == 3 else WHOLE for p in params]
    old = [] if saved is None else list(saved)
    n_in = 4 + len(params)
    result = pl.pallas_call(
        partial(forward_kernel, section, row, x_row, len(old), heads),
        out_shape=out_shape,
        in_specs=[ANY, WHOLE, WHOLE, WHOLE] + param_specs + [ANY] * len(old),
        out_specs=[ANY] * len(out_shape),
        input_output_aliases={n_in + i: i for i in range(len(old))},
        scratch_shapes=[pltpu.VMEM(*shapes[name]) for name in SAVED]
        + [
            pltpu.VMEM((width, 3 * width), BF16),
            pltpu.VMEM((width, width), BF16),
            pltpu.VMEM((width, inner), BF16),
            pltpu.VMEM((inner, width), BF16),
            pltpu.VMEM((SEQ, width), F32),
            pltpu.VMEM((SEQ, width), F32),
            pltpu.VMEM((SEQ, width), BF16),
            pltpu.VMEM((24, width), F32),
            pltpu.VMEM((SEQ, LANES), F32),
            pltpu.VMEM((8, width), F32),
            pltpu.SemaphoreType.DMA((24,)),
        ],
        compiler_params=pltpu.CompilerParams(vmem_limit_bytes=58 * MIB),
        cost_estimate=SHORT,
        name="layer_forward",
    )(x, *ids, *params, *old)
    return tuple(result[: len(SAVED)]), result[-2], result[-1]


MATRICES = ("wq", "wk", "wv", "wo", "wu", "wd")
PARTS = dict(
    ffn=(("g", "n2", "r2", "wd", "gp"), ("dffn", "dup", "wide", "sums_a")),
    mid=(("dup", "wide", "wu", "n1", "r1", "wo", "ctx"), ("dbr", "wide", "dctx", "delta", "sums_b")),
    att=(("dctx", "delta", "lse", "kid", "qid", "qkv"), ("dqkv", "sums_c")),
    dx=(("dqkv", "wide", "wq", "wk", "wv"), ("dx",)),
)
GRADS = ("dffn", "dup", "sums_a", "dbr", "sums_b", "dqkv", "sums_c")
BETWEEN = ("wide", "dctx", "delta")
SUM_ROWS = dict(
    sums_a=("gain2", "shift2", "bdown", "bup"),
    sums_b=("gain1", "shift1", "bout"),
    sums_c=("bq", "bv"),
)


def backward_shapes(width, inner):
    shapes = dict(saved_shapes(width, inner))
    shapes.update(
        g=((SEQ, width), BF16),
        dffn=((SEQ, width), BF16),
        dup=((SEQ, inner), BF16),
        dbr=((SEQ, width), BF16),
        dqkv=((SEQ, 3 * width), BF16),
        sums_a=((32, inner), F32),
        sums_b=((24, width), F32),
        sums_c=((16, width), F32),
        wide=((SEQ, width), F32),
        dctx=((SEQ, width), BF16),
        delta=((16, SEQ), F32),
        dx=((SEQ, width), BF16),
        wo=((width, width), BF16),
        wu=((width, inner), BF16),
        wd=((inner, width), BF16),
    )
    return shapes


def attend_pair_back(j, width, qkv, dctx, kid, qid, lse, delta, dqkv):
    low = low_lanes()
    lanes = [lanes_at(i * width + j * LANES) for i in range(3)]
    query, key, value = (qkv[:, part] for part in lanes)
    d_out = dctx[:, lanes[0]]
    kid_pair = kid[:, lanes[0]]
    d_query, d_key, d_value = [], [], []
    for half in (0, 1):
        h = pl.ds(2 * j + half, 1)
        own = low if half == 0 else ~low
        own_query = jnp.where(own, query, jnp.zeros_like(query))
        own_out = jnp.where(own, d_out, jnp.zeros_like(d_out))
        kid_column = kid_pair[:, half * HEAD_DIM : half * HEAD_DIM + 1]
        ok = allowed_pairs(kid_column, qid[h, :])
        scores = mm(key, own_query, NT) * SCORE_SCALE - lse[h, :]
        weights = jnp.exp2(jnp.where(ok, scores, -1e30))
        d_weights = mm(value, own_out, NT)
        d_scores = (weights * (d_weights - delta[h, :])).astype(BF16)
        d_value.append(mm(weights.astype(BF16), own_out, NN))
        d_key.append(mm(d_scores, own_query, NN))
        d_query.append(mm(d_scores, key, TN))
    dqkv[:, lanes[0]] = (jnp.where(low, d_query[0], d_query[1]) * SCALE).astype(BF16)
    dqkv[:, lanes[1]] = ((d_key[0] + d_key[1]) * SCALE).astype(BF16)
    dqkv[:, lanes[2]] = (d_value[0] + d_value[1]).astype(BF16)


def norm_back(grad, unit, rate, gain):
    scaled = grad * gain
    mean = jnp.mean(scaled, axis=-1, keepdims=True)
    along = jnp.mean(scaled * unit, axis=-1, keepdims=True)
    return (scaled - mean - unit * along) * rate


def needs_and_gives(parts):
    needs, gives = [], []
    for part in parts:
        for name in PARTS[part][0]:
            if name not in needs and name not in gives:
                needs.append(name)
        for name in PARTS[part][1]:
            if name not in gives:
                gives.append(name)
    if len(parts) == len(PARTS):
        gives = [name for name in gives if name not in BETWEEN]
    return needs, gives


def backward_kernel(section, g_row, parts, pairs, n_alias, names, *refs):
    needs, gives, held = names
    given = dict(zip(needs, refs))
    gain1_ref, gain2_ref = refs[len(needs) : len(needs) + 2]
    refs = refs[len(needs) + 2 + n_alias :]
    out = dict(zip(gives, refs))
    refs = refs[len(gives) :]
    at = dict(zip(held, refs))
    sems = refs[-1]
    width = gain1_ref.shape[1]

    @pl.when(lax.axis_index("section") == section)
    def _():
        copies = Copies(sems)
        got = {}
        for name in needs:
            source = given[name]
            if name in MATRICES:
                source = source.at[0]
            if name == "g":
                source = source.at[pl.ds(g_row * SEQ, SEQ), :]
            if name in ("wq", "wk", "wv"):
                third = MATRICES.index(name)
                target = at["wqkv"].at[:, pl.ds(third * width, width)]
            else:
                target = at[name]
            got[name] = copies.start(source, target)
        puts = []

        def ready(*wanted):
            for name in wanted:
                if name in got:
                    got.pop(name).wait()

        def save(*made):
            for name in made:
                if name not in out:
                    continue
                if name == "dqkv" and len(parts) == 1:
                    for i in range(3):
                        lanes = pl.ds(i * width + pairs[0] * LANES, (pairs[1] - pairs[0]) * LANES)
                        puts.append(copies.start(at[name].at[:, lanes], out[name].at[:, lanes]))
                else:
                    puts.append(copies.start(at[name], out[name]))

        def add_sum(group, name, value):
            first = 8 * SUM_ROWS[group].index(name)
            at[group][first : first + 8, 0:width] += fold8(value)

        for group in SUM_ROWS:
            if group in at:
                at[group][...] = jnp.zeros(at[group].shape, F32)

        if "ffn" in parts:
            ready("g", "n2", "r2")

            def second_back(rows):
                grad = at["g"][rows, :].astype(F32)
                unit = at["n2"][rows, :].astype(F32)
                add_sum("sums_a", "gain2", grad * unit)
                add_sum("sums_a", "shift2", grad)
                d_second = norm_back(grad, unit, at["r2"][rows, 0:1], vec(gain2_ref))
                at["wide"][rows, :] = d_second
                low = d_second.astype(BF16)
                at["dffn"][rows, :] = low
                add_sum("sums_a", "bdown", low.astype(F32))

            over_rows(second_back)
            save("dffn")
            ready("wd", "gp")

            def up_back(part):
                d_act = mm(at["dffn"][...], at["wd"][part, :], NT)
                low = (d_act * at["gp"][:, part].astype(F32)).astype(BF16)
                at["dup"][:, part] = low
                at["sums_a"][24:32, part] += fold8(low.astype(F32))

            inner = at["dup"].shape[1]
            over_tiles(inner, inner // 4, up_back)
            save("dup", "sums_a")
            if "mid" not in parts:
                save("wide")

        if "mid" in parts:
            ready("dup", "wide", "wu")
            at["wide"][...] += mm(at["dup"][...], at["wu"][...], NT)
            ready("n1", "r1")

            def first_back(rows):
                grad = at["wide"][rows, :]
                unit = at["n1"][rows, :].astype(F32)
                add_sum("sums_b", "gain1", grad * unit)
                add_sum("sums_b", "shift1", grad)
                d_first = norm_back(grad, unit, at["r1"][rows, 0:1], vec(gain1_ref))
                at["wide"][rows, :] = d_first
                low = d_first.astype(BF16)
                at["dbr"][rows, :] = low
                add_sum("sums_b", "bout", low.astype(F32))

            over_rows(first_back)
            save("dbr", "wide", "sums_b")
            ready("wo")
            at["dctx"][...] = mm(at["dbr"][...], at["wo"][...], NT).astype(BF16)
            ready("ctx")
            product = at["dctx"][...].astype(F32) * at["ctx"][...].astype(F32)
            high = product.astype(BF16)
            rest = (product - high.astype(F32)).astype(BF16)
            of_head = (
                lax.broadcasted_iota(jnp.int32, (16, width), 1) // HEAD_DIM
                == lax.broadcasted_iota(jnp.int32, (16, width), 0)
            )
            pick = jnp.where(of_head, 1.0, 0.0).astype(BF16)
            at["delta"][...] = mm(pick, high, NT) + mm(pick, rest, NT)
            save("dctx", "delta")

        if "att" in parts:
            ready(*PARTS["att"][0])

            def attend_back(j, carry):
                attend_pair_back(
                    j,
                    width,
                    at["qkv"],
                    at["dctx"],
                    at["kid"],
                    at["qid"],
                    at["lse"],
                    at["delta"],
                    at["dqkv"],
                )
                for i, name in ((0, "bq"), (2, "bv")):
                    made = at["dqkv"][:, lanes_at(i * width + j * LANES)]
                    first = 8 * SUM_ROWS["sums_c"].index(name)
                    at["sums_c"][first : first + 8, lanes_at(j * LANES)] = fold8(made.astype(F32))
                return carry

            lax.fori_loop(pairs[0], pairs[1], attend_back, 0)
            save("dqkv", "sums_c")

        if "dx" in parts:
            ready(*PARTS["dx"][0])
            at["dx"][...] = (at["wide"][...] + mm(at["dqkv"][...], at["wqkv"][...], NT)).astype(
                BF16
            )
            save("dx")
        for put in puts:
            put.wait()


def backward(section, parts, g_row, known, gains, old, pairs=None):
    width, inner = known["wu"].shape[1:]
    shapes = backward_shapes(width, inner)
    if pairs is None:
        pairs = (0, width // LANES)
    needs, gives = needs_and_gives(parts)
    held = [name for name in needs if name not in ("wq", "wk", "wv")]
    made = [name for part in parts for name in PARTS[part][1]]
    held += [name for name in dict.fromkeys(made) if name not in held]
    scratch = [pltpu.VMEM(*shapes[name]) for name in held]
    if "dx" in parts:
        held.append("wqkv")
        scratch.append(pltpu.VMEM((width, 3 * width), BF16))
    reused = [name for name in gives if name in old]
    n_in = len(needs) + 2
    aliases = {n_in + i: gives.index(name) for i, name in enumerate(reused)}
    result = pl.pallas_call(
        partial(backward_kernel, section, g_row, parts, pairs, len(reused), (needs, gives, held)),
        out_shape=[jax.ShapeDtypeStruct(*shapes[name]) for name in gives],
        in_specs=[ANY] * len(needs) + [WHOLE] * 2 + [ANY] * len(reused),
        out_specs=[ANY] * len(gives),
        input_output_aliases=aliases,
        scratch_shapes=scratch + [pltpu.SemaphoreType.DMA((36,))],
        compiler_params=pltpu.CompilerParams(vmem_limit_bytes=58 * MIB),
        cost_estimate=SHORT,
        name="backward_" + "_".join(parts),
    )(*(known[name] for name in needs), *gains, *(old[name] for name in reused))
    return dict(zip(gives, result))


def outer_kernel(n_rows, tile, split_left, pairs, *refs):
    lefts = refs[:n_rows]
    rights = refs[n_rows : 2 * n_rows]
    outs = refs[2 * n_rows : -4]
    left, right, out, sems = refs[-4:]
    copies = Copies(sems)
    gets = [
        copies.start(ref, buf.at[pl.ds(i * SEQ, SEQ), :])
        for i in range(n_rows)
        for ref, buf in ((lefts[i], left), (rights[i], right))
    ]
    for get in gets:
        get.wait()

    size = left.shape[1] if split_left else right.shape[1]

    def body(i, carry):
        part = pl.ds(pl.multiple_of(i * tile, tile), tile)
        if split_left:
            out[part, :] = mm(left[:, part], right[...], TN).astype(BF16)
        else:
            out[:, part] = mm(left[...], right[:, part], TN).astype(BF16)
        return carry

    lax.fori_loop(0, size // tile, body, 0)
    if pairs == 0:
        puts = [copies.start(out, outs[0])]
    else:
        core = lax.axis_index("dp") % 2
        block = out.shape[0] // (2 * pairs)
        puts = []
        for i in range(pairs):
            for target, which in zip(outs, (core, 1 - core)):
                rows = pl.ds(pl.multiple_of((2 * i + which) * block, 16), block)
                puts.append(copies.start(out.at[rows, :], target.at[i]))
    for put in puts:
        put.wait()


def outer(lefts, rights, tile, split_left):
    n_rows = len(lefts)
    rows, columns = lefts[0].shape[1], rights[0].shape[1]
    count = lax.axis_size("dp")
    if count == 16:
        pairs = 8
        out_shape = [jax.ShapeDtypeStruct((pairs, rows // count, columns), BF16)] * 2
    else:
        pairs = 0
        out_shape = [jax.ShapeDtypeStruct((rows, columns), BF16)]
    return pl.pallas_call(
        partial(outer_kernel, n_rows, tile, split_left, pairs),
        out_shape=out_shape,
        in_specs=[ANY] * (2 * n_rows),
        out_specs=[ANY] * len(out_shape),
        scratch_shapes=[
            pltpu.VMEM((n_rows * SEQ, rows), BF16),
            pltpu.VMEM((n_rows * SEQ, columns), BF16),
            pltpu.VMEM((rows, columns), BF16),
            pltpu.SemaphoreType.DMA((2 * n_rows + 16,)),
        ],
        compiler_params=pltpu.CompilerParams(vmem_limit_bytes=58 * MIB),
        cost_estimate=SHORT,
        name="weight_gradient",
    )(*lefts, *rights)


def swap(array, stride):
    count = lax.axis_size("dp")
    return lax.ppermute(array, "dp", [(d, d ^ stride) for d in range(count)])


def place(stride):
    return (lax.axis_index("dp") // stride) % 2


def add(left, right):
    return (left.astype(F32) + right.astype(F32)).astype(BF16)


class ScatterSum:
    def __init__(self, blocks, order):
        self.shape = blocks[0].shape[1:]
        self.blocks = blocks
        self.order = (1,) + order
        self.axes = [8, 4, 2]
        self.done = 0
        self.arrived = blocks[0]
        self.plain = lax.axis_size("dp") != 16

    def pick(self, array, stride, index):
        at = self.axes.index(stride)
        split = array.reshape((2**at, 2, 2 ** (len(self.axes) - at - 1)) + self.shape)
        taken = lax.dynamic_index_in_dim(split, index, 1, keepdims=False)
        return taken.reshape((-1,) + self.shape)

    def advance(self):
        before = self.arrived
        if self.plain or self.done == 4:
            return before
        stride = self.order[self.done]
        self.done += 1
        if stride == 1:
            self.kept, send = self.blocks
        else:
            own = place(stride)
            send, self.kept = (
                add(self.pick(self.kept, stride, side), self.pick(before, stride, side))
                for side in (1 - own, own)
            )
            self.axes.remove(stride)
        self.arrived = swap(send, stride)
        return before

    def finish(self):
        if self.plain:
            total = lax.psum_scatter(self.blocks[0], "dp", scatter_dimension=0, tiled=True)
            return total.astype(F32)
        while self.done < 4:
            self.advance()
        return (self.kept.astype(F32) + self.arrived.astype(F32)).reshape(self.shape)


def small_sum(values):
    count = lax.axis_size("dp")
    if count != 16:
        return lax.psum(values, "dp")
    for stride in (1, 2, 4, 8):
        values = values + swap(values, stride)
    return values


X_FIRST = (2, 4, 8)
Z_FIRST = (4, 2, 8)


def on_device(
    tokens,
    cotangent,
    segment_ids,
    valid_mask,
    cluster_perm,
    *params,
):
    section = lax.axis_index("section")
    width = tokens.shape[1]
    inner = params[9].shape[2]
    ids = (cluster_perm, segment_ids, valid_mask)
    wq, _, wk, wv, _, wo, _, gain1, _, wu, _, wd, _, gain2, _ = params
    matrices = dict(wq=wq, wk=wk, wv=wv, wo=wo, wu=wu, wd=wd)
    gains = (gain1, gain2)

    def hop(array, source, target):
        return lax.ppermute(array, "section", [(source, target)])

    def after(array, first):
        return lax.optimization_barrier((array, first))[0]

    whole = tuple(PARTS)
    kept0, y0, stats00 = forward(0, 0, tokens, 0, ids, params, None)
    in0 = hop(y0, 0, 1)
    kept1, y1, stats01 = forward(0, 1, tokens, 1, ids, params, None)
    in1 = hop(y1, 0, 1)
    kept0, out0, stats10 = forward(1, 0, in0, 0, ids, params, kept0)
    known = dict(zip(SAVED, kept0), g=cotangent, **matrices)
    first = backward(1, whole, 0, known, gains, {})
    in1 = after(in1, first["dx"])
    g0 = hop(first["dx"], 1, 0)
    kept1, out1, stats11 = forward(1, 1, in1, 0, ids, params, kept1)
    known = dict(zip(SAVED, kept1), g=cotangent, **matrices)
    second = backward(1, whole, 1, known, gains, {})
    g0 = after(g0, second["dx"])
    g1 = hop(second["dx"], 1, 0)
    known = dict(zip(SAVED, kept0), g=g0, **matrices)
    first = backward(0, whole, 0, known, gains, first)
    g1 = after(g1, first["dx"])
    known = dict(zip(SAVED, kept1), g=g1, **matrices)

    def step(parts, pairs=None):
        made = backward(0, parts, 0, known, gains, second, pairs)
        known.update(made)
        second.update({name: made[name] for name in made if name in second})

    row0, row1 = dict(zip(SAVED, kept0)), dict(zip(SAVED, kept1))

    def both(left, right, tile, split_left):
        return outer((row0[left], row1[left]), (first[right], second[right]), tile, split_left)

    step(("ffn",))
    down = both("act", "dffn", width, True)
    down_sum = ScatterSum(down, X_FIRST)
    down_sum.advance()
    second["dup"] = after(second["dup"], down[0])
    up = both("hid", "dup", width, False)
    up_sum = ScatterSum(up, Z_FIRST)
    up_sum.advance()
    known["wide"] = after(known["wide"], (up[0], down_sum.advance()))
    step(("mid",))
    known["dctx"] = after(known["dctx"], up_sum.advance())
    out = both("ctx", "dbr", width, False)
    out_sum = ScatterSum(out, X_FIRST)
    out_sum.advance()
    known["dctx"] = after(known["dctx"], out[0])
    half_pairs = width // LANES // 2
    step(("att",), (0, half_pairs))
    early = second.pop("sums_c")
    known["dctx"] = after(known["dctx"], (out_sum.arrived, known["dqkv"]))
    step(("att",), (half_pairs, 2 * half_pairs))
    qkv = both("x", "dqkv", width, False)
    qkv_sum = ScatterSum(qkv, X_FIRST)
    qkv_sum.advance()
    waited = (qkv[0], down_sum.advance(), up_sum.advance())
    known["wide"] = after(known["wide"], waited)
    step(("dx",))
    out_sum.arrived = after(out_sum.arrived, second["dx"])

    w_down = down_sum.finish()
    w_up = up_sum.finish()
    w_out = out_sum.finish()
    w_qkv = qkv_sum.finish()
    dx0, dx1 = first["dx"], second["dx"]
    is_first = section == 0

    late = jnp.where(
        (lax.broadcasted_iota(jnp.int32, (1, width), 1) >= half_pairs * LANES) & is_first,
        known["sums_c"],
        early,
    )
    sum_a = (first["sums_a"] + second["sums_a"]).reshape(4, 8, inner).sum(axis=1)
    sum_b = (first["sums_b"] + second["sums_b"]).reshape(3, 8, width).sum(axis=1)
    sum_c = (first["sums_c"] + late).reshape(2, 8, width).sum(axis=1)
    stats = jnp.where(is_first, stats00 + stats01, stats10 + stats11)
    stats = stats.reshape(3, 8 * width).sum(axis=1)
    count = jnp.sum(valid_mask.astype(F32))
    pieces = [sum_a[:3, :width].reshape(-1), sum_b.reshape(-1), sum_c.reshape(-1), sum_a[3]]
    base = 8 * width + inner
    spare = -(base + 4) % (8 * LANES)
    tail = jnp.concatenate([stats, jnp.broadcast_to(count, (1,)), jnp.zeros((spare,), F32)])
    small = jnp.concatenate(pieces + [tail]).reshape(-1, LANES)
    small = after(small, dx1)
    small = small_sum(small).reshape(-1)
    shares = lax.axis_size("dp")
    me = lax.axis_index("dp")
    order = ("gain2", "shift2", "bdown", "gain1", "shift1", "bout", "bq", "bv", "bup")

    def small_part(name):
        size = inner if name == "bup" else width
        own = size // shares
        start = order.index(name) * width + me * own
        return lax.dynamic_slice_in_dim(small, start, own, 0)[None]

    root_means = jnp.sqrt(small[base : base + 3] / (small[base + 3] * width))[None, :]

    half = width // 2
    dx0, out0, out1 = (after(array, dx1) for array in (dx0, out0, out1))
    outgoing = jnp.concatenate(
        [
            jnp.where(is_first, grad[:, half:], made[:, :half])
            for grad, made in ((dx0, out0), (dx1, out1))
        ]
    )
    arrived = lax.ppermute(outgoing, "section", [(0, 1), (1, 0)])
    block_own = jnp.concatenate([out0[:, half:], out1[:, half:]])
    grad_own = jnp.concatenate([dx0[:, :half], dx1[:, :half]])
    block_part = jnp.where(is_first, arrived, block_own)
    grad_part = jnp.where(is_first, grad_own, arrived)
    return (
        block_part,
        grad_part,
        w_qkv[None, :, :width],
        small_part("bq"),
        w_qkv[None, :, width : 2 * width],
        w_qkv[None, :, 2 * width :],
        small_part("bv"),
        w_out[None],
        small_part("bout"),
        small_part("gain1"),
        small_part("shift1"),
        w_up[None],
        small_part("bup"),
        w_down[None],
        small_part("bdown"),
        small_part("gain2"),
        small_part("shift2"),
        root_means,
    )


def solution(mesh):
    by_layer = P("section", None)
    matrix = P("section", None, None)
    share = P("section", "dp")
    matrix_share = P("section", "dp", None)
    return jax.shard_map(
        on_device,
        mesh=mesh,
        in_specs=(
            P("dp", None),
            P("dp", None),
            P("dp", None),
            P("dp", None),
            P("section", "dp", None, None),
            matrix,
            by_layer,
            matrix,
            matrix,
            by_layer,
            matrix,
            by_layer,
            by_layer,
            by_layer,
            matrix,
            by_layer,
            matrix,
            by_layer,
            by_layer,
            by_layer,
        ),
        out_specs=(
            P("dp", "section"),
            P("dp", "section"),
            matrix_share,
            share,
            matrix_share,
            matrix_share,
            share,
            matrix_share,
            share,
            share,
            share,
            matrix_share,
            share,
            matrix_share,
            share,
            share,
            share,
            P("section", None),
        ),
        check_vma=False,
    )
```

```python
from functools import partial

import jax
import jax.numpy as jnp
from jax import lax
from jax.experimental import pallas as pl
from jax.experimental.pallas import tpu as pltpu
from jax.sharding import PartitionSpec as P

HEAD_DIM = 64
CLUSTER = 128
SEQ = 512
LANES = 128
ROW_BLOCK = 128
PAIR_UNROLL = 2
MIB = 1024 * 1024

BF16 = jnp.bfloat16
F32 = jnp.float32
LOG2E = 1.4426950408889634
SCALE = HEAD_DIM**-0.5
SCORE_SCALE = SCALE * LOG2E

NN = ((1,), (0,))
NT = ((1,), (1,))
TN = ((0,), (0,))

ROWS = "dp"
LAYER = "section"
ANY = pl.BlockSpec(memory_space=pltpu.HBM)
WHOLE = pl.BlockSpec(memory_space=pltpu.VMEM)
SHORT = pl.CostEstimate(flops=1, bytes_accessed=1, transcendentals=0)

X, QKV, CTX, LSE, KID, QID, N1, R1, HID, ACT, GP, N2, R2 = range(13)
G, DFFN, DUP, DBR, DQKV, SUMS_A, SUMS_B, SUMS_C, WIDE, DCTX, DELTA, DX, FEED, LIVE = range(13, 27)
BIAS, WQKV, Y, STATS, WO, WU, WD, REST = range(27, 35)
SAVED = (X, QKV, CTX, LSE, KID, QID, N1, R1, HID, ACT, GP, N2, R2)
GRADS = (DFFN, DUP, DBR, DQKV, SUMS_A, SUMS_B, SUMS_C)
GAIN2, SHIFT2, B_DOWN, B_UP = 0, 8, 16, 24
GAIN1, SHIFT1, B_OUT = 0, 8, 16
B_QUERY, B_VALUE = 0, 8


def shapes_of(width, inner):
    token, token32, narrow = ((SEQ, width), BF16), ((SEQ, width), F32), ((SEQ, LANES), F32)
    heads = ((16, SEQ), F32)
    shapes = {name: token for name in (X, CTX, N1, HID, N2, G, DFFN, DBR, DCTX, DX, Y)}
    shapes.update({name: token32 for name in (KID, WIDE, FEED)})
    shapes.update({name: narrow for name in (R1, R2, LIVE)})
    shapes.update({name: heads for name in (LSE, QID, DELTA)})
    shapes.update({name: ((SEQ, inner), BF16) for name in (ACT, GP, DUP)})
    shapes.update({name: ((SEQ, 3 * width), BF16) for name in (QKV, DQKV)})
    shapes.update({SUMS_A: ((32, inner), F32), SUMS_B: ((24, width), F32)})
    shapes.update({SUMS_C: ((16, width), F32), STATS: ((24, width), F32), BIAS: ((8, width), F32)})
    shapes.update({WQKV: ((width, 3 * width), BF16), WO: ((width, width), BF16)})
    shapes.update({WU: ((width, inner), BF16), WD: ((inner, width), BF16)})
    shapes[REST] = ((width, 4 * width), BF16)
    return shapes


def mm(left, right, dims):
    return lax.dot_general(left, right, (dims, ((), ())), preferred_element_type=F32)


def vec(ref):
    return ref[0:1, :].astype(F32)


def lanes_at(start, size=LANES):
    return pl.ds(pl.multiple_of(start, LANES), size)


def fold8(block):
    return jnp.sum(block.reshape(-1, 8, block.shape[-1]), axis=0)


def over_rows(step):
    def body(i, carry):
        step(pl.ds(pl.multiple_of(i * ROW_BLOCK, ROW_BLOCK), ROW_BLOCK))
        return carry

    lax.fori_loop(0, SEQ // ROW_BLOCK, body, 0)


def over_tiles(size, tile, step):
    def body(i, carry):
        step(pl.ds(pl.multiple_of(i * tile, tile), tile))
        return carry

    lax.fori_loop(0, size // tile, body, 0)


class Copies:
    def __init__(self, at, sems):
        self.at, self.sems = at, sems
        self.used = 0
        self.loads = {}
        self.stores = []

    def plan(self, source, target):
        self.used += 1
        return pltpu.make_async_copy(source, target, self.sems.at[self.used - 1])

    def load(self, name, source, target=None, now=True):
        target = self.at[name] if target is None else target
        copy = self.plan(source, target)
        self.loads.setdefault(name, []).append(copy)
        if now:
            copy.start()

    def go(self):
        for copies in self.loads.values():
            for copy in copies:
                copy.start()

    def ready(self, *names):
        for name in names:
            for copy in self.loads.pop(name, ()):
                copy.wait()

    def store(self, source, target, now=True):
        copy = self.plan(source, target)
        self.stores.append(copy)
        if now:
            copy.start()
        return copy

    def finish(self):
        for copy in self.stores:
            copy.wait()


def load_qkv(copies, weights, width):
    for i, weight in enumerate(weights):
        copies.load(WQKV, weight.at[0], copies.at[WQKV].at[:, pl.ds(i * width, width)])


def call(body, name, inputs, old, outs, scratch, n_sems):
    arrays = [array for array, _ in inputs]
    n_in = len(arrays)
    return pl.pallas_call(
        partial(body, n_in, len(old), len(outs)),
        out_shape=[jax.ShapeDtypeStruct(*shape) for shape in outs],
        in_specs=[spec for _, spec in inputs] + [ANY] * len(old),
        out_specs=[ANY] * len(outs),
        input_output_aliases={n_in + i: place for i, place in enumerate(old)},
        scratch_shapes=[pltpu.VMEM(*shape) for shape in scratch]
        + [pltpu.SemaphoreType.DMA((n_sems,))],
        compiler_params=pltpu.CompilerParams(vmem_limit_bytes=58 * MIB),
        cost_estimate=SHORT,
        name=name,
    )(*arrays, *old.values())


def split_refs(n_in, n_old, n_out, refs):
    return refs[:n_in], refs[n_in + n_old : n_in + n_old + n_out], refs[n_in + n_old + n_out :]


def low_lanes():
    return lax.broadcasted_iota(jnp.int32, (SEQ, LANES), 1) < HEAD_DIM


def masked(scores, kid_column, qid_row):
    shape = (CLUSTER, CLUSTER)
    same = lax.broadcasted_iota(jnp.int32, shape, 0) == lax.broadcasted_iota(jnp.int32, shape, 1)
    count = SEQ // CLUSTER
    parts = [slice(i * CLUSTER, (i + 1) * CLUSTER) for i in range(count)]
    rows = []
    for i in range(count):
        tiles = []
        for j in range(count):
            ok = kid_column[parts[i]] == qid_row[:, parts[j]]
            if i == j:
                ok = ok | same
            tiles.append(jnp.where(ok, scores[parts[i], parts[j]], -1e30))
        rows.append(jnp.concatenate(tiles, axis=1))
    return jnp.concatenate(rows, axis=0)


def attend_pair(j, width, at):
    low = low_lanes()
    lanes = lanes_at(j * LANES)
    query = at[QKV][:, lanes]
    key = at[QKV][:, lanes_at(width + j * LANES)]
    value = at[QKV][:, lanes_at(2 * width + j * LANES)]
    kid_pair = at[KID][:, lanes]
    mixed, tops = [], []
    for half in (0, 1):
        own = low if half == 0 else ~low
        own_query = jnp.where(own, query, jnp.zeros_like(query))
        value_ones = jnp.where(own, value, jnp.ones_like(value))
        kid_column = kid_pair[:, half * HEAD_DIM : half * HEAD_DIM + 1]
        scores = mm(key, own_query, NT) * SCORE_SCALE
        scores = masked(scores, kid_column, at[QID][pl.ds(2 * j + half, 1), :])
        top = jnp.max(scores, axis=0, keepdims=True)
        tops.append(top)
        mixed.append(mm(jnp.exp2(scores - top).astype(BF16), value_ones, TN))
    sums = [pltpu.roll(part, HEAD_DIM, 1) for part in mixed]
    total = jnp.where(low, sums[0], sums[1])
    at[CTX][:, lanes] = (jnp.where(low, mixed[0], mixed[1]) / total).astype(BF16)
    turned = total.T
    for half in (0, 1):
        row = turned[half * HEAD_DIM : half * HEAD_DIM + 1, :]
        at[LSE][pl.ds(2 * j + half, 1), :] = tops[half] + jnp.log2(row)


def attend_pair_back(j, width, at, target, base):
    low = low_lanes()
    lanes = [lanes_at(i * width + j * LANES) for i in range(3)]
    query, key, value = (at[QKV][:, part] for part in lanes)
    d_out = at[DCTX][:, lanes[0]]
    kid_pair = at[KID][:, lanes[0]]
    d_query, d_key, d_value = [], [], []
    for half in (0, 1):
        h = pl.ds(2 * j + half, 1)
        own = low if half == 0 else ~low
        own_query = jnp.where(own, query, jnp.zeros_like(query))
        own_out = jnp.where(own, d_out, jnp.zeros_like(d_out))
        kid_column = kid_pair[:, half * HEAD_DIM : half * HEAD_DIM + 1]
        scores = mm(key, own_query, NT) * SCORE_SCALE - at[LSE][h, :]
        weights = jnp.exp2(masked(scores, kid_column, at[QID][h, :]))
        d_weights = mm(value, own_out, NT)
        d_scores = (weights * (d_weights - at[DELTA][h, :])).astype(BF16)
        d_value.append(mm(weights.astype(BF16), own_out, NN))
        d_key.append(mm(d_scores, own_query, NN))
        d_query.append(mm(d_scores, key, TN))
    made = (
        jnp.where(low, d_query[0], d_query[1]) * SCALE,
        (d_key[0] + d_key[1]) * SCALE,
        d_value[0] + d_value[1],
    )
    rows = pl.ds(base, SEQ)
    for i, place in ((0, B_QUERY), (1, None), (2, B_VALUE)):
        rounded = made[i].astype(BF16)
        target[rows, lanes[i]] = rounded
        if place is not None:
            at[SUMS_C][place : place + 8, lanes[0]] = fold8(rounded.astype(F32))


def over_pairs(width, step):
    def body(j, carry):
        step(j)
        return carry

    lax.fori_loop(0, width // LANES, body, 0, unroll=PAIR_UNROLL)


def token_ids(row, heads, perm_ref, seg_ref, valid_ref, kid_ref, qid_ref):
    token = lax.broadcasted_iota(jnp.int32, (SEQ, LANES), 0)
    lane = lax.broadcasted_iota(jnp.int32, (SEQ, LANES), 1)
    seg_row = seg_ref[row : row + 1, :].astype(F32)
    valid_row = valid_ref[row : row + 1, :].astype(F32)
    at = lax.broadcasted_iota(jnp.int32, (LANES, SEQ), 0)
    both = jnp.where(at == 0, seg_row, jnp.where(at == 1, valid_row, 0.0)).T
    segment, live = both[:, 0:1], both[:, 1:2]

    def column(h):
        places = perm_ref[0, row, pl.ds(h, 1), :]
        mine = jnp.zeros((SEQ, LANES), F32)
        for c in range(1, SEQ // CLUSTER):
            part = places[:, c * CLUSTER : (c + 1) * CLUSTER]
            mine = jnp.where(token == part, float(c), mine)
        return jnp.sum(mine, axis=1, keepdims=True) * 4.0 + segment

    def pair(j, ids):
        left, right = column(2 * j), column(2 * j + 1)
        own = jnp.where(lane < HEAD_DIM, left, right)
        kid_ref[:, lanes_at(j * LANES)] = jnp.where(live > 0.5, own, -1.0)
        ids = jnp.where(lane == 2 * j, left, ids)
        return jnp.where(lane == 2 * j + 1, right, ids)

    qid = lax.fori_loop(0, heads // 2, pair, jnp.zeros((SEQ, LANES), F32))
    qid_ref[...] = qid.T[0:16, :]
    return live


def normed(total):
    centre = total - jnp.mean(total, axis=-1, keepdims=True)
    spread = jnp.mean(centre * centre, axis=-1, keepdims=True)
    rate = lax.rsqrt(spread + 1e-05)
    return centre * rate, rate


FORWARD_HELD = SAVED + (WQKV, WO, WU, WD, WIDE, FEED, Y, STATS, LIVE, BIAS)


def forward_kernel(section, row, x_row, heads, n_in, n_old, n_out, *refs):
    ins, outs, refs = split_refs(n_in, n_old, n_out, refs)
    x_hbm, perm_ref, seg_ref, valid_ref = ins[:4]
    wq, bq, wk, wv, bv, wo, bo, g1, s1, wu, bu, wd, bd, g2, s2 = ins[4:]
    out = dict(zip(SAVED + (Y, STATS), outs))
    at = dict(zip(FORWARD_HELD, refs))
    width, inner = at[WU].shape

    @pl.when(lax.axis_index(LAYER) == section)
    def _():
        copies = Copies(at, refs[-1])

        def save(*names):
            for name in names:
                copies.store(at[name], out[name])

        copies.load(X, x_hbm.at[pl.ds(x_row * SEQ, SEQ), :])
        first = copies.used
        load_qkv(copies, (wq, wk, wv), width)
        live = token_ids(row, heads, perm_ref, seg_ref, valid_ref, at[KID], at[QID])
        at[LIVE][...] = jnp.broadcast_to(live, (SEQ, LANES))
        at[LSE][...] = jnp.zeros((16, SEQ), F32)
        at[STATS][...] = jnp.zeros((24, width), F32)
        at[BIAS][0:1, :] = vec(bq)
        at[BIAS][1:2, :] = jnp.zeros((1, width), F32)
        at[BIAS][2:3, :] = vec(bv)
        copies.ready(X)

        def to_qkv(i, carry):
            part = pl.ds(pl.multiple_of(i * width, LANES), width)
            weight = at[WQKV].at[:, part]
            pltpu.make_async_copy(weight, weight, copies.sems.at[first + i]).wait()
            made = mm(at[X][...], at[WQKV][:, part], NN) + at[BIAS][pl.ds(i, 1), :]
            at[QKV][:, part] = made.astype(BF16)
            return carry

        lax.fori_loop(0, 3, to_qkv, 0)
        copies.load(WO, wo.at[0])
        copies.load(WU, wu.at[0])
        copies.load(WD, wd.at[0])
        save(KID, QID, X, QKV)
        over_pairs(width, lambda j: attend_pair(j, width, at))
        save(LSE, CTX)
        copies.ready(WO)
        at[WIDE][...] = mm(at[CTX][...], at[WO][...], NN)

        def first_norm(rows):
            branch = at[WIDE][rows, :] + vec(bo)
            alive = at[LIVE][rows, 0:1]
            at[STATS][0:8, :] += fold8(branch * branch * alive)
            unit, rate = normed(at[X][rows, :].astype(F32) + branch)
            hidden = unit * vec(g1) + vec(s1)
            at[N1][rows, :] = unit.astype(BF16)
            at[R1][rows, :] = jnp.broadcast_to(rate, (ROW_BLOCK, LANES))
            at[HID][rows, :] = hidden.astype(BF16)
            at[WIDE][rows, :] = hidden

        over_rows(first_norm)
        save(N1, R1, HID)
        copies.ready(WU)

        def up(part):
            upper = mm(at[HID][...], at[WU][:, part], NN) + bu[0:1, part].astype(F32)
            half = 0.5 + 0.5 * lax.erf(upper * 0.5**0.5)
            bell = jnp.exp2(upper * upper * (-0.5 * LOG2E)) * 0.3989422804014327
            at[ACT][:, part] = (upper * half).astype(BF16)
            at[GP][:, part] = (half + upper * bell).astype(BF16)

        over_tiles(inner, inner // 4, up)
        save(ACT, GP)
        copies.ready(WD)
        at[FEED][...] = mm(at[ACT][...], at[WD][...], NN)

        def second_norm(rows):
            ffn = at[FEED][rows, :] + vec(bd)
            alive = at[LIVE][rows, 0:1]
            at[STATS][8:16, :] += fold8(ffn * ffn * alive)
            unit, rate = normed(at[WIDE][rows, :] + ffn)
            result = unit * vec(g2) + vec(s2)
            at[STATS][16:24, :] += fold8(result * result * alive)
            at[N2][rows, :] = unit.astype(BF16)
            at[R2][rows, :] = jnp.broadcast_to(rate, (ROW_BLOCK, LANES))
            at[Y][rows, :] = result.astype(BF16)

        over_rows(second_norm)
        save(Y, STATS, N2, R2)
        copies.finish()


def forward(section, row, x, x_row, ids, params, kept):
    width, inner = params[9].shape[1:]
    shapes = shapes_of(width, inner)
    inputs = [(x, ANY)] + [(array, WHOLE) for array in ids]
    inputs += [(array, ANY if array.ndim == 3 else WHOLE) for array in params]
    made = call(
        partial(forward_kernel, section, row, x_row, width // HEAD_DIM),
        "forward",
        inputs,
        {} if kept is None else {i: kept[name] for i, name in enumerate(SAVED)},
        [shapes[name] for name in SAVED + (Y, STATS)],
        [shapes[name] for name in FORWARD_HELD],
        32,
    )
    return dict(zip(SAVED, made)), made[-2], made[-1]


def norm_back(grad, unit, rate, gain):
    scaled = grad * gain
    mean = jnp.mean(scaled, axis=-1, keepdims=True)
    along = jnp.mean(scaled * unit, axis=-1, keepdims=True)
    return (scaled - mean - unit * along) * rate


def add_sum(ref, place, value):
    ref[place : place + 8, 0 : value.shape[-1]] += fold8(value)


def second_norm_back(at, gain2, target, base):
    def step(rows):
        grad = at[G][rows, :].astype(F32)
        unit = at[N2][rows, :].astype(F32)
        add_sum(at[SUMS_A], GAIN2, grad * unit)
        add_sum(at[SUMS_A], SHIFT2, grad)
        d_second = norm_back(grad, unit, at[R2][rows, 0:1], vec(gain2))
        at[WIDE][rows, :] = d_second
        low = d_second.astype(BF16)
        target[pl.ds(pl.multiple_of(rows.start + base, ROW_BLOCK), ROW_BLOCK), :] = low
        add_sum(at[SUMS_A], B_DOWN, low.astype(F32))

    over_rows(step)


def up_back(at, dffn, part):
    d_act = mm(dffn, at[WD][part, :], NT)
    low = (d_act * at[GP][:, part].astype(F32)).astype(BF16)
    at[SUMS_A][B_UP : B_UP + 8, part] += fold8(low.astype(F32))
    return low


def first_norm_back(at, gain1, target, base):
    def step(rows):
        grad = at[WIDE][rows, :]
        unit = at[N1][rows, :].astype(F32)
        add_sum(at[SUMS_B], GAIN1, grad * unit)
        add_sum(at[SUMS_B], SHIFT1, grad)
        d_first = norm_back(grad, unit, at[R1][rows, 0:1], vec(gain1))
        at[WIDE][rows, :] = d_first
        low = d_first.astype(BF16)
        target[pl.ds(pl.multiple_of(rows.start + base, ROW_BLOCK), ROW_BLOCK), :] = low
        add_sum(at[SUMS_B], B_OUT, low.astype(F32))

    over_rows(step)


def context_back(at, dbr, context):
    width = dbr.shape[1]
    d_context = mm(dbr, at[WO][...], NT).astype(BF16)
    at[DCTX][...] = d_context
    product = d_context.astype(F32) * context.astype(F32)
    high = product.astype(BF16)
    rest = (product - high.astype(F32)).astype(BF16)
    of_head = (
        lax.broadcasted_iota(jnp.int32, (16, width), 1) // HEAD_DIM
        == lax.broadcasted_iota(jnp.int32, (16, width), 0)
    )
    pick = jnp.where(of_head, 1.0, 0.0).astype(BF16)
    at[DELTA][...] = mm(pick, high, NT) + mm(pick, rest, NT)


BACK_READ = (N2, R2, GP, N1, R1, CTX, LSE, KID, QID, QKV)
SHARE_READ = (ACT, HID, X)
BACK_HELD = (G,) + BACK_READ + GRADS + (WIDE, DCTX, DELTA, DX, WQKV, WO, WU, WD)


def backward_kernel(section, g_row, n_in, n_old, n_out, *refs):
    ins, outs, refs = split_refs(n_in, n_old, n_out, refs)
    g_hbm, gain1, gain2, wq, wk, wv, wo, wu, wd = ins[:9]
    given = dict(zip(BACK_READ + SHARE_READ, ins[9:]))
    with_shares = section == 0
    out = dict(zip(GRADS + (DX,), outs))
    at = dict(zip(BACK_HELD + (SHARE_READ if with_shares else ()), refs))
    width, inner = at[WU].shape
    shared = Copies(at, refs[-1])
    shared.used = 40
    if with_shares:
        for name in SHARE_READ:
            shared.load(name, given[name], now=False)

        @pl.when(lax.axis_index(LAYER) != section)
        def _():
            others = Copies(at, refs[-1])
            others.used = 50
            for name in (DFFN, DUP, DBR, DQKV):
                others.load(name, out[name])
            others.load(CTX, given[CTX])
            shared.go()
            others.ready(DFFN, DUP, DBR, DQKV, CTX)

    @pl.when(lax.axis_index(LAYER) == section)
    def _():
        copies = Copies(at, refs[-1])

        def get(*names):
            for name in names:
                copies.load(name, given[name])

        def save(*names):
            for name in names:
                copies.store(at[name], out[name])

        copies.load(G, g_hbm.at[pl.ds(g_row * SEQ, SEQ), :])
        get(N2, R2)
        for name in (SUMS_A, SUMS_B):
            at[name][...] = jnp.zeros(at[name].shape, F32)
        copies.ready(G, N2, R2)
        copies.load(WD, wd.at[0])
        get(GP)
        second_norm_back(at, gain2, at[DFFN], 0)
        save(DFFN)
        copies.ready(WD, GP)
        copies.load(WU, wu.at[0])
        get(N1, R1)
        copies.load(WO, wo.at[0])
        get(CTX)

        def up(part):
            at[DUP][:, part] = up_back(at, at[DFFN][...], part)

        over_tiles(inner, inner // 4, up)
        save(DUP, SUMS_A)
        copies.ready(WU)
        get(QKV, KID, QID, LSE)
        load_qkv(copies, (wq, wk, wv), width)
        at[WIDE][...] += mm(at[DUP][...], at[WU][...], NT)
        copies.ready(N1, R1)
        first_norm_back(at, gain1, at[DBR], 0)
        save(DBR, SUMS_B)
        copies.ready(WO, CTX)
        context_back(at, at[DBR][...], at[CTX][...])
        copies.ready(QKV, KID, QID, LSE)
        if with_shares:
            shared.go()
        over_pairs(width, lambda j: attend_pair_back(j, width, at, at[DQKV], 0))
        save(DQKV, SUMS_C)
        copies.ready(WQKV)
        at[DX][...] = (at[WIDE][...] + mm(at[DQKV][...], at[WQKV][...], NT)).astype(BF16)
        save(DX)
        copies.finish()

    if not with_shares:
        return
    down, up, rest = at[WD], at[WU], refs[-2]
    shared.ready(*SHARE_READ)

    def to_down(part):
        down[part, :] = mm(at[ACT][:, part], at[DFFN][...], TN).astype(BF16)

    over_tiles(inner, width, to_down)
    shared.store(down, outs[-3])

    def to_up(part):
        up[:, part] = mm(at[HID][...], at[DUP][:, part], TN).astype(BF16)

    over_tiles(inner, width, to_up)
    shared.store(up, outs[-2])
    rest[:, 0:width] = mm(at[CTX][...], at[DBR][...], TN).astype(BF16)

    def to_rest(i, carry):
        made = mm(at[X][...], at[DQKV][:, lanes_at(i * width - width, width)], TN)
        rest[:, lanes_at(i * width, width)] = made.astype(BF16)
        return carry

    lax.fori_loop(1, 4, to_rest, 0)
    shared.store(rest, outs[-1])
    shared.finish()


def backward(section, g, g_row, params, kept, old):
    wq, _, wk, wv, _, wo, _, gain1, _, wu, _, wd, _, gain2, _ = params
    shapes = shapes_of(*wu.shape[1:])
    inputs = [(g, ANY), (gain1, WHOLE), (gain2, WHOLE)]
    inputs += [(array, ANY) for array in (wq, wk, wv, wo, wu, wd)]
    inputs += [(kept[name], ANY) for name in BACK_READ]
    outs, held = list(GRADS + (DX,)), list(BACK_HELD)
    if section == 0:
        inputs += [(kept[name], ANY) for name in SHARE_READ]
        outs += [WD, WU, REST]
        held += SHARE_READ + (REST,)
    made = call(
        partial(backward_kernel, section, g_row),
        "backward",
        inputs,
        {} if old is None else {i: old[name] for i, name in enumerate(GRADS)},
        [shapes[name] for name in outs],
        [shapes[name] for name in held],
        56,
    )
    return dict(zip(GRADS, made)), made[len(GRADS) :]


N_TILES = 4


def gradient_shapes(rows, columns):
    count = lax.axis_size(ROWS)
    if count == 16:
        return ((8, 2, rows // count, columns), BF16), [((8, rows // count, columns), BF16)] * 2
    return ((rows, columns), BF16), [((rows, columns), BF16)]


class GradientOut:
    def __init__(self, ref, targets, sems, first_sem, by_rows):
        self.ref, self.targets, self.sems, self.first_sem = ref, targets, sems, first_sem
        self.by_rows = by_rows
        self.plain = len(targets) == 1
        if self.plain:
            self.rows, self.columns = ref.shape
        else:
            self.rows, self.columns = ref.shape[0] * 2 * ref.shape[2], ref.shape[3]
        self.tile = (self.rows if by_rows else self.columns) // N_TILES

    def moves(self, i):
        start = i * self.tile
        if self.plain:
            at = (
                (pl.ds(start, self.tile), slice(None))
                if self.by_rows
                else (slice(None), lanes_at(start, self.tile))
            )
            pairs = [(self.ref.at[at], self.targets[0].at[at])]
        else:
            block = self.ref.shape[2]
            count = self.tile // (2 * block)
            core = lax.axis_index(ROWS) % 2
            pairs = []
            for target, which in zip(self.targets, (core, 1 - core)):
                if self.by_rows:
                    rows = pl.ds(i * count, count)
                    pairs.append((self.ref.at[rows, which], target.at[rows]))
                else:
                    lanes = lanes_at(start, self.tile)
                    pairs.append((self.ref.at[:, which, :, lanes], target.at[:, :, lanes]))
        base = self.first_sem + i * len(pairs)
        return [
            pltpu.make_async_copy(source, target, self.sems.at[base + k])
            for k, (source, target) in enumerate(pairs)
        ]

    def put(self, i, value):
        value = value.astype(BF16)
        start = i * self.tile
        if self.plain and self.by_rows:
            self.ref[pl.ds(pl.multiple_of(start, 16), self.tile), :] = value
        elif self.plain:
            self.ref[:, lanes_at(start, self.tile)] = value
        else:
            split = value.reshape(-1, 2, self.ref.shape[2], value.shape[1])
            if self.by_rows:
                self.ref[pl.ds(i * split.shape[0], split.shape[0])] = split
            else:
                self.ref[:, :, :, lanes_at(start, self.tile)] = split
        for move in self.moves(i):
            move.start()

    def finish(self):
        for i in range(N_TILES):
            for move in self.moves(i):
                move.wait()


def loop_tiles(step):
    def body(i, carry):
        step(i)
        return carry

    lax.fori_loop(0, N_TILES, body, 0)


def down_kernel(n_in, n_old, n_out, *refs):
    ins, outs, refs = split_refs(n_in, n_old, n_out, refs)
    g_hbm, gain2, n2, r2, act_hbm, share = ins
    dffn_out, sums_out, wide_out = outs[:3]
    at = dict(zip((G, N2, R2, WIDE, SUMS_A, ACT, DFFN, DX), refs))
    total, sems = refs[-2:]
    copies = Copies(at, sems)
    own = Copies(at, sems)
    own.used = 10
    own.load(G, g_hbm, now=False)
    own.load(N2, n2, now=False)
    own.load(R2, r2, now=False)
    for name, target in ((DFFN, dffn_out), (SUMS_A, sums_out), (WIDE, wide_out)):
        own.store(at[name], target, now=False)
    other = Copies(at, sems)
    other.used = 20
    other.load(DFFN, dffn_out, now=False)
    is_first = lax.axis_index(LAYER) == 0

    @pl.when(is_first)
    def _():
        own.go()
        at[SUMS_A][...] = jnp.zeros(at[SUMS_A].shape, F32)
        own.ready(G, N2, R2)

    copies.load(ACT, act_hbm)
    copies.load(DX, share)

    @pl.when(is_first)
    def _():
        second_norm_back(at, gain2, at[DFFN], 0)
        for way in own.stores:
            way.start()

    @pl.when(jnp.logical_not(is_first))
    def _():
        other.go()
        other.ready(DFFN)

    copies.ready(ACT, DX)
    way_out = GradientOut(total, outs[3:], sems, 24, True)

    def step(i):
        part = lanes_at(i * way_out.tile, way_out.tile)
        made = mm(at[ACT][:, part], at[DFFN][...], TN)
        way_out.put(i, made + at[DX][part, :].astype(F32))

    loop_tiles(step)
    way_out.finish()

    @pl.when(is_first)
    def _():
        own.finish()


def up_kernel(n_in, n_old, n_out, *refs):
    ins, outs, refs = split_refs(n_in, n_old, n_out, refs)
    wd_hbm, gp_hbm, hid_hbm, dffn_hbm, share = ins
    dup_out, sums_out = outs[:2]
    at = dict(zip((WD, GP, HID, DUP, DFFN, SUMS_A, DX), refs))
    total, sems = refs[-2:]
    is_first = lax.axis_index(LAYER) == 0
    way_out = GradientOut(total, outs[2:], sems, 24, False)
    copies = Copies(at, sems)
    copies.load(HID, hid_hbm)
    own = Copies(at, sems)
    own.used = 1
    own.load(DFFN, dffn_hbm, now=False)
    own.load(SUMS_A, sums_out, now=False)
    own.store(at[SUMS_A], sums_out, now=False)
    other = Copies(at, sems)
    other.used = 4
    other.load(DUP, dup_out, now=False)

    def fetch(i):
        part = lanes_at(i * way_out.tile, way_out.tile)
        pairs = (
            (share.at[:, part], at[DX].at[:, part]),
            (wd_hbm.at[0, part, :], at[WD].at[part, :]),
            (gp_hbm.at[:, part], at[GP].at[:, part]),
        )
        return [
            pltpu.make_async_copy(source, target, sems.at[8 + 3 * i + k])
            for k, (source, target) in enumerate(pairs)
        ]

    def away(i):
        part = lanes_at(i * way_out.tile, way_out.tile)
        return pltpu.make_async_copy(at[DUP].at[:, part], dup_out.at[:, part], sems.at[20 + i])

    def fetch_start(i):
        moves = fetch(i)
        moves[0].start()

        @pl.when(is_first)
        def _():
            for move in fetch(i)[1:]:
                move.start()

    @pl.when(is_first)
    def _():
        own.go()

    @pl.when(jnp.logical_not(is_first))
    def _():
        other.go()
        other.ready(DUP)

    fetch_start(0)
    copies.ready(HID)

    @pl.when(is_first)
    def _():
        own.ready(DFFN, SUMS_A)

    def step(i):
        @pl.when(i < N_TILES - 1)
        def _():
            fetch_start(i + 1)

        part = lanes_at(i * way_out.tile, way_out.tile)

        @pl.when(is_first)
        def _():
            for move in fetch(i)[1:]:
                move.wait()
            at[DUP][:, part] = up_back(at, at[DFFN][...], part)
            away(i).start()

        fetch(i)[0].wait()
        made = mm(at[HID][...], at[DUP][:, part], TN)
        way_out.put(i, made + at[DX][:, part].astype(F32))

    loop_tiles(step)
    way_out.finish()

    @pl.when(is_first)
    def _():
        own.stores[0].start()
        for i in range(N_TILES):
            away(i).wait()
        own.finish()


def middle_kernel(n_in, n_old, n_out, *refs):
    ins, outs, refs = split_refs(n_in, n_old, n_out, refs)
    dup_hbm, wide_in, wu_hbm, gain1, n1, r1, wo_hbm, ctx_hbm = ins
    at = dict(zip((DUP, WIDE, WU, N1, R1, WO, CTX, DBR, DCTX, DELTA, SUMS_B), refs))

    @pl.when(lax.axis_index(LAYER) == 0)
    def _():
        copies = Copies(at, refs[-1])
        parts = [pl.ds(i * at[DUP].shape[1] // 2, at[DUP].shape[1] // 2) for i in range(2)]

        def get_half(i):
            copies.load(DUP, dup_hbm.at[:, parts[i]], at[DUP].at[:, parts[i]])
            copies.load(WU, wu_hbm.at[0, :, parts[i]], at[WU].at[:, parts[i]])

        get_half(0)
        copies.load(WIDE, wide_in)
        at[SUMS_B][...] = jnp.zeros(at[SUMS_B].shape, F32)
        copies.ready(DUP, WU, WIDE)
        get_half(1)
        at[WIDE][...] += mm(at[DUP][:, parts[0]], at[WU][:, parts[0]], NT)
        copies.ready(DUP, WU)
        copies.load(N1, n1)
        copies.load(R1, r1)
        copies.load(WO, wo_hbm.at[0])
        copies.load(CTX, ctx_hbm)
        at[WIDE][...] += mm(at[DUP][:, parts[1]], at[WU][:, parts[1]], NT)
        copies.ready(N1, R1)
        first_norm_back(at, gain1, at[DBR], 0)
        for name, target in ((DBR, outs[0]), (WIDE, outs[1]), (SUMS_B, outs[4])):
            copies.store(at[name], target)
        copies.ready(WO, CTX)
        context_back(at, at[DBR][...], at[CTX][...])
        copies.store(at[DCTX], outs[2])
        copies.store(at[DELTA], outs[3])
        copies.finish()


ATTEND_READ = (QKV, DCTX, KID, QID, LSE, DELTA)


def attend_kernel(n_in, n_old, n_out, *refs):
    ins, outs, refs = split_refs(n_in, n_old, n_out, refs)
    x_hbm, ctx_hbm, dbr_hbm, share = ins[len(ATTEND_READ) :]
    dqkv_out, sums_out = outs[:2]
    at = dict(zip(ATTEND_READ + (X, CTX, DBR, DX, DQKV, SUMS_C), refs))
    total, sems = refs[-2:]
    width = at[X].shape[1]
    is_first = lax.axis_index(LAYER) == 0
    copies = Copies(at, sems)
    own = Copies(at, sems)
    own.used = 6
    for name, source in zip(ATTEND_READ, ins):
        own.load(name, source, now=False)
    own.store(at[DQKV], dqkv_out, now=False)
    own.store(at[SUMS_C], sums_out, now=False)
    other = Copies(at, sems)
    other.used = 20
    other.load(DQKV, dqkv_out, now=False)

    @pl.when(is_first)
    def _():
        own.go()
        own.ready(*ATTEND_READ)

    for name, source in ((X, x_hbm), (CTX, ctx_hbm), (DBR, dbr_hbm), (DX, share)):
        copies.load(name, source)

    @pl.when(is_first)
    def _():
        over_pairs(width, lambda j: attend_pair_back(j, width, at, at[DQKV], 0))
        for way in own.stores:
            way.start()

    @pl.when(jnp.logical_not(is_first))
    def _():
        other.go()
        other.ready(DQKV)

    copies.ready(X, CTX, DBR, DX)
    way_out = GradientOut(total, outs[2:], sems, 24, False)
    way_out.put(0, mm(at[CTX][...], at[DBR][...], TN) + at[DX][:, 0:width].astype(F32))

    def step(i, carry):
        made = mm(at[X][...], at[DQKV][:, lanes_at((i - 1) * width, width)], TN)
        way_out.put(i, made + at[DX][:, lanes_at(i * width, width)].astype(F32))
        return carry

    lax.fori_loop(1, N_TILES, step, 0)
    way_out.finish()

    @pl.when(is_first)
    def _():
        own.finish()


def input_kernel(n_in, n_old, n_out, *refs):
    ins, outs, refs = split_refs(n_in, n_old, n_out, refs)
    dqkv1, wide_in, wq, wk, wv = ins
    at = dict(zip((DQKV, WIDE, WQKV, DX), refs))

    @pl.when(lax.axis_index(LAYER) == 0)
    def _():
        copies = Copies(at, refs[-1])
        copies.load(DQKV, dqkv1)
        load_qkv(copies, (wq, wk, wv), at[WIDE].shape[1])
        copies.load(WIDE, wide_in)
        copies.ready(DQKV, WQKV, WIDE)
        at[DX][...] = (at[WIDE][...] + mm(at[DQKV][...], at[WQKV][...], NT)).astype(BF16)
        copies.store(at[DX], outs[0])
        copies.finish()


def swap(array, stride):
    count = lax.axis_size(ROWS)
    return lax.ppermute(array, ROWS, [(d, d ^ stride) for d in range(count)])


def halves_kernel(ways, merged, n_in, n_old, n_out, *refs):
    ins, outs, refs = split_refs(n_in, n_old, n_out, refs)
    copies = Copies({}, refs[-1])
    jobs = []
    for side in (0, 1):
        for way, (stride, before, after) in enumerate(ways):
            left, right, total = refs[3 * len(jobs) : 3 * len(jobs) + 3]
            size = total.shape[-1]
            own = (lax.axis_index(ROWS) // stride) % 2
            which = own if side else 1 - own
            sources = ins if n_in == 2 else ins[2 * way : 2 * way + 2]
            columns = pl.ds(way * size if n_in == 2 and len(ways) == 2 else 0, size)
            for i in range(before):
                taken = pl.ds((2 * i + which) * after, after)
                for source, buffer in zip(sources, (left, right)):
                    target = buffer.at[pl.ds(i * after, after)]
                    copies.load(len(jobs), source.at[taken, :, columns], target)
            if merged:
                target = outs[side].at[:, :, pl.ds(way * size, size)]
            else:
                target = outs[2 * way + side]
            jobs.append((left, right, total, target))
    for i, (left, right, total, target) in enumerate(jobs):
        copies.ready(i)
        total[...] = (left[...].astype(F32) + right[...].astype(F32)).astype(BF16)
        copies.store(total, target)
    copies.finish()


def halves(ways, arrays, merged=False):
    block = arrays[0].shape[1:]
    columns = block[1] // 2 if len(arrays) == 2 else block[1]
    parts = [((before * after, block[0], columns), BF16) for _, before, after in ways]
    if merged:
        outs = [((1, block[0], 2 * columns), BF16)] * 2
    else:
        outs = [part for part in parts for _ in (0, 1)]
    scratch = [part for _ in (0, 1) for part in parts for _ in range(3)]
    inputs = [(array, ANY) for array in arrays]
    return call(partial(halves_kernel, ways, merged), "halves", inputs, {}, outs, scratch, 32)


class ScatterSum:
    def __init__(self, blocks):
        self.shape = blocks[0].shape[1:]
        self.blocks = blocks
        self.done = 0
        self.plain = lax.axis_size(ROWS) != 16
        self.kept = blocks[0]

    def advance(self, first=None):
        if self.plain:
            return self.blocks[0]
        if first is not None:
            self.kept = lax.optimization_barrier((self.kept, first))[0]
        self.done += 1
        if self.done == 1:
            self.kept, send = self.blocks
            self.arrived = swap(send, 1)
            return send
        before = self.arrived
        if self.done == 2:
            made = halves(((2, 4, 1), (4, 2, 2)), (self.kept, before))
            self.kept = made[1::2]
            self.arrived = (swap(made[0], 2), swap(made[2], 4))
        elif self.done == 3:
            arrays = (self.kept[0], before[0], self.kept[1], before[1])
            made = halves(((4, 2, 1), (2, 2, 1)), arrays)
            self.kept = made[1::2]
            self.arrived = (swap(made[0], 4), swap(made[2], 2))
        else:
            arrays = (self.kept[0], before[0], self.kept[1], before[1])
            send, self.kept = halves(((8, 1, 1), (8, 1, 1)), arrays, True)
            self.arrived = swap(send, 8)
        return before

    def finish(self):
        if self.plain:
            total = lax.psum_scatter(self.blocks[0], ROWS, scatter_dimension=0, tiled=True)
            return total.astype(F32)
        while self.done < 4:
            self.advance()
        return (self.kept.astype(F32) + self.arrived.astype(F32)).reshape(self.shape)


def small_sum(values, beside, after):
    if lax.axis_size(ROWS) != 16:
        return lax.psum(values, ROWS)
    for stride, first in zip((1, 2, 4, 8), (*beside, None)):
        values = values + swap(values, stride)
        if first is not None:
            values = after(values, first)
    return values


def on_device(tokens, cotangent, segment_ids, valid_mask, cluster_perm, *params):
    section = lax.axis_index(LAYER)
    is_first = section == 0
    wq, _, wk, wv, _, wo, _, gain1, _, wu, _, wd, _, gain2, _ = params
    width, inner = wu.shape[1:]
    ids = (cluster_perm, segment_ids, valid_mask)
    shapes = shapes_of(width, inner)

    def hop(array, source, target):
        return lax.ppermute(array, LAYER, [(source, target)])

    def after(array, first):
        return lax.optimization_barrier((array, first))[0]

    row0, y0, stats00 = forward(0, 0, tokens, 0, ids, params, None)
    in0 = hop(y0, 0, 1)
    row1, y1, stats01 = forward(0, 1, tokens, 1, ids, params, None)
    in1 = hop(y1, 0, 1)
    row0, out0, stats10 = forward(1, 0, in0, 0, ids, params, row0)
    grads0, (dx0,) = backward(1, cotangent, 0, params, row0, None)
    in1 = after(in1, dx0)
    g0 = hop(dx0, 1, 0)
    row1, out1, stats11 = forward(1, 1, in1, 0, ids, params, row1)
    grads1, (dx1,) = backward(1, cotangent, 1, params, row1, None)
    g0 = after(g0, dx1)
    g1 = hop(dx1, 1, 0)
    grads0, (dx0, down_share, up_share, rest_share) = backward(0, g0, 0, params, row0, grads0)
    g1 = after(g1, dx0)

    def at_hbm(*arrays):
        return [(array, ANY) for array in arrays]

    def of(*names):
        return [shapes[name] for name in names]

    total, parts = gradient_shapes(inner, width)
    made = call(
        down_kernel,
        "down_gradient",
        at_hbm(g1)
        + [(gain2, WHOLE)]
        + at_hbm(row1[N2], row1[R2], row1[ACT], down_share),
        {0: grads1[DFFN], 1: grads1[SUMS_A]},
        of(DFFN, SUMS_A, WIDE) + parts,
        of(G, N2, R2, WIDE, SUMS_A, ACT, DFFN) + of(WD) + [total],
        40,
    )
    dffn1, sums_a1, wide = made[:3]
    down_sum = ScatterSum(made[3:])
    down_sum.advance()

    total, parts = gradient_shapes(width, inner)
    made = call(
        up_kernel,
        "up_gradient",
        at_hbm(wd, row1[GP], row1[HID], dffn1, up_share),
        {0: grads1[DUP], 1: sums_a1},
        of(DUP, SUMS_A) + parts,
        of(WD, GP, HID, DUP, DFFN, SUMS_A) + of(WU) + [total],
        40,
    )
    dup1, sums_a1 = made[:2]
    down_sum.advance(dup1)
    up_sum = ScatterSum(after(tuple(made[2:]), down_sum.kept))
    up_sum.advance()
    wide = after(wide, down_sum.kept)

    made = call(
        middle_kernel,
        "middle",
        at_hbm(dup1, wide, wu) + [(gain1, WHOLE)] + at_hbm(row1[N1], row1[R1], wo, row1[CTX]),
        {0: grads1[DBR], 4: grads1[SUMS_B]},
        of(DBR, WIDE, DCTX, DELTA, SUMS_B),
        of(DUP, WIDE, WU, N1, R1, WO, CTX, DBR, DCTX, DELTA, SUMS_B),
        20,
    )
    dbr1, wide, dctx, delta, sums_b1 = made
    up_sum.advance(dctx)
    dctx = after(dctx, up_sum.kept)

    total, parts = gradient_shapes(width, 4 * width)
    made = call(
        attend_kernel,
        "attend_gradient",
        at_hbm(row1[QKV], dctx, *(row1[name] for name in (KID, QID, LSE)), delta)
        + at_hbm(row1[X], row1[CTX], dbr1, rest_share),
        {0: grads1[DQKV], 1: grads1[SUMS_C]},
        of(DQKV, SUMS_C) + parts,
        of(*ATTEND_READ) + of(X, CTX, DBR) + of(REST) + of(DQKV, SUMS_C) + [total],
        40,
    )
    dqkv1, sums_c1 = made[:2]
    down_sum.advance(dqkv1)
    up_sum.advance(down_sum.kept)
    rest_sum = ScatterSum(after(tuple(made[2:]), (down_sum.kept, up_sum.kept)))
    rest_sum.advance()
    wide = after(wide, up_sum.kept)
    made = call(
        input_kernel,
        "input_gradient",
        at_hbm(dqkv1, wide, wq, wk, wv),
        {},
        of(DX),
        of(DQKV, WIDE, WQKV, DX),
        8,
    )
    dx1 = made[0]
    came = [rest_sum.advance(dx1)]
    down_sum.advance(rest_sum.kept)
    up_sum.advance(down_sum.kept)
    came.append(rest_sum.advance(up_sum.kept))
    came.append(rest_sum.advance())

    sums_a1, sums_b1, sums_c1 = (after(array, dx1) for array in (sums_a1, sums_b1, sums_c1))
    stats10 = after(stats10, dx1)
    sum_a = (grads0[SUMS_A] + sums_a1).reshape(4, 8, inner).sum(axis=1)
    sum_b = (grads0[SUMS_B] + sums_b1).reshape(3, 8, width).sum(axis=1)
    sum_c = (grads0[SUMS_C] + sums_c1).reshape(2, 8, width).sum(axis=1)
    stats = jnp.where(is_first, stats00 + stats01, stats10 + stats11)
    stats = stats.reshape(3, 8 * width).sum(axis=1)
    count = jnp.sum(valid_mask.astype(F32))
    pieces = [sum_a[:3, :width].reshape(-1), sum_b.reshape(-1), sum_c.reshape(-1), sum_a[3]]
    base = 8 * width + inner
    spare = -(base + 4) % (8 * LANES)
    tail = jnp.concatenate([stats, jnp.broadcast_to(count, (1,)), jnp.zeros((spare,), F32)])
    small = jnp.concatenate(pieces + [tail]).reshape(-1, LANES)
    small = small_sum(small, came, after).reshape(-1)
    w_down = down_sum.finish()
    w_up = up_sum.finish()
    w_rest = rest_sum.finish()
    shares = lax.axis_size(ROWS)
    me = lax.axis_index(ROWS)

    def small_part(place, size):
        own = size // shares
        return lax.dynamic_slice_in_dim(small, place * width + me * own, own, 0)[None]

    gain2_sum, shift2_sum, down_bias, gain1_sum, shift1_sum, out_bias, query_bias, value_bias = (
        small_part(i, width) for i in range(8)
    )
    up_bias = small_part(8, inner)
    root_means = jnp.sqrt(small[base : base + 3] / (small[base + 3] * width))[None, :]

    half = width // 2
    dx0, out0, out1 = (after(array, dx1) for array in (dx0, out0, out1))
    outgoing = jnp.concatenate(
        [
            jnp.where(is_first, grad[:, half:], made[:, :half])
            for grad, made in ((dx0, out0), (dx1, out1))
        ]
    )
    arrived = lax.ppermute(outgoing, LAYER, [(0, 1), (1, 0)])
    block_own = jnp.concatenate([out0[:, half:], out1[:, half:]])
    grad_own = jnp.concatenate([dx0[:, :half], dx1[:, :half]])
    block_part = jnp.where(is_first, arrived, block_own)
    grad_part = jnp.where(is_first, grad_own, arrived)
    return (
        block_part,
        grad_part,
        w_rest[None, :, width : 2 * width],
        query_bias,
        w_rest[None, :, 2 * width : 3 * width],
        w_rest[None, :, 3 * width :],
        value_bias,
        w_rest[None, :, :width],
        out_bias,
        gain1_sum,
        shift1_sum,
        w_up[None],
        up_bias,
        w_down[None],
        down_bias,
        gain2_sum,
        shift2_sum,
        root_means,
    )


def solution(mesh):
    by_layer = P(LAYER, None)
    matrix = P(LAYER, None, None)
    share = P(LAYER, ROWS)
    matrix_share = P(LAYER, ROWS, None)
    rows = P(ROWS, None)
    vectors = {1, 4, 6, 7, 8, 10, 12, 13, 14}
    matrices = {2, 4, 5, 7, 11, 13}
    return jax.shard_map(
        on_device,
        mesh=mesh,
        in_specs=(rows, rows, rows, rows, P(LAYER, ROWS, None, None))
        + tuple(by_layer if i in vectors else matrix for i in range(15)),
        out_specs=(P(ROWS, LAYER), P(ROWS, LAYER))
        + tuple(matrix_share if i in matrices else share for i in range(2, 17))
        + (P(LAYER, None),),
        check_vma=False,
    )
```

```python
from functools import partial

import jax
import jax.numpy as jnp
from jax import lax
from jax.experimental import pallas as pl
from jax.experimental.pallas import tpu as pltpu
from jax.sharding import PartitionSpec as P

HEAD_DIM = 64
CLUSTER = 128
SEQ = 512
LANES = 128
ROW_BLOCK = 128
PAIR_UNROLL = 2
MIB = 1024 * 1024

BF16 = jnp.bfloat16
F32 = jnp.float32
LOG2E = 1.4426950408889634
SCALE = HEAD_DIM**-0.5
SCORE_SCALE = SCALE * LOG2E

NN = ((1,), (0,))
NT = ((1,), (1,))
TN = ((0,), (0,))

ROWS = "dp"
LAYER = "section"
ANY = pl.BlockSpec(memory_space=pltpu.HBM)
WHOLE = pl.BlockSpec(memory_space=pltpu.VMEM)
SHORT = pl.CostEstimate(flops=1, bytes_accessed=1, transcendentals=0)

X, QKV, CTX, LSE, KID, QID, N1, R1, HID, ACT, GP, N2, R2 = range(13)
G, DFFN, DUP, DBR, DQKV, SUMS_A, SUMS_B, SUMS_C, WIDE, DCTX, DELTA, DX, FEED, LIVE = range(13, 27)
BIAS, WQKV, Y, STATS, WO, WU, WD, REST = range(27, 35)
SAVED = (X, QKV, CTX, LSE, KID, QID, N1, R1, HID, ACT, GP, N2, R2)
GRADS = (DFFN, DUP, DBR, DQKV, SUMS_A, SUMS_B, SUMS_C)
GAIN2, SHIFT2, B_DOWN, B_UP = 0, 8, 16, 24
GAIN1, SHIFT1, B_OUT = 0, 8, 16
B_QUERY, B_VALUE = 0, 8


def shapes_of(width, inner):
    token, token32, narrow = ((SEQ, width), BF16), ((SEQ, width), F32), ((SEQ, LANES), F32)
    heads = ((16, SEQ), F32)
    shapes = {name: token for name in (X, CTX, N1, HID, N2, G, DFFN, DBR, DCTX, DX, Y)}
    shapes.update({name: token32 for name in (KID, WIDE, FEED)})
    shapes.update({name: narrow for name in (R1, R2, LIVE)})
    shapes.update({name: heads for name in (LSE, QID, DELTA)})
    shapes.update({name: ((SEQ, inner), BF16) for name in (ACT, GP, DUP)})
    shapes.update({name: ((SEQ, 3 * width), BF16) for name in (QKV, DQKV)})
    shapes.update({SUMS_A: ((32, inner), F32), SUMS_B: ((24, width), F32)})
    shapes.update({SUMS_C: ((16, width), F32), STATS: ((24, width), F32), BIAS: ((8, width), F32)})
    shapes.update({WQKV: ((width, 3 * width), BF16), WO: ((width, width), BF16)})
    shapes.update({WU: ((width, inner), BF16), WD: ((inner, width), BF16)})
    shapes[REST] = ((width, 4 * width), BF16)
    return shapes


def mm(left, right, dims):
    return lax.dot_general(left, right, (dims, ((), ())), preferred_element_type=F32)


def vec(ref):
    return ref[0:1, :].astype(F32)


def lanes_at(start, size=LANES):
    return pl.ds(pl.multiple_of(start, LANES), size)


def fold8(block):
    return jnp.sum(block.reshape(-1, 8, block.shape[-1]), axis=0)


def over_rows(step):
    def body(i, carry):
        step(pl.ds(pl.multiple_of(i * ROW_BLOCK, ROW_BLOCK), ROW_BLOCK))
        return carry

    lax.fori_loop(0, SEQ // ROW_BLOCK, body, 0)


def over_tiles(size, tile, step):
    def body(i, carry):
        step(pl.ds(pl.multiple_of(i * tile, tile), tile))
        return carry

    lax.fori_loop(0, size // tile, body, 0)


class Copies:
    def __init__(self, at, sems):
        self.at, self.sems = at, sems
        self.used = 0
        self.loads = {}
        self.stores = []

    def plan(self, source, target):
        self.used += 1
        return pltpu.make_async_copy(source, target, self.sems.at[self.used - 1])

    def load(self, name, source, target=None, now=True):
        target = self.at[name] if target is None else target
        copy = self.plan(source, target)
        self.loads.setdefault(name, []).append(copy)
        if now:
            copy.start()

    def go(self):
        for copies in self.loads.values():
            for copy in copies:
                copy.start()

    def ready(self, *names):
        for name in names:
            for copy in self.loads.pop(name, ()):
                copy.wait()

    def store(self, source, target, now=True):
        copy = self.plan(source, target)
        self.stores.append(copy)
        if now:
            copy.start()
        return copy

    def finish(self):
        for copy in self.stores:
            copy.wait()


def load_qkv(copies, weights, width):
    for i, weight in enumerate(weights):
        copies.load(WQKV, weight.at[0], copies.at[WQKV].at[:, pl.ds(i * width, width)])


def call(body, name, inputs, old, outs, scratch, n_sems):
    arrays = [array for array, _ in inputs]
    n_in = len(arrays)
    return pl.pallas_call(
        partial(body, n_in, len(old), len(outs)),
        out_shape=[jax.ShapeDtypeStruct(*shape) for shape in outs],
        in_specs=[spec for _, spec in inputs] + [ANY] * len(old),
        out_specs=[ANY] * len(outs),
        input_output_aliases={n_in + i: place for i, place in enumerate(old)},
        scratch_shapes=[pltpu.VMEM(*shape) for shape in scratch]
        + [pltpu.SemaphoreType.DMA((n_sems,))],
        compiler_params=pltpu.CompilerParams(vmem_limit_bytes=58 * MIB),
        cost_estimate=SHORT,
        name=name,
    )(*arrays, *old.values())


def split_refs(n_in, n_old, n_out, refs):
    return refs[:n_in], refs[n_in + n_old : n_in + n_old + n_out], refs[n_in + n_old + n_out :]


def low_lanes():
    return lax.broadcasted_iota(jnp.int32, (SEQ, LANES), 1) < HEAD_DIM


def masked(scores, kid_column, qid_row):
    shape = (CLUSTER, CLUSTER)
    same = lax.broadcasted_iota(jnp.int32, shape, 0) == lax.broadcasted_iota(jnp.int32, shape, 1)
    count = SEQ // CLUSTER
    parts = [slice(i * CLUSTER, (i + 1) * CLUSTER) for i in range(count)]
    rows = []
    for i in range(count):
        tiles = []
        for j in range(count):
            ok = kid_column[parts[i]] == qid_row[:, parts[j]]
            if i == j:
                ok = ok | same
            tiles.append(jnp.where(ok, scores[parts[i], parts[j]], -1e30))
        rows.append(jnp.concatenate(tiles, axis=1))
    return jnp.concatenate(rows, axis=0)


def attend_pair(j, width, at):
    low = low_lanes()
    lanes = lanes_at(j * LANES)
    query = at[QKV][:, lanes]
    key = at[QKV][:, lanes_at(width + j * LANES)]
    value = at[QKV][:, lanes_at(2 * width + j * LANES)]
    kid_pair = at[KID][:, lanes]
    mixed, tops = [], []
    for half in (0, 1):
        own = low if half == 0 else ~low
        own_query = jnp.where(own, query, jnp.zeros_like(query))
        value_ones = jnp.where(own, value, jnp.ones_like(value))
        kid_column = kid_pair[:, half * HEAD_DIM : half * HEAD_DIM + 1]
        scores = mm(key, own_query, NT) * SCORE_SCALE
        scores = masked(scores, kid_column, at[QID][pl.ds(2 * j + half, 1), :])
        top = jnp.max(scores, axis=0, keepdims=True)
        tops.append(top)
        mixed.append(mm(jnp.exp2(scores - top).astype(BF16), value_ones, TN))
    sums = [pltpu.roll(part, HEAD_DIM, 1) for part in mixed]
    total = jnp.where(low, sums[0], sums[1])
    at[CTX][:, lanes] = (jnp.where(low, mixed[0], mixed[1]) / total).astype(BF16)
    turned = total.T
    for half in (0, 1):
        row = turned[half * HEAD_DIM : half * HEAD_DIM + 1, :]
        at[LSE][pl.ds(2 * j + half, 1), :] = tops[half] + jnp.log2(row)


def attend_pair_back(j, width, at, target, base):
    low = low_lanes()
    lanes = [lanes_at(i * width + j * LANES) for i in range(3)]
    query, key, value = (at[QKV][:, part] for part in lanes)
    d_out = at[DCTX][:, lanes[0]]
    kid_pair = at[KID][:, lanes[0]]
    d_query, d_key, d_value = [], [], []
    for half in (0, 1):
        h = pl.ds(2 * j + half, 1)
        own = low if half == 0 else ~low
        own_query = jnp.where(own, query, jnp.zeros_like(query))
        own_out = jnp.where(own, d_out, jnp.zeros_like(d_out))
        kid_column = kid_pair[:, half * HEAD_DIM : half * HEAD_DIM + 1]
        scores = mm(key, own_query, NT) * SCORE_SCALE - at[LSE][h, :]
        weights = jnp.exp2(masked(scores, kid_column, at[QID][h, :]))
        d_weights = mm(value, own_out, NT)
        d_scores = (weights * (d_weights - at[DELTA][h, :])).astype(BF16)
        d_value.append(mm(weights.astype(BF16), own_out, NN))
        d_key.append(mm(d_scores, own_query, NN))
        d_query.append(mm(d_scores, key, TN))
    made = (
        jnp.where(low, d_query[0], d_query[1]) * SCALE,
        (d_key[0] + d_key[1]) * SCALE,
        d_value[0] + d_value[1],
    )
    rows = pl.ds(base, SEQ)
    for i, place in ((0, B_QUERY), (1, None), (2, B_VALUE)):
        rounded = made[i].astype(BF16)
        target[rows, lanes[i]] = rounded
        if place is not None:
            at[SUMS_C][place : place + 8, lanes[0]] = fold8(rounded.astype(F32))


def over_pairs(width, step):
    def body(j, carry):
        step(j)
        return carry

    lax.fori_loop(0, width // LANES, body, 0, unroll=PAIR_UNROLL)


def token_ids(row, heads, perm_ref, seg_ref, valid_ref, kid_ref, qid_ref):
    token = lax.broadcasted_iota(jnp.int32, (SEQ, LANES), 0)
    lane = lax.broadcasted_iota(jnp.int32, (SEQ, LANES), 1)
    seg_row = seg_ref[row : row + 1, :].astype(F32)
    valid_row = valid_ref[row : row + 1, :].astype(F32)
    at = lax.broadcasted_iota(jnp.int32, (LANES, SEQ), 0)
    both = jnp.where(at == 0, seg_row, jnp.where(at == 1, valid_row, 0.0)).T
    segment, live = both[:, 0:1], both[:, 1:2]

    def column(h):
        places = perm_ref[0, row, pl.ds(h, 1), :]
        mine = jnp.zeros((SEQ, LANES), F32)
        for c in range(1, SEQ // CLUSTER):
            part = places[:, c * CLUSTER : (c + 1) * CLUSTER]
            mine = jnp.where(token == part, float(c), mine)
        return jnp.sum(mine, axis=1, keepdims=True) * 4.0 + segment

    def pair(j, ids):
        left, right = column(2 * j), column(2 * j + 1)
        own = jnp.where(lane < HEAD_DIM, left, right)
        kid_ref[:, lanes_at(j * LANES)] = jnp.where(live > 0.5, own, -1.0)
        ids = jnp.where(lane == 2 * j, left, ids)
        return jnp.where(lane == 2 * j + 1, right, ids)

    qid = lax.fori_loop(0, heads // 2, pair, jnp.zeros((SEQ, LANES), F32))
    qid_ref[...] = qid.T[0:16, :]
    return live


def normed(total):
    centre = total - jnp.mean(total, axis=-1, keepdims=True)
    spread = jnp.mean(centre * centre, axis=-1, keepdims=True)
    rate = lax.rsqrt(spread + 1e-05)
    return centre * rate, rate


FORWARD_HELD = SAVED + (WQKV, WO, WU, WD, WIDE, FEED, Y, STATS, LIVE, BIAS)


def run_forward(at, copies, save, row, source, ids, params, later=None):
    perm_ref, seg_ref, valid_ref = ids
    wq, bq, wk, wv, bv, wo, bo, g1, s1, wu, bu, wd, bd, g2, s2 = params
    width, inner = at[WU].shape
    heads = width // HEAD_DIM
    copies.load(X, source)
    first = copies.used
    load_qkv(copies, (wq, wk, wv), width)
    live = token_ids(row, heads, perm_ref, seg_ref, valid_ref, at[KID], at[QID])
    at[LIVE][...] = jnp.broadcast_to(live, (SEQ, LANES))
    at[LSE][...] = jnp.zeros((16, SEQ), F32)
    at[STATS][...] = jnp.zeros((24, width), F32)
    at[BIAS][0:1, :] = vec(bq)
    at[BIAS][1:2, :] = jnp.zeros((1, width), F32)
    at[BIAS][2:3, :] = vec(bv)
    copies.ready(X)

    def to_qkv(i, carry):
        part = pl.ds(pl.multiple_of(i * width, LANES), width)
        weight = at[WQKV].at[:, part]
        pltpu.make_async_copy(weight, weight, copies.sems.at[first + i]).wait()
        made = mm(at[X][...], at[WQKV][:, part], NN) + at[BIAS][pl.ds(i, 1), :]
        at[QKV][:, part] = made.astype(BF16)
        return carry

    lax.fori_loop(0, 3, to_qkv, 0)
    copies.loads.pop(WQKV)
    copies.load(WO, wo.at[0])
    copies.load(WU, wu.at[0])
    copies.load(WD, wd.at[0])
    if later is not None:
        later()
    save(KID, QID, X, QKV)
    over_pairs(width, lambda j: attend_pair(j, width, at))
    save(LSE, CTX)
    copies.ready(WO)
    at[WIDE][...] = mm(at[CTX][...], at[WO][...], NN)

    def first_norm(rows):
        branch = at[WIDE][rows, :] + vec(bo)
        alive = at[LIVE][rows, 0:1]
        at[STATS][0:8, :] += fold8(branch * branch * alive)
        unit, rate = normed(at[X][rows, :].astype(F32) + branch)
        hidden = unit * vec(g1) + vec(s1)
        at[N1][rows, :] = unit.astype(BF16)
        at[R1][rows, :] = jnp.broadcast_to(rate, (ROW_BLOCK, LANES))
        at[HID][rows, :] = hidden.astype(BF16)
        at[WIDE][rows, :] = hidden

    over_rows(first_norm)
    save(N1, R1, HID)
    copies.ready(WU)

    def up(part):
        upper = mm(at[HID][...], at[WU][:, part], NN) + bu[0:1, part].astype(F32)
        half = 0.5 + 0.5 * lax.erf(upper * 0.5**0.5)
        bell = jnp.exp2(upper * upper * (-0.5 * LOG2E)) * 0.3989422804014327
        at[ACT][:, part] = (upper * half).astype(BF16)
        at[GP][:, part] = (half + upper * bell).astype(BF16)

    over_tiles(inner, inner // 4, up)
    save(ACT, GP)
    copies.ready(WD)
    at[FEED][...] = mm(at[ACT][...], at[WD][...], NN)

    def second_norm(rows):
        ffn = at[FEED][rows, :] + vec(bd)
        alive = at[LIVE][rows, 0:1]
        at[STATS][8:16, :] += fold8(ffn * ffn * alive)
        unit, rate = normed(at[WIDE][rows, :] + ffn)
        result = unit * vec(g2) + vec(s2)
        at[STATS][16:24, :] += fold8(result * result * alive)
        at[N2][rows, :] = unit.astype(BF16)
        at[R2][rows, :] = jnp.broadcast_to(rate, (ROW_BLOCK, LANES))
        at[Y][rows, :] = result.astype(BF16)

    over_rows(second_norm)
    save(Y, STATS, N2, R2)


def forward_kernel(section, row, x_row, n_in, n_old, n_out, *refs):
    ins, outs, refs = split_refs(n_in, n_old, n_out, refs)
    out = dict(zip(SAVED + (Y, STATS), outs))
    at = dict(zip(FORWARD_HELD, refs))

    @pl.when(lax.axis_index(LAYER) == section)
    def _():
        copies = Copies(at, refs[-1])

        def save(*names):
            for name in names:
                copies.store(at[name], out[name])

        source = ins[0].at[pl.ds(x_row * SEQ, SEQ), :]
        run_forward(at, copies, save, row, source, ins[1:4], ins[4:])
        copies.finish()


def forward(section, row, x, x_row, ids, params, kept):
    width, inner = params[9].shape[1:]
    shapes = shapes_of(width, inner)
    inputs = [(x, ANY)] + [(array, WHOLE) for array in ids]
    inputs += [(array, ANY if array.ndim == 3 else WHOLE) for array in params]
    made = call(
        partial(forward_kernel, section, row, x_row),
        "forward",
        inputs,
        {} if kept is None else {i: kept[name] for i, name in enumerate(SAVED)},
        [shapes[name] for name in SAVED + (Y, STATS)],
        [shapes[name] for name in FORWARD_HELD],
        32,
    )
    return dict(zip(SAVED, made)), made[-2], made[-1]


def norm_back(grad, unit, rate, gain):
    scaled = grad * gain
    mean = jnp.mean(scaled, axis=-1, keepdims=True)
    along = jnp.mean(scaled * unit, axis=-1, keepdims=True)
    return (scaled - mean - unit * along) * rate


def add_sum(ref, place, value):
    ref[place : place + 8, 0 : value.shape[-1]] += fold8(value)


def second_norm_back(at, gain2, target, base):
    def step(rows):
        grad = at[G][rows, :].astype(F32)
        unit = at[N2][rows, :].astype(F32)
        add_sum(at[SUMS_A], GAIN2, grad * unit)
        add_sum(at[SUMS_A], SHIFT2, grad)
        d_second = norm_back(grad, unit, at[R2][rows, 0:1], vec(gain2))
        at[WIDE][rows, :] = d_second
        low = d_second.astype(BF16)
        target[pl.ds(pl.multiple_of(rows.start + base, ROW_BLOCK), ROW_BLOCK), :] = low
        add_sum(at[SUMS_A], B_DOWN, low.astype(F32))

    over_rows(step)


def up_back(at, dffn, part):
    d_act = mm(dffn, at[WD][part, :], NT)
    low = (d_act * at[GP][:, part].astype(F32)).astype(BF16)
    at[SUMS_A][B_UP : B_UP + 8, part] += fold8(low.astype(F32))
    return low


def first_norm_back(at, gain1, target, base):
    def step(rows):
        grad = at[WIDE][rows, :]
        unit = at[N1][rows, :].astype(F32)
        add_sum(at[SUMS_B], GAIN1, grad * unit)
        add_sum(at[SUMS_B], SHIFT1, grad)
        d_first = norm_back(grad, unit, at[R1][rows, 0:1], vec(gain1))
        at[WIDE][rows, :] = d_first
        low = d_first.astype(BF16)
        target[pl.ds(pl.multiple_of(rows.start + base, ROW_BLOCK), ROW_BLOCK), :] = low
        add_sum(at[SUMS_B], B_OUT, low.astype(F32))

    over_rows(step)


def context_back(at, dbr, context):
    width = dbr.shape[1]
    d_context = mm(dbr, at[WO][...], NT).astype(BF16)
    at[DCTX][...] = d_context
    product = d_context.astype(F32) * context.astype(F32)
    high = product.astype(BF16)
    rest = (product - high.astype(F32)).astype(BF16)
    of_head = (
        lax.broadcasted_iota(jnp.int32, (16, width), 1) // HEAD_DIM
        == lax.broadcasted_iota(jnp.int32, (16, width), 0)
    )
    pick = jnp.where(of_head, 1.0, 0.0).astype(BF16)
    at[DELTA][...] = mm(pick, high, NT) + mm(pick, rest, NT)


def run_backward(at, copies, get, save, params, shared):
    gain1, gain2 = params[:2]
    width, inner = at[WU].shape
    get(G, N2, R2)
    for name in (SUMS_A, SUMS_B):
        at[name][...] = jnp.zeros(at[name].shape, F32)
    copies.ready(G, N2, R2)
    get(WD, GP)
    second_norm_back(at, gain2, at[DFFN], 0)
    save(DFFN)
    get(WU, N1, R1, WO, CTX)
    copies.ready(WD, GP)

    def up(part):
        at[DUP][:, part] = up_back(at, at[DFFN][...], part)

    over_tiles(inner, inner // 4, up)
    save(DUP, SUMS_A)
    get(QKV, KID, QID, LSE, WQKV)
    copies.ready(WU)
    at[WIDE][...] += mm(at[DUP][...], at[WU][...], NT)
    copies.ready(N1, R1)
    first_norm_back(at, gain1, at[DBR], 0)
    save(DBR, SUMS_B)
    copies.ready(WO, CTX)
    context_back(at, at[DBR][...], at[CTX][...])
    copies.ready(QKV, KID, QID, LSE)
    if shared is not None:
        shared.go()
    over_pairs(width, lambda j: attend_pair_back(j, width, at, at[DQKV], 0))
    save(DQKV, SUMS_C)
    copies.ready(WQKV)
    at[DX][...] = (at[WIDE][...] + mm(at[DQKV][...], at[WQKV][...], NT)).astype(BF16)
    save(DX)


BACK_READ = (N2, R2, GP, N1, R1, CTX, LSE, KID, QID, QKV)
SHARE_READ = (ACT, HID, X)
BACK_HELD = (G,) + BACK_READ + GRADS + (WIDE, DCTX, DELTA, DX, WQKV, WO, WU, WD)


def backward_kernel(section, g_row, n_in, n_old, n_out, *refs):
    ins, outs, refs = split_refs(n_in, n_old, n_out, refs)
    g_hbm, gain1, gain2, wq, wk, wv, wo, wu, wd = ins[:9]
    given = dict(zip(BACK_READ + SHARE_READ, ins[9:]))
    given.update({WO: wo.at[0], WU: wu.at[0], WD: wd.at[0]})
    given[G] = g_hbm.at[pl.ds(g_row * SEQ, SEQ), :]
    with_shares = section == 0
    out = dict(zip(GRADS + (DX,), outs))
    at = dict(zip(BACK_HELD + (SHARE_READ if with_shares else ()), refs))
    width, inner = at[WU].shape
    shared = Copies(at, refs[-1])
    shared.used = 40
    if with_shares:
        for name in SHARE_READ:
            shared.load(name, given[name], now=False)

        @pl.when(lax.axis_index(LAYER) != section)
        def _():
            others = Copies(at, refs[-1])
            others.used = 50
            for name in (DFFN, DUP, DBR, DQKV):
                others.load(name, out[name])
            others.load(CTX, given[CTX])
            shared.go()
            others.ready(DFFN, DUP, DBR, DQKV, CTX)

    @pl.when(lax.axis_index(LAYER) == section)
    def _():
        copies = Copies(at, refs[-1])

        def get(*names):
            for name in names:
                if name == WQKV:
                    load_qkv(copies, (wq, wk, wv), width)
                else:
                    copies.load(name, given[name])

        def save(*names):
            for name in names:
                copies.store(at[name], out[name])

        run_backward(at, copies, get, save, ins[1:3], shared if with_shares else None)
        copies.finish()

    if not with_shares:
        return
    down, up, rest = at[WD], at[WU], refs[-2]
    shared.ready(*SHARE_READ)

    def to_down(part):
        down[part, :] = mm(at[ACT][:, part], at[DFFN][...], TN).astype(BF16)

    over_tiles(inner, width, to_down)
    shared.store(down, outs[-3])

    def to_up(part):
        up[:, part] = mm(at[HID][...], at[DUP][:, part], TN).astype(BF16)

    over_tiles(inner, width, to_up)
    shared.store(up, outs[-2])
    rest[:, 0:width] = mm(at[CTX][...], at[DBR][...], TN).astype(BF16)

    def to_rest(i, carry):
        made = mm(at[X][...], at[DQKV][:, lanes_at(i * width - width, width)], TN)
        rest[:, lanes_at(i * width, width)] = made.astype(BF16)
        return carry

    lax.fori_loop(1, 4, to_rest, 0)
    shared.store(rest, outs[-1])
    shared.finish()


def backward(section, g, g_row, params, kept, old):
    wq, _, wk, wv, _, wo, _, gain1, _, wu, _, wd, _, gain2, _ = params
    shapes = shapes_of(*wu.shape[1:])
    inputs = [(g, ANY), (gain1, WHOLE), (gain2, WHOLE)]
    inputs += [(array, ANY) for array in (wq, wk, wv, wo, wu, wd)]
    inputs += [(kept[name], ANY) for name in BACK_READ]
    outs, held = list(GRADS + (DX,)), list(BACK_HELD)
    if section == 0:
        inputs += [(kept[name], ANY) for name in SHARE_READ]
        outs += [WD, WU, REST]
        held += SHARE_READ + (REST,)
    made = call(
        partial(backward_kernel, section, g_row),
        "backward",
        inputs,
        {} if old is None else {i: old[name] for i, name in enumerate(GRADS)},
        [shapes[name] for name in outs],
        [shapes[name] for name in held],
        56,
    )
    return dict(zip(GRADS, made)), made[len(GRADS) :]


KEPT = (X, CTX, HID, ACT)
BOTH_HELD = FORWARD_HELD + (G,) + GRADS + (DCTX, DELTA, DX)


def both_kernel(row, n_in, n_old, n_out, *refs):
    ins, outs, refs = split_refs(n_in, n_old, n_out, refs)
    out = dict(zip(KEPT + (Y, STATS) + GRADS + (DX,), outs))
    at = dict(zip(BOTH_HELD, refs))
    params = ins[5:]

    @pl.when(lax.axis_index(LAYER) == 1)
    def _():
        copies = Copies(at, refs[-1])

        def save(*names):
            for name in names:
                if name in out:
                    copies.store(at[name], out[name])

        def get(*names):
            pass

        def later():
            copies.load(G, ins[1].at[pl.ds(row * SEQ, SEQ), :])

        run_forward(at, copies, save, row, ins[0], ins[2:5], params, later)
        run_backward(at, copies, get, save, (params[7], params[13]), None)
        copies.finish()


def through_and_back(row, x, g, ids, params, kept):
    shapes = shapes_of(*params[9].shape[1:])
    inputs = [(x, ANY), (g, ANY)] + [(array, WHOLE) for array in ids]
    inputs += [(array, ANY if array.ndim == 3 else WHOLE) for array in params]
    names = KEPT + (Y, STATS) + GRADS + (DX,)
    made = call(
        partial(both_kernel, row),
        "both",
        inputs,
        {i: kept[name] for i, name in enumerate(KEPT)},
        [shapes[name] for name in names],
        [shapes[name] for name in BOTH_HELD],
        48,
    )
    made = dict(zip(names, made))
    kept = {**kept, **{name: made[name] for name in KEPT}}
    return kept, made[Y], made[STATS], {name: made[name] for name in GRADS}, made[DX]


N_TILES = 4


def gradient_shapes(*sizes):
    count = lax.axis_size(ROWS)
    if count != 16:
        shapes = [(size, BF16) for size in sizes]
        return shapes, shapes
    tall = sum(rows * columns for rows, columns in sizes) // (count * min(map(min, sizes)))
    width = min(map(min, sizes))
    return [((8, 2, tall, width), BF16)], [((8, tall, width), BF16)] * 2


class GradientOut:
    def __init__(self, ref, targets, sems, first_sem, tile, by_rows, base=0):
        self.ref, self.targets, self.sems, self.first_sem = ref, targets, sems, first_sem
        self.tile, self.by_rows, self.base = tile, by_rows, base
        self.plain = len(targets) == 1
        self.tall = tile // 4 if by_rows else tile // 16

    def at(self, i):
        start = i * self.tile
        if self.plain and self.by_rows:
            return (pl.ds(pl.multiple_of(start, 16), self.tile),)
        if self.plain:
            return (slice(None), lanes_at(start, self.tile))
        if self.by_rows:
            return (pl.ds(2 * i, 2), pl.ds(self.base, self.tall))
        return (slice(None), pl.ds(pl.multiple_of(self.base + i * self.tall, 16), self.tall))

    def moves(self, i):
        at = self.at(i)
        if self.plain:
            pairs = [(self.ref.at[at], self.targets[0].at[at])]
        else:
            core = lax.axis_index(ROWS) % 2
            pairs = [
                (self.ref.at[at[0], which, at[1]], target.at[at])
                for target, which in zip(self.targets, (core, 1 - core))
            ]
        base = self.first_sem + i * len(pairs)
        return [
            pltpu.make_async_copy(source, target, self.sems.at[base + k])
            for k, (source, target) in enumerate(pairs)
        ]

    def put(self, i, value):
        value = value.astype(BF16)
        at = self.at(i)
        if self.plain:
            self.ref[at] = value
        else:
            split = value.reshape(-1, 2, self.tall, value.shape[1])
            self.ref[at[0], :, at[1], :] = split
        for move in self.moves(i):
            move.start()

    def finish(self):
        for i in range(N_TILES):
            for move in self.moves(i):
                move.wait()


def loop_tiles(step):
    def body(i, carry):
        step(i)
        return carry

    lax.fori_loop(0, N_TILES, body, 0)


FEED_HELD = (G, N2, R2, WIDE, SUMS_A, ACT, DFFN, WD, GP, HID, DUP, FEED, REST)


def feed_kernel(n_in, n_old, n_out, *refs):
    ins, outs, refs = split_refs(n_in, n_old, n_out, refs)
    g_hbm, gain2, n2, r2, act_hbm, down_share, wd_hbm, gp_hbm, hid_hbm, up_share = ins
    dffn_out, dup_out, sums_out, wide_out = outs[:4]
    at = dict(zip(FEED_HELD, refs))
    totals, sems = refs[len(FEED_HELD) : -1], refs[-1]
    inner, width = at[WD].shape
    tile = inner // N_TILES
    if len(totals) == 1:
        ways = [(totals[0], outs[4:]), (totals[0], outs[4:])]
    else:
        ways = [(total, [target]) for total, target in zip(totals, outs[4:])]
    down_way = GradientOut(*ways[0], sems, 40, tile, True)
    up_way = GradientOut(*ways[1], sems, 50, tile, False, tile // 4)
    is_first = lax.axis_index(LAYER) == 0
    copies = Copies(at, sems)
    own = Copies(at, sems)
    own.used = 4
    for name, source in ((G, g_hbm), (N2, n2), (R2, r2)):
        own.load(name, source, now=False)
    targets = ((DFFN, dffn_out), (WIDE, wide_out), (SUMS_A, sums_out))
    stores = [own.store(at[name], target, now=False) for name, target in targets]
    other = Copies(at, sems)
    other.used = 12
    other.load(DFFN, dffn_out, now=False)
    other.load(DUP, dup_out, now=False)

    def fetch(i):
        part = lanes_at(i * tile, tile)
        pairs = (
            (up_share.at[:, part], at[REST].at[:, part]),
            (wd_hbm.at[0, part, :], at[WD].at[part, :]),
            (gp_hbm.at[:, part], at[GP].at[:, part]),
        )
        return [
            pltpu.make_async_copy(source, target, sems.at[16 + 3 * i + k])
            for k, (source, target) in enumerate(pairs)
        ]

    def fetch_start(i):
        fetch(i)[0].start()

        @pl.when(is_first)
        def _():
            for move in fetch(i)[1:]:
                move.start()

    def away(i):
        part = lanes_at(i * tile, tile)
        return pltpu.make_async_copy(at[DUP].at[:, part], dup_out.at[:, part], sems.at[32 + i])

    @pl.when(is_first)
    def _():
        own.go()
        at[SUMS_A][...] = jnp.zeros(at[SUMS_A].shape, F32)
        own.ready(G, N2, R2)

    copies.load(ACT, act_hbm)
    copies.load(FEED, down_share)

    @pl.when(is_first)
    def _():
        second_norm_back(at, gain2, at[DFFN], 0)
        for way in stores[:2]:
            way.start()

    @pl.when(jnp.logical_not(is_first))
    def _():
        other.go()
        other.ready(DFFN, DUP)

    copies.load(HID, hid_hbm)
    fetch_start(0)
    copies.ready(ACT, FEED)
    fetch_start(1)

    def down_step(i):
        part = lanes_at(i * tile, tile)
        made = mm(at[ACT][:, part], at[DFFN][...], TN)
        down_way.put(i, made + at[FEED][part, :].astype(F32))

    loop_tiles(down_step)
    fetch_start(2)
    fetch_start(3)
    copies.ready(HID)

    def up_step(i):
        part = lanes_at(i * tile, tile)

        @pl.when(is_first)
        def _():
            for move in fetch(i)[1:]:
                move.wait()
            at[DUP][:, part] = up_back(at, at[DFFN][...], part)
            away(i).start()

        fetch(i)[0].wait()
        made = mm(at[HID][...], at[DUP][:, part], TN)
        up_way.put(i, made + at[REST][:, part].astype(F32))

    loop_tiles(up_step)
    down_way.finish()
    up_way.finish()

    @pl.when(is_first)
    def _():
        stores[2].start()
        for i in range(N_TILES):
            away(i).wait()
        own.finish()


def middle_kernel(n_in, n_old, n_out, *refs):
    ins, outs, refs = split_refs(n_in, n_old, n_out, refs)
    dup_hbm, wide_in, wu_hbm, gain1, n1, r1, wo_hbm, ctx_hbm = ins
    at = dict(zip((DUP, WIDE, WU, N1, R1, WO, CTX, DBR, DCTX, DELTA, SUMS_B), refs))

    @pl.when(lax.axis_index(LAYER) == 0)
    def _():
        copies = Copies(at, refs[-1])
        parts = [pl.ds(i * at[DUP].shape[1] // 2, at[DUP].shape[1] // 2) for i in range(2)]

        def get_half(i):
            copies.load(DUP, dup_hbm.at[:, parts[i]], at[DUP].at[:, parts[i]])
            copies.load(WU, wu_hbm.at[0, :, parts[i]], at[WU].at[:, parts[i]])

        get_half(0)
        copies.load(WIDE, wide_in)
        at[SUMS_B][...] = jnp.zeros(at[SUMS_B].shape, F32)
        copies.ready(DUP, WU, WIDE)
        get_half(1)
        at[WIDE][...] += mm(at[DUP][:, parts[0]], at[WU][:, parts[0]], NT)
        copies.ready(DUP, WU)
        copies.load(N1, n1)
        copies.load(R1, r1)
        copies.load(WO, wo_hbm.at[0])
        copies.load(CTX, ctx_hbm)
        at[WIDE][...] += mm(at[DUP][:, parts[1]], at[WU][:, parts[1]], NT)
        copies.ready(N1, R1)
        first_norm_back(at, gain1, at[DBR], 0)
        for name, target in ((DBR, outs[0]), (WIDE, outs[1]), (SUMS_B, outs[4])):
            copies.store(at[name], target)
        copies.ready(WO, CTX)
        context_back(at, at[DBR][...], at[CTX][...])
        copies.store(at[DCTX], outs[2])
        copies.store(at[DELTA], outs[3])
        copies.finish()


ATTEND_READ = (QKV, DCTX, KID, QID, LSE, DELTA)
ATTEND_HELD = ATTEND_READ + (X, CTX, DBR, REST, WIDE, WQKV, DQKV, SUMS_C, DX)


def attend_kernel(n_in, n_old, n_out, *refs):
    ins, outs, refs = split_refs(n_in, n_old, n_out, refs)
    x_hbm, ctx_hbm, dbr_hbm, share, wide_hbm, wq, wk, wv = ins[len(ATTEND_READ) :]
    dqkv_out, sums_out, dx_out = outs[:3]
    at = dict(zip(ATTEND_HELD, refs))
    total, sems = refs[-2:]
    width = at[X].shape[1]
    is_first = lax.axis_index(LAYER) == 0
    copies = Copies(at, sems)
    own = Copies(at, sems)
    own.used = 6
    for name, source in zip(ATTEND_READ, ins):
        own.load(name, source, now=False)
    targets = ((DQKV, dqkv_out), (SUMS_C, sums_out), (DX, dx_out))
    stores = [own.store(at[name], target, now=False) for name, target in targets]
    late = Copies(at, sems)
    late.used = 16
    late.load(WIDE, wide_hbm, now=False)
    for i, weight in enumerate((wq, wk, wv)):
        late.load(WQKV, weight.at[0], at[WQKV].at[:, pl.ds(i * width, width)], now=False)
    other = Copies(at, sems)
    other.used = 22
    other.load(DQKV, dqkv_out, now=False)

    @pl.when(is_first)
    def _():
        own.go()
        own.ready(*ATTEND_READ)

    for name, source in ((X, x_hbm), (CTX, ctx_hbm), (DBR, dbr_hbm), (REST, share)):
        copies.load(name, source)

    @pl.when(is_first)
    def _():
        late.go()
        over_pairs(width, lambda j: attend_pair_back(j, width, at, at[DQKV], 0))
        for way in stores[:2]:
            way.start()

    @pl.when(jnp.logical_not(is_first))
    def _():
        other.go()
        other.ready(DQKV)

    copies.ready(X, CTX, DBR, REST)
    way_out = GradientOut(total, outs[3:], sems, 24, width, False)
    way_out.put(0, mm(at[CTX][...], at[DBR][...], TN) + at[REST][:, 0:width].astype(F32))

    def step(i, carry):
        made = mm(at[X][...], at[DQKV][:, lanes_at((i - 1) * width, width)], TN)
        way_out.put(i, made + at[REST][:, lanes_at(i * width, width)].astype(F32))
        return carry

    lax.fori_loop(1, N_TILES, step, 0)

    @pl.when(is_first)
    def _():
        late.ready(WIDE, WQKV)
        at[DX][...] = (at[WIDE][...] + mm(at[DQKV][...], at[WQKV][...], NT)).astype(BF16)
        stores[2].start()
        own.finish()

    way_out.finish()


def swap(array, stride):
    count = lax.axis_size(ROWS)
    return lax.ppermute(array, ROWS, [(d, d ^ stride) for d in range(count)])


def halves_kernel(jobs, n_in, n_old, n_out, *refs):
    ins, outs, refs = split_refs(n_in, n_old, n_out, refs)
    copies = Copies({}, refs[-1])
    buffers = [refs[3 * i : 3 * i + 3] for i in range(len(jobs))]
    for i, job in enumerate(jobs):
        sources, stride, before, after, start, size, keep = job[:7]
        own = (lax.axis_index(ROWS) // stride) % 2
        which = own if keep else 1 - own
        for k in range(before):
            taken = pl.ds((2 * k + which) * after, after)
            for source, buffer in zip(sources, buffers[i]):
                target = buffer.at[pl.ds(k * after, after)]
                copies.load(i, ins[source].at[taken, :, pl.ds(start, size)], target)
    for i, job in enumerate(jobs):
        left, right, total = buffers[i]
        copies.ready(i)
        total[...] = (left[...].astype(F32) + right[...].astype(F32)).astype(BF16)
        place, start = job[7:]
        copies.store(total, outs[place].at[:, :, pl.ds(start, total.shape[-1])])
    copies.finish()


def halves(ways, arrays, n_outs):
    tall = arrays[0].shape[1]
    jobs, scratch = [], []
    outs = [None] * (2 * n_outs)
    for keep in (0, 1):
        for sources, stride, before, after, start, size, place, column in ways:
            jobs.append((sources, stride, before, after, start, size, keep, place + keep * n_outs, column))
            scratch += [((before * after, tall, size), BF16)] * 3
            outs[place + keep * n_outs] = ((before * after, tall, column + size), BF16)
    inputs = [(array, ANY) for array in arrays]
    made = call(partial(halves_kernel, tuple(jobs)), "halves", inputs, {}, outs, scratch, 48)
    return made[:n_outs], made[n_outs:]


class ScatterSum:
    def __init__(self, kept, came):
        self.kept, self.came = kept, came

    @staticmethod
    def cores(blocks):
        return ScatterSum(blocks[0], swap(blocks[1], 1))

    def second(self, first):
        kept = lax.optimization_barrier((self.kept, first))[0]
        half = kept.shape[-1] // 2
        ways = (((0, 1), 2, 4, 1, 0, half, 0, 0), ((0, 1), 4, 2, 2, half, half, 1, 0))
        sent, kept = halves(ways, (kept, self.came), 2)
        return ScatterSum(tuple(kept), (swap(sent[0], 2), swap(sent[1], 4)))

    def third(self, first):
        kept = lax.optimization_barrier((self.kept, first))[0]
        half = kept[0].shape[-1]
        ways = (((0, 1), 4, 2, 1, 0, half, 0, 0), ((2, 3), 2, 2, 1, 0, half, 1, 0))
        sent, kept = halves(ways, (kept[0], self.came[0], kept[1], self.came[1]), 2)
        return ScatterSum(tuple(kept), (swap(sent[0], 4), swap(sent[1], 2)))

    def fourth(self, first):
        kept = lax.optimization_barrier((self.kept, first))[0]
        half = kept[0].shape[-1]
        ways = tuple(((2 * i, 2 * i + 1), 8, 1, 1, 0, half, 0, i * half) for i in range(2))
        sent, kept = halves(ways, (kept[0], self.came[0], kept[1], self.came[1]), 1)
        return ScatterSum(kept[0], swap(sent[0], 8))

    def finish(self):
        return (self.kept.astype(F32) + self.came.astype(F32))[0]


def whole_sum(partial_sum):
    return lax.psum_scatter(partial_sum, ROWS, scatter_dimension=0, tiled=True).astype(F32)


def small_sum(values, beside, after):
    if lax.axis_size(ROWS) != 16:
        return lax.psum(values, ROWS)
    for stride, first in zip((1, 2, 4, 8), (*beside, None)):
        values = values + swap(values, stride)
        if first is not None:
            values = after(values, first)
    return values


def on_device(tokens, cotangent, segment_ids, valid_mask, cluster_perm, *params):
    section = lax.axis_index(LAYER)
    is_first = section == 0
    wq, _, wk, wv, _, wo, _, gain1, _, wu, _, wd, _, gain2, _ = params
    width, inner = wu.shape[1:]
    ids = (cluster_perm, segment_ids, valid_mask)
    shapes = shapes_of(width, inner)

    def hop(array, source, target):
        return lax.ppermute(array, LAYER, [(source, target)])

    def after(array, first):
        return lax.optimization_barrier((array, first))[0]

    row0, y0, stats00 = forward(0, 0, tokens, 0, ids, params, None)
    in0 = hop(y0, 0, 1)
    row1, y1, stats01 = forward(0, 1, tokens, 1, ids, params, None)
    in1 = hop(y1, 0, 1)
    row0, out0, stats10, grads0, dx0 = through_and_back(0, in0, cotangent, ids, params, row0)
    in1 = after(in1, dx0)
    g0 = hop(dx0, 1, 0)
    row1, out1, stats11, grads1, dx1 = through_and_back(1, in1, cotangent, ids, params, row1)
    g0 = after(g0, dx1)
    g1 = hop(dx1, 1, 0)
    grads0, (dx0, down_share, up_share, rest_share) = backward(0, g0, 0, params, row0, grads0)
    g1 = after(g1, dx0)

    def at_hbm(*arrays):
        return [(array, ANY) for array in arrays]

    def of(*names):
        return [shapes[name] for name in names]

    totals, parts = gradient_shapes((inner, width), (width, inner))
    plain = len(totals) == 2
    made = call(
        feed_kernel,
        "feed",
        at_hbm(g1)
        + [(gain2, WHOLE)]
        + at_hbm(row1[N2], row1[R2], row1[ACT], down_share, wd, row1[GP], row1[HID], up_share),
        {0: grads1[DFFN], 1: grads1[DUP], 2: grads1[SUMS_A]},
        of(DFFN, DUP, SUMS_A, WIDE) + parts,
        of(G, N2, R2, WIDE, SUMS_A, ACT, DFFN, WD, GP, HID, DUP, WD, WU) + totals,
        60,
    )
    _, dup1, sums_a1, wide = made[:4]
    feed_parts = made[4:]
    if not plain:
        feed_sum = ScatterSum.cores(feed_parts)

    made = call(
        middle_kernel,
        "middle",
        at_hbm(dup1, wide, wu) + [(gain1, WHOLE)] + at_hbm(row1[N1], row1[R1], wo, row1[CTX]),
        {0: grads1[DBR], 4: grads1[SUMS_B]},
        of(DBR, WIDE, DCTX, DELTA, SUMS_B),
        of(DUP, WIDE, WU, N1, R1, WO, CTX, DBR, DCTX, DELTA, SUMS_B),
        20,
    )
    dbr1, wide, dctx, delta, sums_b1 = made
    if not plain:
        feed_sum = feed_sum.second(dctx)
        dctx = after(dctx, feed_sum.kept)

    totals, parts = gradient_shapes((width, 4 * width))
    made = call(
        attend_kernel,
        "attend",
        at_hbm(row1[QKV], dctx, *(row1[name] for name in (KID, QID, LSE)), delta)
        + at_hbm(row1[X], row1[CTX], dbr1, rest_share, wide, wq, wk, wv),
        {0: grads1[DQKV], 1: grads1[SUMS_C]},
        of(DQKV, SUMS_C, DX) + parts,
        of(*ATTEND_HELD) + totals,
        40,
    )
    _, sums_c1, dx1 = made[:3]
    came = []
    if plain:
        w_down, w_up, w_rest = (whole_sum(part) for part in (*feed_parts, made[3]))
        w_out, w_query, w_key, w_value = jnp.split(w_rest, 4, axis=1)
    else:
        feed_sum = feed_sum.third(dx1)
        rest_sum = ScatterSum.cores(after(tuple(made[3:]), feed_sum.kept))
        came.append(rest_sum.came)
        rest_sum = rest_sum.second(feed_sum.kept)
        dx1 = after(dx1, rest_sum.kept)
        came.append(rest_sum.came)
        feed_sum = feed_sum.fourth(rest_sum.kept)
        rest_sum = rest_sum.third(feed_sum.kept)
        came.append(rest_sum.came)
        rest_sum = rest_sum.fourth(rest_sum.kept)
        w_feed, w_rest = feed_sum.finish(), rest_sum.finish()
        tall = inner // 16
        w_down = w_feed[:tall]
        w_up = jnp.concatenate(jnp.split(w_feed[tall:], N_TILES, axis=0), axis=1)
        w_out, w_query, w_key, w_value = jnp.split(w_rest, 4, axis=0)

    sums_a1, sums_b1, sums_c1 = (after(array, dx1) for array in (sums_a1, sums_b1, sums_c1))
    stats10 = after(stats10, dx1)
    sum_a = (grads0[SUMS_A] + sums_a1).reshape(4, 8, inner).sum(axis=1)
    sum_b = (grads0[SUMS_B] + sums_b1).reshape(3, 8, width).sum(axis=1)
    sum_c = (grads0[SUMS_C] + sums_c1).reshape(2, 8, width).sum(axis=1)
    stats = jnp.where(is_first, stats00 + stats01, stats10 + stats11)
    stats = stats.reshape(3, 8 * width).sum(axis=1)
    count = jnp.sum(valid_mask.astype(F32))
    pieces = [sum_a[:3, :width].reshape(-1), sum_b.reshape(-1), sum_c.reshape(-1), sum_a[3]]
    base = 8 * width + inner
    spare = -(base + 4) % (8 * LANES)
    tail = jnp.concatenate([stats, jnp.broadcast_to(count, (1,)), jnp.zeros((spare,), F32)])
    small = jnp.concatenate(pieces + [tail]).reshape(-1, LANES)
    small = small_sum(small, came, after).reshape(-1)
    shares = lax.axis_size(ROWS)
    me = lax.axis_index(ROWS)

    def small_part(place, size):
        own = size // shares
        return lax.dynamic_slice_in_dim(small, place * width + me * own, own, 0)[None]

    gain2_sum, shift2_sum, down_bias, gain1_sum, shift1_sum, out_bias, query_bias, value_bias = (
        small_part(i, width) for i in range(8)
    )
    up_bias = small_part(8, inner)
    root_means = jnp.sqrt(small[base : base + 3] / (small[base + 3] * width))[None, :]

    half = width // 2
    dx0, out0, out1 = (after(array, dx1) for array in (dx0, out0, out1))
    outgoing = jnp.concatenate(
        [
            jnp.where(is_first, grad[:, half:], made[:, :half])
            for grad, made in ((dx0, out0), (dx1, out1))
        ]
    )
    arrived = lax.ppermute(outgoing, LAYER, [(0, 1), (1, 0)])
    block_own = jnp.concatenate([out0[:, half:], out1[:, half:]])
    grad_own = jnp.concatenate([dx0[:, :half], dx1[:, :half]])
    block_part = jnp.where(is_first, arrived, block_own)
    grad_part = jnp.where(is_first, grad_own, arrived)
    return (
        block_part,
        grad_part,
        w_query[None],
        query_bias,
        w_key[None],
        w_value[None],
        value_bias,
        w_out[None],
        out_bias,
        gain1_sum,
        shift1_sum,
        w_up[None],
        up_bias,
        w_down[None],
        down_bias,
        gain2_sum,
        shift2_sum,
        root_means,
    )


def solution(mesh):
    by_layer = P(LAYER, None)
    matrix = P(LAYER, None, None)
    share = P(LAYER, ROWS)
    matrix_share = P(LAYER, ROWS, None)
    rows = P(ROWS, None)
    vectors = {1, 4, 6, 7, 8, 10, 12, 13, 14}
    matrices = {2, 4, 5, 7, 11, 13}
    return jax.shard_map(
        on_device,
        mesh=mesh,
        in_specs=(rows, rows, rows, rows, P(LAYER, ROWS, None, None))
        + tuple(by_layer if i in vectors else matrix for i in range(15)),
        out_specs=(P(ROWS, LAYER), P(ROWS, LAYER))
        + tuple(matrix_share if i in matrices else share for i in range(2, 17))
        + (P(LAYER, None),),
        check_vma=False,
    )
```

```python
from functools import partial

import jax
import jax.numpy as jnp
from jax import lax
from jax.experimental import pallas as pl
from jax.experimental.pallas import tpu as pltpu
from jax.sharding import PartitionSpec as P

HEAD_DIM = 64
CLUSTER = 128
SEQ = 512
LANES = 128
ROW_BLOCK = 512
PAIR_UNROLL = 3
MIB = 1024 * 1024

BF16 = jnp.bfloat16
F32 = jnp.float32
LOG2E = 1.4426950408889634
SCALE = HEAD_DIM**-0.5
SCORE_SCALE = SCALE * LOG2E

NN = ((1,), (0,))
NT = ((1,), (1,))
TN = ((0,), (0,))

ROWS = "dp"
LAYER = "section"
ANY = pl.BlockSpec(memory_space=pltpu.HBM)
WHOLE = pl.BlockSpec(memory_space=pltpu.VMEM)
SHORT = pl.CostEstimate(flops=1, bytes_accessed=1, transcendentals=0)

X, QKV, CTX, LSE, KID, QID, N1, R1, HID, ACT, GP, N2, R2 = range(13)
G, DFFN, DUP, DBR, DQKV, SUMS_A, SUMS_B, SUMS_C, WIDE, DCTX, DELTA, DX, FEED, LIVE = range(13, 27)
BIAS, WQKV, Y, STATS, WO, WU, WD, REST = range(27, 35)
SAVED = (X, QKV, CTX, LSE, KID, QID, N1, R1, HID, ACT, GP, N2, R2)
GRADS = (DFFN, DUP, DBR, DQKV, SUMS_A, SUMS_B, SUMS_C)
GAIN2, SHIFT2, B_DOWN, B_UP = 0, 8, 16, 24
GAIN1, SHIFT1, B_OUT = 0, 8, 16
B_QUERY, B_VALUE = 0, 8


def shapes_of(width, inner):
    token, token32, narrow = ((SEQ, width), BF16), ((SEQ, width), F32), ((SEQ, LANES), F32)
    heads = ((16, SEQ), F32)
    shapes = {name: token for name in (X, CTX, N1, HID, N2, G, DFFN, DBR, DCTX, DX, Y)}
    shapes.update({name: token32 for name in (KID, WIDE, FEED)})
    shapes.update({name: narrow for name in (R1, R2, LIVE)})
    shapes.update({name: heads for name in (LSE, QID, DELTA)})
    shapes.update({name: ((SEQ, inner), BF16) for name in (ACT, GP, DUP)})
    shapes.update({name: ((SEQ, 3 * width), BF16) for name in (QKV, DQKV)})
    shapes.update({SUMS_A: ((32, inner), F32), SUMS_B: ((24, width), F32)})
    shapes.update({SUMS_C: ((16, width), F32), STATS: ((24, width), F32), BIAS: ((8, width), F32)})
    shapes.update({WQKV: ((width, 3 * width), BF16), WO: ((width, width), BF16)})
    shapes.update({WU: ((width, inner), BF16), WD: ((inner, width), BF16)})
    shapes[REST] = ((width, 4 * width), BF16)
    return shapes


def mm(left, right, dims):
    return lax.dot_general(left, right, (dims, ((), ())), preferred_element_type=F32)


def vec(ref):
    return ref[0:1, :].astype(F32)


def lanes_at(start, size=LANES):
    return pl.ds(pl.multiple_of(start, LANES), size)


def fold8(block):
    return jnp.sum(block.reshape(-1, 8, block.shape[-1]), axis=0)


def over_rows(step):
    def body(i, carry):
        step(pl.ds(pl.multiple_of(i * ROW_BLOCK, ROW_BLOCK), ROW_BLOCK))
        return carry

    lax.fori_loop(0, SEQ // ROW_BLOCK, body, 0)


def over_tiles(size, tile, step):
    def body(i, carry):
        step(pl.ds(pl.multiple_of(i * tile, tile), tile))
        return carry

    lax.fori_loop(0, size // tile, body, 0)


class Copies:
    def __init__(self, at, sems):
        self.at, self.sems = at, sems
        self.used = 0
        self.loads = {}
        self.stores = []

    def plan(self, source, target):
        self.used += 1
        return pltpu.make_async_copy(source, target, self.sems.at[self.used - 1])

    def load(self, name, source, target=None, now=True):
        target = self.at[name] if target is None else target
        copy = self.plan(source, target)
        self.loads.setdefault(name, []).append(copy)
        if now:
            copy.start()

    def go(self):
        for copies in self.loads.values():
            for copy in copies:
                copy.start()

    def ready(self, *names):
        for name in names:
            for copy in self.loads.pop(name, ()):
                copy.wait()

    def store(self, source, target, now=True):
        copy = self.plan(source, target)
        self.stores.append(copy)
        if now:
            copy.start()
        return copy

    def finish(self):
        for copy in self.stores:
            copy.wait()


def load_qkv(copies, weights, width):
    for i, weight in enumerate(weights):
        copies.load(WQKV, weight.at[0], copies.at[WQKV].at[:, pl.ds(i * width, width)])


def call(body, name, inputs, old, outs, scratch, n_sems):
    arrays = [array for array, _ in inputs]
    n_in = len(arrays)
    return pl.pallas_call(
        partial(body, n_in, len(old), len(outs)),
        out_shape=[jax.ShapeDtypeStruct(*shape) for shape in outs],
        in_specs=[spec for _, spec in inputs] + [ANY] * len(old),
        out_specs=[ANY] * len(outs),
        input_output_aliases={n_in + i: place for i, place in enumerate(old)},
        scratch_shapes=[pltpu.VMEM(*shape) for shape in scratch]
        + [pltpu.SemaphoreType.DMA((n_sems,))],
        compiler_params=pltpu.CompilerParams(vmem_limit_bytes=58 * MIB),
        cost_estimate=SHORT,
        name=name,
    )(*arrays, *old.values())


def split_refs(n_in, n_old, n_out, refs):
    return refs[:n_in], refs[n_in + n_old : n_in + n_old + n_out], refs[n_in + n_old + n_out :]


def low_lanes():
    return lax.broadcasted_iota(jnp.int32, (SEQ, LANES), 1) < HEAD_DIM


def masked(scores, kid_column, qid_row):
    shape = (CLUSTER, CLUSTER)
    same = lax.broadcasted_iota(jnp.int32, shape, 0) == lax.broadcasted_iota(jnp.int32, shape, 1)
    count = SEQ // CLUSTER
    parts = [slice(i * CLUSTER, (i + 1) * CLUSTER) for i in range(count)]
    rows = []
    for i in range(count):
        tiles = []
        for j in range(count):
            ok = kid_column[parts[i]] == qid_row[:, parts[j]]
            if i == j:
                ok = ok | same
            tiles.append(jnp.where(ok, scores[parts[i], parts[j]], -1e30))
        rows.append(jnp.concatenate(tiles, axis=1))
    return jnp.concatenate(rows, axis=0)


def attend_pair(j, width, at):
    low = low_lanes()
    lanes = lanes_at(j * LANES)
    query = at[QKV][:, lanes]
    key = at[QKV][:, lanes_at(width + j * LANES)]
    value = at[QKV][:, lanes_at(2 * width + j * LANES)]
    kid_pair = at[KID][:, lanes]
    mixed, tops = [], []
    for half in (0, 1):
        own = low if half == 0 else ~low
        own_query = jnp.where(own, query, jnp.zeros_like(query))
        value_ones = jnp.where(own, value, jnp.ones_like(value))
        kid_column = kid_pair[:, half * HEAD_DIM : half * HEAD_DIM + 1]
        scores = mm(key, own_query, NT) * SCORE_SCALE
        scores = masked(scores, kid_column, at[QID][pl.ds(2 * j + half, 1), :])
        top = jnp.max(scores, axis=0, keepdims=True)
        tops.append(top)
        mixed.append(mm(jnp.exp2(scores - top).astype(BF16), value_ones, TN))
    sums = [pltpu.roll(part, HEAD_DIM, 1) for part in mixed]
    total = jnp.where(low, sums[0], sums[1])
    at[CTX][:, lanes] = (jnp.where(low, mixed[0], mixed[1]) / total).astype(BF16)
    turned = total.T
    for half in (0, 1):
        row = turned[half * HEAD_DIM : half * HEAD_DIM + 1, :]
        at[LSE][pl.ds(2 * j + half, 1), :] = tops[half] + jnp.log2(row)


def attend_pair_back(j, width, at, target, base):
    low = low_lanes()
    lanes = [lanes_at(i * width + j * LANES) for i in range(3)]
    query, key, value = (at[QKV][:, part] for part in lanes)
    d_out = at[DCTX][:, lanes[0]]
    kid_pair = at[KID][:, lanes[0]]
    d_query, d_key, d_value = [], [], []
    for half in (0, 1):
        h = pl.ds(2 * j + half, 1)
        own = low if half == 0 else ~low
        own_query = jnp.where(own, query, jnp.zeros_like(query))
        own_out = jnp.where(own, d_out, jnp.zeros_like(d_out))
        kid_column = kid_pair[:, half * HEAD_DIM : half * HEAD_DIM + 1]
        scores = mm(key, own_query, NT) * SCORE_SCALE - at[LSE][h, :]
        weights = jnp.exp2(masked(scores, kid_column, at[QID][h, :]))
        d_weights = mm(value, own_out, NT)
        d_scores = (weights * (d_weights - at[DELTA][h, :])).astype(BF16)
        d_value.append(mm(weights.astype(BF16), own_out, NN))
        d_key.append(mm(d_scores, own_query, NN))
        d_query.append(mm(d_scores, key, TN))
    made = (
        jnp.where(low, d_query[0], d_query[1]) * SCALE,
        (d_key[0] + d_key[1]) * SCALE,
        d_value[0] + d_value[1],
    )
    rows = pl.ds(base, SEQ)
    for i, place in ((0, B_QUERY), (1, None), (2, B_VALUE)):
        rounded = made[i].astype(BF16)
        target[rows, lanes[i]] = rounded
        if place is not None:
            at[SUMS_C][place : place + 8, lanes[0]] = fold8(rounded.astype(F32))


def over_pairs(width, step):
    def body(j, carry):
        step(j)
        return carry

    lax.fori_loop(0, width // LANES, body, 0, unroll=PAIR_UNROLL)


def token_ids(row, heads, perm_ref, seg_ref, valid_ref, kid_ref, qid_ref):
    token = lax.broadcasted_iota(jnp.int32, (SEQ, LANES), 0)
    lane = lax.broadcasted_iota(jnp.int32, (SEQ, LANES), 1)
    seg_row = seg_ref[row : row + 1, :].astype(F32)
    valid_row = valid_ref[row : row + 1, :].astype(F32)
    at = lax.broadcasted_iota(jnp.int32, (LANES, SEQ), 0)
    both = jnp.where(at == 0, seg_row, jnp.where(at == 1, valid_row, 0.0)).T
    segment, live = both[:, 0:1], both[:, 1:2]

    def column(h):
        places = perm_ref[0, row, pl.ds(h, 1), :]
        mine = jnp.zeros((SEQ, LANES), F32)
        for c in range(1, SEQ // CLUSTER):
            part = places[:, c * CLUSTER : (c + 1) * CLUSTER]
            mine = jnp.where(token == part, float(c), mine)
        return jnp.sum(mine, axis=1, keepdims=True) * 4.0 + segment

    def pair(j, ids):
        left, right = column(2 * j), column(2 * j + 1)
        own = jnp.where(lane < HEAD_DIM, left, right)
        kid_ref[:, lanes_at(j * LANES)] = jnp.where(live > 0.5, own, -1.0)
        ids = jnp.where(lane == 2 * j, left, ids)
        return jnp.where(lane == 2 * j + 1, right, ids)

    qid = lax.fori_loop(0, heads // 2, pair, jnp.zeros((SEQ, LANES), F32))
    qid_ref[...] = qid.T[0:16, :]
    return live


def normed(total):
    centre = total - jnp.mean(total, axis=-1, keepdims=True)
    spread = jnp.mean(centre * centre, axis=-1, keepdims=True)
    rate = lax.rsqrt(spread + 1e-05)
    return centre * rate, rate


FORWARD_HELD = SAVED + (WQKV, WO, WU, WD, WIDE, FEED, Y, STATS, LIVE, BIAS)


def run_forward(at, copies, save, row, source, ids, params, later=None):
    perm_ref, seg_ref, valid_ref = ids
    wq, bq, wk, wv, bv, wo, bo, g1, s1, wu, bu, wd, bd, g2, s2 = params
    width, inner = at[WU].shape
    heads = width // HEAD_DIM
    copies.load(X, source)
    first = copies.used
    load_qkv(copies, (wq, wk, wv), width)
    live = token_ids(row, heads, perm_ref, seg_ref, valid_ref, at[KID], at[QID])
    at[LIVE][...] = jnp.broadcast_to(live, (SEQ, LANES))
    at[LSE][...] = jnp.zeros((16, SEQ), F32)
    at[STATS][...] = jnp.zeros((24, width), F32)
    at[BIAS][0:1, :] = vec(bq)
    at[BIAS][1:2, :] = jnp.zeros((1, width), F32)
    at[BIAS][2:3, :] = vec(bv)
    copies.ready(X)

    def to_qkv(i, carry):
        part = pl.ds(pl.multiple_of(i * width, LANES), width)
        weight = at[WQKV].at[:, part]
        pltpu.make_async_copy(weight, weight, copies.sems.at[first + i]).wait()
        made = mm(at[X][...], at[WQKV][:, part], NN) + at[BIAS][pl.ds(i, 1), :]
        at[QKV][:, part] = made.astype(BF16)
        return carry

    lax.fori_loop(0, 3, to_qkv, 0)
    copies.loads.pop(WQKV)
    copies.load(WO, wo.at[0])
    copies.load(WU, wu.at[0])
    copies.load(WD, wd.at[0])
    if later is not None:
        later()
    save(KID, QID, X, QKV)
    over_pairs(width, lambda j: attend_pair(j, width, at))
    save(LSE, CTX)
    copies.ready(WO)
    at[WIDE][...] = mm(at[CTX][...], at[WO][...], NN)

    def first_norm(rows):
        branch = at[WIDE][rows, :] + vec(bo)
        alive = at[LIVE][rows, 0:1]
        at[STATS][0:8, :] += fold8(branch * branch * alive)
        unit, rate = normed(at[X][rows, :].astype(F32) + branch)
        hidden = unit * vec(g1) + vec(s1)
        at[N1][rows, :] = unit.astype(BF16)
        at[R1][rows, :] = jnp.broadcast_to(rate, (ROW_BLOCK, LANES))
        at[HID][rows, :] = hidden.astype(BF16)
        at[WIDE][rows, :] = hidden

    over_rows(first_norm)
    save(N1, R1, HID)
    copies.ready(WU)

    def up(part):
        upper = mm(at[HID][...], at[WU][:, part], NN) + bu[0:1, part].astype(F32)
        half = 0.5 + 0.5 * lax.erf(upper * 0.5**0.5)
        bell = jnp.exp2(upper * upper * (-0.5 * LOG2E)) * 0.3989422804014327
        at[ACT][:, part] = (upper * half).astype(BF16)
        at[GP][:, part] = (half + upper * bell).astype(BF16)

    over_tiles(inner, inner // 2, up)
    save(ACT, GP)
    copies.ready(WD)
    at[FEED][...] = mm(at[ACT][...], at[WD][...], NN)

    def second_norm(rows):
        ffn = at[FEED][rows, :] + vec(bd)
        alive = at[LIVE][rows, 0:1]
        at[STATS][8:16, :] += fold8(ffn * ffn * alive)
        unit, rate = normed(at[WIDE][rows, :] + ffn)
        result = unit * vec(g2) + vec(s2)
        at[STATS][16:24, :] += fold8(result * result * alive)
        at[N2][rows, :] = unit.astype(BF16)
        at[R2][rows, :] = jnp.broadcast_to(rate, (ROW_BLOCK, LANES))
        at[Y][rows, :] = result.astype(BF16)

    over_rows(second_norm)
    save(Y, STATS, N2, R2)


def forward_kernel(section, row, x_row, n_in, n_old, n_out, *refs):
    ins, outs, refs = split_refs(n_in, n_old, n_out, refs)
    out = dict(zip(SAVED + (Y, STATS), outs))
    at = dict(zip(FORWARD_HELD, refs))

    @pl.when(lax.axis_index(LAYER) == section)
    def _():
        copies = Copies(at, refs[-1])

        def save(*names):
            for name in names:
                copies.store(at[name], out[name])

        source = ins[0].at[pl.ds(x_row * SEQ, SEQ), :]
        run_forward(at, copies, save, row, source, ins[1:4], ins[4:])
        copies.finish()


def forward(section, row, x, x_row, ids, params, kept):
    width, inner = params[9].shape[1:]
    shapes = shapes_of(width, inner)
    inputs = [(x, ANY)] + [(array, WHOLE) for array in ids]
    inputs += [(array, ANY if array.ndim == 3 else WHOLE) for array in params]
    made = call(
        partial(forward_kernel, section, row, x_row),
        "forward",
        inputs,
        {} if kept is None else {i: kept[name] for i, name in enumerate(SAVED)},
        [shapes[name] for name in SAVED + (Y, STATS)],
        [shapes[name] for name in FORWARD_HELD],
        32,
    )
    return dict(zip(SAVED, made)), made[-2], made[-1]


def norm_back(grad, unit, rate, gain):
    scaled = grad * gain
    mean = jnp.mean(scaled, axis=-1, keepdims=True)
    along = jnp.mean(scaled * unit, axis=-1, keepdims=True)
    return (scaled - mean - unit * along) * rate


def add_sum(ref, place, value):
    ref[place : place + 8, 0 : value.shape[-1]] += fold8(value)


def second_norm_back(at, gain2, target, base):
    def step(rows):
        grad = at[G][rows, :].astype(F32)
        unit = at[N2][rows, :].astype(F32)
        add_sum(at[SUMS_A], GAIN2, grad * unit)
        add_sum(at[SUMS_A], SHIFT2, grad)
        d_second = norm_back(grad, unit, at[R2][rows, 0:1], vec(gain2))
        at[WIDE][rows, :] = d_second
        low = d_second.astype(BF16)
        target[pl.ds(pl.multiple_of(rows.start + base, ROW_BLOCK), ROW_BLOCK), :] = low
        add_sum(at[SUMS_A], B_DOWN, low.astype(F32))

    over_rows(step)


def up_back(at, dffn, part):
    d_act = mm(dffn, at[WD][part, :], NT)
    low = (d_act * at[GP][:, part].astype(F32)).astype(BF16)
    at[SUMS_A][B_UP : B_UP + 8, part] += fold8(low.astype(F32))
    return low


def first_norm_back(at, gain1, target, base):
    def step(rows):
        grad = at[WIDE][rows, :]
        unit = at[N1][rows, :].astype(F32)
        add_sum(at[SUMS_B], GAIN1, grad * unit)
        add_sum(at[SUMS_B], SHIFT1, grad)
        d_first = norm_back(grad, unit, at[R1][rows, 0:1], vec(gain1))
        at[WIDE][rows, :] = d_first
        low = d_first.astype(BF16)
        target[pl.ds(pl.multiple_of(rows.start + base, ROW_BLOCK), ROW_BLOCK), :] = low
        add_sum(at[SUMS_B], B_OUT, low.astype(F32))

    over_rows(step)


def context_back(at, dbr, context):
    width = dbr.shape[1]
    d_context = mm(dbr, at[WO][...], NT).astype(BF16)
    at[DCTX][...] = d_context
    product = d_context.astype(F32) * context.astype(F32)
    high = product.astype(BF16)
    rest = (product - high.astype(F32)).astype(BF16)
    of_head = (
        lax.broadcasted_iota(jnp.int32, (16, width), 1) // HEAD_DIM
        == lax.broadcasted_iota(jnp.int32, (16, width), 0)
    )
    pick = jnp.where(of_head, 1.0, 0.0).astype(BF16)
    at[DELTA][...] = mm(pick, high, NT) + mm(pick, rest, NT)


def run_backward(at, copies, get, save, params, shared):
    gain1, gain2 = params[:2]
    width, inner = at[WU].shape
    get(G, N2, R2)
    for name in (SUMS_A, SUMS_B):
        at[name][...] = jnp.zeros(at[name].shape, F32)
    copies.ready(G, N2, R2)
    get(WD, GP)
    second_norm_back(at, gain2, at[DFFN], 0)
    save(DFFN)
    get(WU, N1, R1, WO, CTX)
    copies.ready(WD, GP)

    def up(part):
        at[DUP][:, part] = up_back(at, at[DFFN][...], part)

    over_tiles(inner, inner // 2, up)
    save(DUP, SUMS_A)
    get(QKV, KID, QID, LSE, WQKV)
    copies.ready(WU)
    at[WIDE][...] += mm(at[DUP][...], at[WU][...], NT)
    copies.ready(N1, R1)
    first_norm_back(at, gain1, at[DBR], 0)
    save(DBR, SUMS_B)
    copies.ready(WO, CTX)
    context_back(at, at[DBR][...], at[CTX][...])
    copies.ready(QKV, KID, QID, LSE)
    if shared is not None:
        shared.go()
    over_pairs(width, lambda j: attend_pair_back(j, width, at, at[DQKV], 0))
    save(DQKV, SUMS_C)
    copies.ready(WQKV)
    at[DX][...] = (at[WIDE][...] + mm(at[DQKV][...], at[WQKV][...], NT)).astype(BF16)
    save(DX)


BACK_READ = (N2, R2, GP, N1, R1, CTX, LSE, KID, QID, QKV)
SHARE_READ = (ACT, HID, X)
BACK_HELD = (G,) + BACK_READ + GRADS + (WIDE, DCTX, DELTA, DX, WQKV, WO, WU, WD)


def backward_kernel(section, g_row, n_in, n_old, n_out, *refs):
    ins, outs, refs = split_refs(n_in, n_old, n_out, refs)
    g_hbm, gain1, gain2, wq, wk, wv, wo, wu, wd = ins[:9]
    given = dict(zip(BACK_READ + SHARE_READ, ins[9:]))
    given.update({WO: wo.at[0], WU: wu.at[0], WD: wd.at[0]})
    given[G] = g_hbm.at[pl.ds(g_row * SEQ, SEQ), :]
    with_shares = section == 0
    out = dict(zip(GRADS + (DX,), outs))
    at = dict(zip(BACK_HELD + (SHARE_READ if with_shares else ()), refs))
    width, inner = at[WU].shape
    shared = Copies(at, refs[-1])
    shared.used = 40
    if with_shares:
        for name in SHARE_READ:
            shared.load(name, given[name], now=False)

        @pl.when(lax.axis_index(LAYER) != section)
        def _():
            others = Copies(at, refs[-1])
            others.used = 50
            for name in (DFFN, DUP, DBR, DQKV):
                others.load(name, out[name])
            others.load(CTX, given[CTX])
            shared.go()
            others.ready(DFFN, DUP, DBR, DQKV, CTX)

    @pl.when(lax.axis_index(LAYER) == section)
    def _():
        copies = Copies(at, refs[-1])

        def get(*names):
            for name in names:
                if name == WQKV:
                    load_qkv(copies, (wq, wk, wv), width)
                else:
                    copies.load(name, given[name])

        def save(*names):
            for name in names:
                copies.store(at[name], out[name])

        run_backward(at, copies, get, save, ins[1:3], shared if with_shares else None)
        copies.finish()

    if not with_shares:
        return
    down, up, rest = at[WD], at[WU], refs[-2]
    shared.ready(*SHARE_READ)

    def to_down(part):
        down[part, :] = mm(at[ACT][:, part], at[DFFN][...], TN).astype(BF16)

    over_tiles(inner, width, to_down)
    shared.store(down, outs[-3])

    def to_up(part):
        up[:, part] = mm(at[HID][...], at[DUP][:, part], TN).astype(BF16)

    over_tiles(inner, width, to_up)
    shared.store(up, outs[-2])
    rest[:, 0:width] = mm(at[CTX][...], at[DBR][...], TN).astype(BF16)

    def to_rest(i, carry):
        made = mm(at[X][...], at[DQKV][:, lanes_at(i * width - width, width)], TN)
        rest[:, lanes_at(i * width, width)] = made.astype(BF16)
        return carry

    lax.fori_loop(1, 4, to_rest, 0)
    shared.store(rest, outs[-1])
    shared.finish()


def backward(section, g, g_row, params, kept, old):
    wq, _, wk, wv, _, wo, _, gain1, _, wu, _, wd, _, gain2, _ = params
    shapes = shapes_of(*wu.shape[1:])
    inputs = [(g, ANY), (gain1, WHOLE), (gain2, WHOLE)]
    inputs += [(array, ANY) for array in (wq, wk, wv, wo, wu, wd)]
    inputs += [(kept[name], ANY) for name in BACK_READ]
    outs, held = list(GRADS + (DX,)), list(BACK_HELD)
    if section == 0:
        inputs += [(kept[name], ANY) for name in SHARE_READ]
        outs += [WD, WU, REST]
        held += SHARE_READ + (REST,)
    made = call(
        partial(backward_kernel, section, g_row),
        "backward",
        inputs,
        {} if old is None else {i: old[name] for i, name in enumerate(GRADS)},
        [shapes[name] for name in outs],
        [shapes[name] for name in held],
        56,
    )
    return dict(zip(GRADS, made)), made[len(GRADS) :]


KEPT = (X, CTX, HID, ACT)
BOTH_HELD = FORWARD_HELD + (G,) + GRADS + (DCTX, DELTA, DX)


def both_kernel(row, n_in, n_old, n_out, *refs):
    ins, outs, refs = split_refs(n_in, n_old, n_out, refs)
    out = dict(zip(KEPT + (Y, STATS) + GRADS + (DX,), outs))
    at = dict(zip(BOTH_HELD, refs))
    params = ins[5:]

    @pl.when(lax.axis_index(LAYER) == 1)
    def _():
        copies = Copies(at, refs[-1])

        def save(*names):
            for name in names:
                if name in out:
                    copies.store(at[name], out[name])

        def get(*names):
            pass

        def later():
            copies.load(G, ins[1].at[pl.ds(row * SEQ, SEQ), :])

        run_forward(at, copies, save, row, ins[0], ins[2:5], params, later)
        run_backward(at, copies, get, save, (params[7], params[13]), None)
        copies.finish()


def through_and_back(row, x, g, ids, params, kept):
    shapes = shapes_of(*params[9].shape[1:])
    inputs = [(x, ANY), (g, ANY)] + [(array, WHOLE) for array in ids]
    inputs += [(array, ANY if array.ndim == 3 else WHOLE) for array in params]
    names = KEPT + (Y, STATS) + GRADS + (DX,)
    made = call(
        partial(both_kernel, row),
        "both",
        inputs,
        {i: kept[name] for i, name in enumerate(KEPT)},
        [shapes[name] for name in names],
        [shapes[name] for name in BOTH_HELD],
        48,
    )
    made = dict(zip(names, made))
    kept = {**kept, **{name: made[name] for name in KEPT}}
    return kept, made[Y], made[STATS], {name: made[name] for name in GRADS}, made[DX]


N_TILES = 4


def gradient_shapes(*sizes):
    count = lax.axis_size(ROWS)
    if count != 16:
        shapes = [(size, BF16) for size in sizes]
        return shapes, shapes
    tall = sum(rows * columns for rows, columns in sizes) // (count * min(map(min, sizes)))
    width = min(map(min, sizes))
    return [((8, 2, tall, width), BF16)], [((8, tall, width), BF16)] * 2


class GradientOut:
    def __init__(self, ref, targets, sems, first_sem, tile, by_rows, base=0):
        self.ref, self.targets, self.sems, self.first_sem = ref, targets, sems, first_sem
        self.tile, self.by_rows, self.base = tile, by_rows, base
        self.plain = len(targets) == 1
        self.tall = tile // 4 if by_rows else tile // 16

    def at(self, i):
        start = i * self.tile
        if self.plain and self.by_rows:
            return (pl.ds(pl.multiple_of(start, 16), self.tile),)
        if self.plain:
            return (slice(None), lanes_at(start, self.tile))
        if self.by_rows:
            return (pl.ds(2 * i, 2), pl.ds(self.base, self.tall))
        return (slice(None), pl.ds(pl.multiple_of(self.base + i * self.tall, 16), self.tall))

    def moves(self, i):
        at = self.at(i)
        if self.plain:
            pairs = [(self.ref.at[at], self.targets[0].at[at])]
        else:
            core = lax.axis_index(ROWS) % 2
            pairs = [
                (self.ref.at[at[0], which, at[1]], target.at[at])
                for target, which in zip(self.targets, (core, 1 - core))
            ]
        base = self.first_sem + i * len(pairs)
        return [
            pltpu.make_async_copy(source, target, self.sems.at[base + k])
            for k, (source, target) in enumerate(pairs)
        ]

    def put(self, i, value):
        value = value.astype(BF16)
        at = self.at(i)
        if self.plain:
            self.ref[at] = value
        else:
            split = value.reshape(-1, 2, self.tall, value.shape[1])
            self.ref[at[0], :, at[1], :] = split
        for move in self.moves(i):
            move.start()

    def finish(self):
        for i in range(N_TILES):
            for move in self.moves(i):
                move.wait()


def loop_tiles(step):
    def body(i, carry):
        step(i)
        return carry

    lax.fori_loop(0, N_TILES, body, 0)


FEED_HELD = (G, N2, R2, WIDE, SUMS_A, ACT, DFFN, WD, GP, HID, DUP, FEED, REST)


def feed_kernel(n_in, n_old, n_out, *refs):
    ins, outs, refs = split_refs(n_in, n_old, n_out, refs)
    g_hbm, gain2, n2, r2, act_hbm, down_share, wd_hbm, gp_hbm, hid_hbm, up_share = ins
    dffn_out, dup_out, sums_out, wide_out = outs[:4]
    at = dict(zip(FEED_HELD, refs))
    totals, sems = refs[len(FEED_HELD) : -1], refs[-1]
    inner, width = at[WD].shape
    tile = inner // N_TILES
    if len(totals) == 1:
        ways = [(totals[0], outs[4:]), (totals[0], outs[4:])]
    else:
        ways = [(total, [target]) for total, target in zip(totals, outs[4:])]
    down_way = GradientOut(*ways[0], sems, 40, tile, True)
    up_way = GradientOut(*ways[1], sems, 50, tile, False, tile // 4)
    is_first = lax.axis_index(LAYER) == 0
    copies = Copies(at, sems)
    own = Copies(at, sems)
    own.used = 4
    for name, source in ((G, g_hbm), (N2, n2), (R2, r2)):
        own.load(name, source, now=False)
    targets = ((DFFN, dffn_out), (WIDE, wide_out), (SUMS_A, sums_out))
    stores = [own.store(at[name], target, now=False) for name, target in targets]
    other = Copies(at, sems)
    other.used = 12
    other.load(DFFN, dffn_out, now=False)
    other.load(DUP, dup_out, now=False)

    def fetch(i):
        part = lanes_at(i * tile, tile)
        pairs = (
            (up_share.at[:, part], at[REST].at[:, part]),
            (wd_hbm.at[0, part, :], at[WD].at[part, :]),
            (gp_hbm.at[:, part], at[GP].at[:, part]),
        )
        return [
            pltpu.make_async_copy(source, target, sems.at[16 + 3 * i + k])
            for k, (source, target) in enumerate(pairs)
        ]

    def fetch_start(i):
        fetch(i)[0].start()

        @pl.when(is_first)
        def _():
            for move in fetch(i)[1:]:
                move.start()

    def away(i):
        part = lanes_at(i * tile, tile)
        return pltpu.make_async_copy(at[DUP].at[:, part], dup_out.at[:, part], sems.at[32 + i])

    @pl.when(is_first)
    def _():
        own.go()
        at[SUMS_A][...] = jnp.zeros(at[SUMS_A].shape, F32)
        own.ready(G, N2, R2)

    copies.load(ACT, act_hbm)
    copies.load(FEED, down_share)

    @pl.when(is_first)
    def _():
        second_norm_back(at, gain2, at[DFFN], 0)
        for way in stores[:2]:
            way.start()

    @pl.when(jnp.logical_not(is_first))
    def _():
        other.go()
        other.ready(DFFN, DUP)

    copies.load(HID, hid_hbm)
    fetch_start(0)
    copies.ready(ACT, FEED)
    fetch_start(1)

    def down_step(i):
        part = lanes_at(i * tile, tile)
        made = mm(at[ACT][:, part], at[DFFN][...], TN)
        down_way.put(i, made + at[FEED][part, :].astype(F32))

    loop_tiles(down_step)
    fetch_start(2)
    fetch_start(3)
    copies.ready(HID)

    def up_step(i):
        part = lanes_at(i * tile, tile)

        @pl.when(is_first)
        def _():
            for move in fetch(i)[1:]:
                move.wait()
            at[DUP][:, part] = up_back(at, at[DFFN][...], part)
            away(i).start()

        fetch(i)[0].wait()
        made = mm(at[HID][...], at[DUP][:, part], TN)
        up_way.put(i, made + at[REST][:, part].astype(F32))

    loop_tiles(up_step)
    down_way.finish()
    up_way.finish()

    @pl.when(is_first)
    def _():
        stores[2].start()
        for i in range(N_TILES):
            away(i).wait()
        own.finish()


def middle_kernel(n_in, n_old, n_out, *refs):
    ins, outs, refs = split_refs(n_in, n_old, n_out, refs)
    dup_hbm, wide_in, wu_hbm, gain1, n1, r1, wo_hbm, ctx_hbm = ins
    at = dict(zip((DUP, WIDE, WU, N1, R1, WO, CTX, DBR, DCTX, DELTA, SUMS_B), refs))

    @pl.when(lax.axis_index(LAYER) == 0)
    def _():
        copies = Copies(at, refs[-1])
        parts = [pl.ds(i * at[DUP].shape[1] // 2, at[DUP].shape[1] // 2) for i in range(2)]

        def get_half(i):
            copies.load(DUP, dup_hbm.at[:, parts[i]], at[DUP].at[:, parts[i]])
            copies.load(WU, wu_hbm.at[0, :, parts[i]], at[WU].at[:, parts[i]])

        get_half(0)
        copies.load(WIDE, wide_in)
        at[SUMS_B][...] = jnp.zeros(at[SUMS_B].shape, F32)
        copies.ready(DUP, WU, WIDE)
        get_half(1)
        at[WIDE][...] += mm(at[DUP][:, parts[0]], at[WU][:, parts[0]], NT)
        copies.ready(DUP, WU)
        copies.load(N1, n1)
        copies.load(R1, r1)
        copies.load(WO, wo_hbm.at[0])
        copies.load(CTX, ctx_hbm)
        at[WIDE][...] += mm(at[DUP][:, parts[1]], at[WU][:, parts[1]], NT)
        copies.ready(N1, R1)
        first_norm_back(at, gain1, at[DBR], 0)
        for name, target in ((DBR, outs[0]), (WIDE, outs[1]), (SUMS_B, outs[4])):
            copies.store(at[name], target)
        copies.ready(WO, CTX)
        context_back(at, at[DBR][...], at[CTX][...])
        copies.store(at[DCTX], outs[2])
        copies.store(at[DELTA], outs[3])
        copies.finish()


ATTEND_READ = (QKV, DCTX, KID, QID, LSE, DELTA)
ATTEND_HELD = ATTEND_READ + (X, CTX, DBR, REST, WIDE, WQKV, DQKV, SUMS_C, DX)


def attend_kernel(n_in, n_old, n_out, *refs):
    ins, outs, refs = split_refs(n_in, n_old, n_out, refs)
    x_hbm, ctx_hbm, dbr_hbm, share, wide_hbm, wq, wk, wv = ins[len(ATTEND_READ) :]
    dqkv_out, sums_out, dx_out = outs[:3]
    at = dict(zip(ATTEND_HELD, refs))
    total, sems = refs[-2:]
    width = at[X].shape[1]
    is_first = lax.axis_index(LAYER) == 0
    copies = Copies(at, sems)
    own = Copies(at, sems)
    own.used = 6
    for name, source in zip(ATTEND_READ, ins):
        own.load(name, source, now=False)
    targets = ((DQKV, dqkv_out), (SUMS_C, sums_out), (DX, dx_out))
    stores = [own.store(at[name], target, now=False) for name, target in targets]
    late = Copies(at, sems)
    late.used = 16
    late.load(WIDE, wide_hbm, now=False)
    for i, weight in enumerate((wq, wk, wv)):
        late.load(WQKV, weight.at[0], at[WQKV].at[:, pl.ds(i * width, width)], now=False)
    other = Copies(at, sems)
    other.used = 22
    other.load(DQKV, dqkv_out, now=False)

    @pl.when(is_first)
    def _():
        own.go()
        own.ready(*ATTEND_READ)

    for name, source in ((X, x_hbm), (CTX, ctx_hbm), (DBR, dbr_hbm), (REST, share)):
        copies.load(name, source)

    @pl.when(is_first)
    def _():
        late.go()
        over_pairs(width, lambda j: attend_pair_back(j, width, at, at[DQKV], 0))
        for way in stores[:2]:
            way.start()

    @pl.when(jnp.logical_not(is_first))
    def _():
        other.go()
        other.ready(DQKV)

    copies.ready(X, CTX, DBR, REST)
    way_out = GradientOut(total, outs[3:], sems, 24, width, False)
    way_out.put(0, mm(at[CTX][...], at[DBR][...], TN) + at[REST][:, 0:width].astype(F32))

    def step(i, carry):
        made = mm(at[X][...], at[DQKV][:, lanes_at((i - 1) * width, width)], TN)
        way_out.put(i, made + at[REST][:, lanes_at(i * width, width)].astype(F32))
        return carry

    lax.fori_loop(1, N_TILES, step, 0)

    @pl.when(is_first)
    def _():
        late.ready(WIDE, WQKV)
        at[DX][...] = (at[WIDE][...] + mm(at[DQKV][...], at[WQKV][...], NT)).astype(BF16)
        stores[2].start()
        own.finish()

    way_out.finish()


def swap(array, stride):
    count = lax.axis_size(ROWS)
    return lax.ppermute(array, ROWS, [(d, d ^ stride) for d in range(count)])


def halves_kernel(jobs, n_in, n_old, n_out, *refs):
    ins, outs, refs = split_refs(n_in, n_old, n_out, refs)
    copies = Copies({}, refs[-1])
    buffers = [refs[3 * i : 3 * i + 3] for i in range(len(jobs))]
    for i, job in enumerate(jobs):
        sources, stride, before, after, start, size, keep = job[:7]
        own = (lax.axis_index(ROWS) // stride) % 2
        which = own if keep else 1 - own
        for k in range(before):
            taken = pl.ds((2 * k + which) * after, after)
            for source, buffer in zip(sources, buffers[i]):
                target = buffer.at[pl.ds(k * after, after)]
                copies.load(i, ins[source].at[taken, :, pl.ds(start, size)], target)
    for i, job in enumerate(jobs):
        left, right, total = buffers[i]
        copies.ready(i)
        total[...] = (left[...].astype(F32) + right[...].astype(F32)).astype(BF16)
        place, start = job[7:]
        copies.store(total, outs[place].at[:, :, pl.ds(start, total.shape[-1])])
    copies.finish()


def halves(ways, arrays, n_outs):
    tall = arrays[0].shape[1]
    jobs, scratch = [], []
    outs = [None] * (2 * n_outs)
    for keep in (0, 1):
        for sources, stride, before, after, start, size, place, column in ways:
            jobs.append((sources, stride, before, after, start, size, keep, place + keep * n_outs, column))
            scratch += [((before * after, tall, size), BF16)] * 3
            outs[place + keep * n_outs] = ((before * after, tall, column + size), BF16)
    inputs = [(array, ANY) for array in arrays]
    made = call(partial(halves_kernel, tuple(jobs)), "halves", inputs, {}, outs, scratch, 48)
    return made[:n_outs], made[n_outs:]


class ScatterSum:
    def __init__(self, kept, came):
        self.kept, self.came = kept, came

    @staticmethod
    def cores(blocks):
        return ScatterSum(blocks[0], swap(blocks[1], 1))

    def second(self, first):
        kept = lax.optimization_barrier((self.kept, first))[0]
        half = kept.shape[-1] // 2
        ways = (((0, 1), 2, 4, 1, 0, half, 0, 0), ((0, 1), 4, 2, 2, half, half, 1, 0))
        sent, kept = halves(ways, (kept, self.came), 2)
        return ScatterSum(tuple(kept), (swap(sent[0], 2), swap(sent[1], 4)))

    def third(self, first):
        kept = lax.optimization_barrier((self.kept, first))[0]
        half = kept[0].shape[-1]
        ways = (((0, 1), 4, 2, 1, 0, half, 0, 0), ((2, 3), 2, 2, 1, 0, half, 1, 0))
        sent, kept = halves(ways, (kept[0], self.came[0], kept[1], self.came[1]), 2)
        return ScatterSum(tuple(kept), (swap(sent[0], 4), swap(sent[1], 2)))

    def fourth(self, first):
        kept = lax.optimization_barrier((self.kept, first))[0]
        half = kept[0].shape[-1]
        ways = tuple(((2 * i, 2 * i + 1), 8, 1, 1, 0, half, 0, i * half) for i in range(2))
        sent, kept = halves(ways, (kept[0], self.came[0], kept[1], self.came[1]), 1)
        return ScatterSum(kept[0], swap(sent[0], 8))

    def finish(self):
        return (self.kept.astype(F32) + self.came.astype(F32))[0]


def whole_sum(partial_sum):
    return lax.psum_scatter(partial_sum, ROWS, scatter_dimension=0, tiled=True).astype(F32)


def small_sum(values, beside, after):
    if lax.axis_size(ROWS) != 16:
        return lax.psum(values, ROWS)
    for stride, first in zip((1, 2, 4, 8), (*beside, None)):
        values = values + swap(values, stride)
        if first is not None:
            values = after(values, first)
    return values


def on_device(tokens, cotangent, segment_ids, valid_mask, cluster_perm, *params):
    section = lax.axis_index(LAYER)
    is_first = section == 0
    wq, _, wk, wv, _, wo, _, gain1, _, wu, _, wd, _, gain2, _ = params
    width, inner = wu.shape[1:]
    ids = (cluster_perm, segment_ids, valid_mask)
    shapes = shapes_of(width, inner)

    def hop(array, source, target):
        return lax.ppermute(array, LAYER, [(source, target)])

    def after(array, first):
        return lax.optimization_barrier((array, first))[0]

    row0, y0, stats00 = forward(0, 0, tokens, 0, ids, params, None)
    in0 = hop(y0, 0, 1)
    row1, y1, stats01 = forward(0, 1, tokens, 1, ids, params, None)
    in1 = hop(y1, 0, 1)
    row0, out0, stats10, grads0, dx0 = through_and_back(0, in0, cotangent, ids, params, row0)
    cotangent = after(cotangent, dx0)
    g0 = hop(dx0, 1, 0)
    row1, out1, stats11, grads1, dx1 = through_and_back(1, in1, cotangent, ids, params, row1)
    g0 = after(g0, dx1)
    g1 = hop(dx1, 1, 0)
    grads0, (dx0, down_share, up_share, rest_share) = backward(0, g0, 0, params, row0, grads0)
    g1 = after(g1, dx0)

    def at_hbm(*arrays):
        return [(array, ANY) for array in arrays]

    def of(*names):
        return [shapes[name] for name in names]

    totals, parts = gradient_shapes((inner, width), (width, inner))
    plain = len(totals) == 2
    made = call(
        feed_kernel,
        "feed",
        at_hbm(g1)
        + [(gain2, WHOLE)]
        + at_hbm(row1[N2], row1[R2], row1[ACT], down_share, wd, row1[GP], row1[HID], up_share),
        {0: grads1[DFFN], 1: grads1[DUP], 2: grads1[SUMS_A]},
        of(DFFN, DUP, SUMS_A, WIDE) + parts,
        of(G, N2, R2, WIDE, SUMS_A, ACT, DFFN, WD, GP, HID, DUP, WD, WU) + totals,
        60,
    )
    _, dup1, sums_a1, wide = made[:4]
    feed_parts = made[4:]
    if not plain:
        feed_sum = ScatterSum.cores(feed_parts)

    made = call(
        middle_kernel,
        "middle",
        at_hbm(dup1, wide, wu) + [(gain1, WHOLE)] + at_hbm(row1[N1], row1[R1], wo, row1[CTX]),
        {0: grads1[DBR], 4: grads1[SUMS_B]},
        of(DBR, WIDE, DCTX, DELTA, SUMS_B),
        of(DUP, WIDE, WU, N1, R1, WO, CTX, DBR, DCTX, DELTA, SUMS_B),
        20,
    )
    dbr1, wide, dctx, delta, sums_b1 = made
    if not plain:
        feed_sum = feed_sum.second(dctx)
        dctx = after(dctx, feed_sum.kept)

    totals, parts = gradient_shapes((width, 4 * width))
    made = call(
        attend_kernel,
        "attend",
        at_hbm(row1[QKV], dctx, *(row1[name] for name in (KID, QID, LSE)), delta)
        + at_hbm(row1[X], row1[CTX], dbr1, rest_share, wide, wq, wk, wv),
        {0: grads1[DQKV], 1: grads1[SUMS_C]},
        of(DQKV, SUMS_C, DX) + parts,
        of(*ATTEND_HELD) + totals,
        40,
    )
    _, sums_c1, dx1 = made[:3]
    came = []
    if plain:
        w_down, w_up, w_rest = (whole_sum(part) for part in (*feed_parts, made[3]))
        w_out, w_query, w_key, w_value = jnp.split(w_rest, 4, axis=1)
    else:
        feed_sum = feed_sum.third(dx1)
        rest_sum = ScatterSum.cores(after(tuple(made[3:]), feed_sum.kept))
        came.append(rest_sum.came)
        rest_sum = rest_sum.second(feed_sum.kept)
        dx1 = after(dx1, rest_sum.kept)
        came.append(rest_sum.came)
        feed_sum = feed_sum.fourth(rest_sum.kept)
        rest_sum = rest_sum.third(feed_sum.kept)
        came.append(rest_sum.came)
        rest_sum = rest_sum.fourth(rest_sum.kept)
        w_feed, w_rest = feed_sum.finish(), rest_sum.finish()
        tall = inner // 16
        w_down = w_feed[:tall]
        w_up = jnp.concatenate(jnp.split(w_feed[tall:], N_TILES, axis=0), axis=1)
        w_out, w_query, w_key, w_value = jnp.split(w_rest, 4, axis=0)

    sums_a1, sums_b1, sums_c1 = (after(array, dx1) for array in (sums_a1, sums_b1, sums_c1))
    stats10 = after(stats10, dx1)
    sum_a = (grads0[SUMS_A] + sums_a1).reshape(4, 8, inner).sum(axis=1)
    sum_b = (grads0[SUMS_B] + sums_b1).reshape(3, 8, width).sum(axis=1)
    sum_c = (grads0[SUMS_C] + sums_c1).reshape(2, 8, width).sum(axis=1)
    stats = jnp.where(is_first, stats00 + stats01, stats10 + stats11)
    stats = stats.reshape(3, 8 * width).sum(axis=1)
    count = jnp.sum(valid_mask.astype(F32))
    pieces = [sum_a[:3, :width].reshape(-1), sum_b.reshape(-1), sum_c.reshape(-1), sum_a[3]]
    base = 8 * width + inner
    spare = -(base + 4) % (8 * LANES)
    tail = jnp.concatenate([stats, jnp.broadcast_to(count, (1,)), jnp.zeros((spare,), F32)])
    small = jnp.concatenate(pieces + [tail]).reshape(-1, LANES)
    small = small_sum(small, came, after).reshape(-1)
    shares = lax.axis_size(ROWS)
    me = lax.axis_index(ROWS)

    def small_part(place, size):
        own = size // shares
        return lax.dynamic_slice_in_dim(small, place * width + me * own, own, 0)[None]

    gain2_sum, shift2_sum, down_bias, gain1_sum, shift1_sum, out_bias, query_bias, value_bias = (
        small_part(i, width) for i in range(8)
    )
    up_bias = small_part(8, inner)
    root_means = jnp.sqrt(small[base : base + 3] / (small[base + 3] * width))[None, :]

    half = width // 2
    dx0, out0, out1 = (after(array, dx1) for array in (dx0, out0, out1))
    outgoing = jnp.concatenate(
        [
            jnp.where(is_first, grad[:, half:], made[:, :half])
            for grad, made in ((dx0, out0), (dx1, out1))
        ]
    )
    arrived = lax.ppermute(outgoing, LAYER, [(0, 1), (1, 0)])
    block_own = jnp.concatenate([out0[:, half:], out1[:, half:]])
    grad_own = jnp.concatenate([dx0[:, :half], dx1[:, :half]])
    block_part = jnp.where(is_first, arrived, block_own)
    grad_part = jnp.where(is_first, grad_own, arrived)
    return (
        block_part,
        grad_part,
        w_query[None],
        query_bias,
        w_key[None],
        w_value[None],
        value_bias,
        w_out[None],
        out_bias,
        gain1_sum,
        shift1_sum,
        w_up[None],
        up_bias,
        w_down[None],
        down_bias,
        gain2_sum,
        shift2_sum,
        root_means,
    )


def solution(mesh):
    by_layer = P(LAYER, None)
    matrix = P(LAYER, None, None)
    share = P(LAYER, ROWS)
    matrix_share = P(LAYER, ROWS, None)
    rows = P(ROWS, None)
    vectors = {1, 4, 6, 7, 8, 10, 12, 13, 14}
    matrices = {2, 4, 5, 7, 11, 13}
    return jax.shard_map(
        on_device,
        mesh=mesh,
        in_specs=(rows, rows, rows, rows, P(LAYER, ROWS, None, None))
        + tuple(by_layer if i in vectors else matrix for i in range(15)),
        out_specs=(P(ROWS, LAYER), P(ROWS, LAYER))
        + tuple(matrix_share if i in matrices else share for i in range(2, 17))
        + (P(LAYER, None),),
        check_vma=False,
    )
```

```python
from functools import partial

import jax
import jax.numpy as jnp
from jax import lax
from jax.experimental import pallas as pl
from jax.experimental.pallas import tpu as pltpu
from jax.sharding import PartitionSpec as P

HEAD_DIM = 64
CLUSTER = 128
SEQ = 512
LANES = 128
ROW_BLOCK = 512
PAIR_UNROLL = 3
MIB = 1024 * 1024

BF16 = jnp.bfloat16
F32 = jnp.float32
LOG2E = 1.4426950408889634
SCALE = HEAD_DIM**-0.5
SCORE_SCALE = SCALE * LOG2E

NN = ((1,), (0,))
NT = ((1,), (1,))
TN = ((0,), (0,))

ROWS = "dp"
LAYER = "section"
ANY = pl.BlockSpec(memory_space=pltpu.HBM)
WHOLE = pl.BlockSpec(memory_space=pltpu.VMEM)
SHORT = pl.CostEstimate(flops=1, bytes_accessed=1, transcendentals=0)

X, QKV, CTX, LSE, KID, QID, N1, R1, HID, ACT, GP, N2, R2 = range(13)
G, DFFN, DUP, DBR, DQKV, SUMS_A, SUMS_B, SUMS_C, WIDE, DCTX, DELTA, DX, FEED, LIVE = range(13, 27)
BIAS, WQKV, Y, STATS, WO, WU, WD, REST = range(27, 35)
SAVED = (X, QKV, CTX, LSE, KID, QID, N1, R1, HID, ACT, GP, N2, R2)
GRADS = (DFFN, DUP, DBR, DQKV, SUMS_A, SUMS_B, SUMS_C)
GAIN2, SHIFT2, B_DOWN, B_UP = 0, 8, 16, 24
GAIN1, SHIFT1, B_OUT = 0, 8, 16
B_QUERY, B_VALUE = 0, 8


def shapes_of(width, inner):
    token, token32, narrow = ((SEQ, width), BF16), ((SEQ, width), F32), ((SEQ, LANES), F32)
    heads = ((16, SEQ), F32)
    shapes = {name: token for name in (X, CTX, N1, HID, N2, G, DFFN, DBR, DCTX, DX, Y)}
    shapes.update({name: token32 for name in (KID, WIDE, FEED)})
    shapes.update({name: narrow for name in (R1, R2, LIVE)})
    shapes.update({name: heads for name in (LSE, QID, DELTA)})
    shapes.update({name: ((SEQ, inner), BF16) for name in (ACT, GP, DUP)})
    shapes.update({name: ((SEQ, 3 * width), BF16) for name in (QKV, DQKV)})
    shapes.update({SUMS_A: ((32, inner), F32), SUMS_B: ((24, width), F32)})
    shapes.update({SUMS_C: ((16, width), F32), STATS: ((24, width), F32), BIAS: ((8, width), F32)})
    shapes.update({WQKV: ((width, 3 * width), BF16), WO: ((width, width), BF16)})
    shapes.update({WU: ((width, inner), BF16), WD: ((inner, width), BF16)})
    shapes[REST] = ((width, 4 * width), BF16)
    return shapes


def mm(left, right, dims):
    return lax.dot_general(left, right, (dims, ((), ())), preferred_element_type=F32)


def vec(ref):
    return ref[0:1, :].astype(F32)


def lanes_at(start, size=LANES):
    return pl.ds(pl.multiple_of(start, LANES), size)


def fold8(block):
    return jnp.sum(block.reshape(-1, 8, block.shape[-1]), axis=0)


def over_rows(step):
    def body(i, carry):
        step(pl.ds(pl.multiple_of(i * ROW_BLOCK, ROW_BLOCK), ROW_BLOCK))
        return carry

    lax.fori_loop(0, SEQ // ROW_BLOCK, body, 0)


def over_tiles(size, tile, step):
    def body(i, carry):
        step(pl.ds(pl.multiple_of(i * tile, tile), tile))
        return carry

    lax.fori_loop(0, size // tile, body, 0)


class Copies:
    def __init__(self, at, sems):
        self.at, self.sems = at, sems
        self.used = 0
        self.loads = {}
        self.stores = []

    def plan(self, source, target):
        self.used += 1
        return pltpu.make_async_copy(source, target, self.sems.at[self.used - 1])

    def load(self, name, source, target=None, now=True):
        target = self.at[name] if target is None else target
        copy = self.plan(source, target)
        self.loads.setdefault(name, []).append(copy)
        if now:
            copy.start()

    def go(self):
        for copies in self.loads.values():
            for copy in copies:
                copy.start()

    def ready(self, *names):
        for name in names:
            for copy in self.loads.pop(name, ()):
                copy.wait()

    def store(self, source, target, now=True):
        copy = self.plan(source, target)
        self.stores.append(copy)
        if now:
            copy.start()
        return copy

    def finish(self):
        for copy in self.stores:
            copy.wait()


def load_qkv(copies, weights, width):
    for i, weight in enumerate(weights):
        copies.load(WQKV, weight.at[0], copies.at[WQKV].at[:, pl.ds(i * width, width)])


def call(body, name, inputs, old, outs, scratch, n_sems):
    arrays = [array for array, _ in inputs]
    n_in = len(arrays)
    return pl.pallas_call(
        partial(body, n_in, len(old), len(outs)),
        out_shape=[jax.ShapeDtypeStruct(*shape) for shape in outs],
        in_specs=[spec for _, spec in inputs] + [ANY] * len(old),
        out_specs=[ANY] * len(outs),
        input_output_aliases={n_in + i: place for i, place in enumerate(old)},
        scratch_shapes=[pltpu.VMEM(*shape) for shape in scratch]
        + [pltpu.SemaphoreType.DMA((n_sems,))],
        compiler_params=pltpu.CompilerParams(vmem_limit_bytes=58 * MIB),
        cost_estimate=SHORT,
        name=name,
    )(*arrays, *old.values())


def split_refs(n_in, n_old, n_out, refs):
    return refs[:n_in], refs[n_in + n_old : n_in + n_old + n_out], refs[n_in + n_old + n_out :]


def low_lanes():
    return lax.broadcasted_iota(jnp.int32, (SEQ, LANES), 1) < HEAD_DIM


def masked(scores, kid_column, qid_row):
    shape = (CLUSTER, CLUSTER)
    same = lax.broadcasted_iota(jnp.int32, shape, 0) == lax.broadcasted_iota(jnp.int32, shape, 1)
    count = SEQ // CLUSTER
    parts = [slice(i * CLUSTER, (i + 1) * CLUSTER) for i in range(count)]
    rows = []
    for i in range(count):
        tiles = []
        for j in range(count):
            ok = kid_column[parts[i]] == qid_row[:, parts[j]]
            if i == j:
                ok = ok | same
            tiles.append(jnp.where(ok, scores[parts[i], parts[j]], -1e30))
        rows.append(jnp.concatenate(tiles, axis=1))
    return jnp.concatenate(rows, axis=0)


def attend_pair(j, width, at):
    low = low_lanes()
    lanes = lanes_at(j * LANES)
    query = at[QKV][:, lanes]
    key = at[QKV][:, lanes_at(width + j * LANES)]
    value = at[QKV][:, lanes_at(2 * width + j * LANES)]
    kid_pair = at[KID][:, lanes]
    mixed, tops = [], []
    for half in (0, 1):
        own = low if half == 0 else ~low
        own_query = jnp.where(own, query, jnp.zeros_like(query))
        value_ones = jnp.where(own, value, jnp.ones_like(value))
        kid_column = kid_pair[:, half * HEAD_DIM : half * HEAD_DIM + 1]
        scores = mm(key, own_query, NT) * SCORE_SCALE
        scores = masked(scores, kid_column, at[QID][pl.ds(2 * j + half, 1), :])
        top = jnp.max(scores, axis=0, keepdims=True)
        tops.append(top)
        mixed.append(mm(jnp.exp2(scores - top).astype(BF16), value_ones, TN))
    sums = [pltpu.roll(part, HEAD_DIM, 1) for part in mixed]
    total = jnp.where(low, sums[0], sums[1])
    at[CTX][:, lanes] = (jnp.where(low, mixed[0], mixed[1]) / total).astype(BF16)
    turned = total.T
    for half in (0, 1):
        row = turned[half * HEAD_DIM : half * HEAD_DIM + 1, :]
        at[LSE][pl.ds(2 * j + half, 1), :] = tops[half] + jnp.log2(row)


def attend_pair_back(j, width, at, target, base):
    low = low_lanes()
    lanes = [lanes_at(i * width + j * LANES) for i in range(3)]
    query, key, value = (at[QKV][:, part] for part in lanes)
    d_out = at[DCTX][:, lanes[0]]
    kid_pair = at[KID][:, lanes[0]]
    d_query, d_key, d_value = [], [], []
    for half in (0, 1):
        h = pl.ds(2 * j + half, 1)
        own = low if half == 0 else ~low
        own_query = jnp.where(own, query, jnp.zeros_like(query))
        own_out = jnp.where(own, d_out, jnp.zeros_like(d_out))
        kid_column = kid_pair[:, half * HEAD_DIM : half * HEAD_DIM + 1]
        scores = mm(key, own_query, NT) * SCORE_SCALE - at[LSE][h, :]
        weights = jnp.exp2(masked(scores, kid_column, at[QID][h, :]))
        d_weights = mm(value, own_out, NT)
        d_scores = (weights * (d_weights - at[DELTA][h, :])).astype(BF16)
        d_value.append(mm(weights.astype(BF16), own_out, NN))
        d_key.append(mm(d_scores, own_query, NN))
        d_query.append(mm(d_scores, key, TN))
    made = (
        jnp.where(low, d_query[0], d_query[1]) * SCALE,
        (d_key[0] + d_key[1]) * SCALE,
        d_value[0] + d_value[1],
    )
    rows = pl.ds(base, SEQ)
    for i, place in ((0, B_QUERY), (1, None), (2, B_VALUE)):
        rounded = made[i].astype(BF16)
        target[rows, lanes[i]] = rounded
        if place is not None:
            at[SUMS_C][place : place + 8, lanes[0]] = fold8(rounded.astype(F32))


def over_pairs(width, step):
    def body(j, carry):
        step(j)
        return carry

    lax.fori_loop(0, width // LANES, body, 0, unroll=PAIR_UNROLL)


def token_ids(row, heads, perm_ref, seg_ref, valid_ref, kid_ref, qid_ref):
    token = lax.broadcasted_iota(jnp.int32, (SEQ, LANES), 0)
    lane = lax.broadcasted_iota(jnp.int32, (SEQ, LANES), 1)
    seg_row = seg_ref[row : row + 1, :].astype(F32)
    valid_row = valid_ref[row : row + 1, :].astype(F32)
    at = lax.broadcasted_iota(jnp.int32, (LANES, SEQ), 0)
    both = jnp.where(at == 0, seg_row, jnp.where(at == 1, valid_row, 0.0)).T
    segment, live = both[:, 0:1], both[:, 1:2]

    def column(h):
        places = perm_ref[0, row, pl.ds(h, 1), :]
        mine = jnp.zeros((SEQ, LANES), F32)
        for c in range(1, SEQ // CLUSTER):
            part = places[:, c * CLUSTER : (c + 1) * CLUSTER]
            mine = jnp.where(token == part, float(c), mine)
        return jnp.sum(mine, axis=1, keepdims=True) * 4.0 + segment

    def pair(j, ids):
        left, right = column(2 * j), column(2 * j + 1)
        own = jnp.where(lane < HEAD_DIM, left, right)
        kid_ref[:, lanes_at(j * LANES)] = jnp.where(live > 0.5, own, -1.0)
        ids = jnp.where(lane == 2 * j, left, ids)
        return jnp.where(lane == 2 * j + 1, right, ids)

    qid = lax.fori_loop(0, heads // 2, pair, jnp.zeros((SEQ, LANES), F32))
    qid_ref[...] = qid.T[0:16, :]
    return live


def normed(total):
    centre = total - jnp.mean(total, axis=-1, keepdims=True)
    spread = jnp.mean(centre * centre, axis=-1, keepdims=True)
    rate = lax.rsqrt(spread + 1e-05)
    return centre * rate, rate


FORWARD_HELD = SAVED + (WQKV, WO, WU, WD, WIDE, FEED, Y, STATS, LIVE, BIAS)


def run_forward(at, copies, save, row, source, ids, params, later=None):
    perm_ref, seg_ref, valid_ref = ids
    wq, bq, wk, wv, bv, wo, bo, g1, s1, wu, bu, wd, bd, g2, s2 = params
    width, inner = at[WU].shape
    heads = width // HEAD_DIM
    copies.load(X, source)
    first = copies.used
    load_qkv(copies, (wq, wk, wv), width)
    live = token_ids(row, heads, perm_ref, seg_ref, valid_ref, at[KID], at[QID])
    at[LIVE][...] = jnp.broadcast_to(live, (SEQ, LANES))
    at[LSE][...] = jnp.zeros((16, SEQ), F32)
    at[STATS][...] = jnp.zeros((24, width), F32)
    at[BIAS][0:1, :] = vec(bq)
    at[BIAS][1:2, :] = jnp.zeros((1, width), F32)
    at[BIAS][2:3, :] = vec(bv)
    copies.ready(X)

    def to_qkv(i, carry):
        part = pl.ds(pl.multiple_of(i * width, LANES), width)
        weight = at[WQKV].at[:, part]
        pltpu.make_async_copy(weight, weight, copies.sems.at[first + i]).wait()
        made = mm(at[X][...], at[WQKV][:, part], NN) + at[BIAS][pl.ds(i, 1), :]
        at[QKV][:, part] = made.astype(BF16)
        return carry

    lax.fori_loop(0, 3, to_qkv, 0)
    copies.loads.pop(WQKV)
    copies.load(WO, wo.at[0])
    copies.load(WU, wu.at[0])
    copies.load(WD, wd.at[0])
    if later is not None:
        later()
    save(KID, QID, X, QKV)
    over_pairs(width, lambda j: attend_pair(j, width, at))
    save(LSE, CTX)
    copies.ready(WO)
    at[WIDE][...] = mm(at[CTX][...], at[WO][...], NN)

    def first_norm(rows):
        branch = at[WIDE][rows, :] + vec(bo)
        alive = at[LIVE][rows, 0:1]
        at[STATS][0:8, :] += fold8(branch * branch * alive)
        unit, rate = normed(at[X][rows, :].astype(F32) + branch)
        hidden = unit * vec(g1) + vec(s1)
        at[N1][rows, :] = unit.astype(BF16)
        at[R1][rows, :] = jnp.broadcast_to(rate, (ROW_BLOCK, LANES))
        at[HID][rows, :] = hidden.astype(BF16)
        at[WIDE][rows, :] = hidden

    over_rows(first_norm)
    save(N1, R1, HID)
    copies.ready(WU)

    def up(part):
        upper = mm(at[HID][...], at[WU][:, part], NN) + bu[0:1, part].astype(F32)
        half = 0.5 + 0.5 * lax.erf(upper * 0.5**0.5)
        bell = jnp.exp2(upper * upper * (-0.5 * LOG2E)) * 0.3989422804014327
        at[ACT][:, part] = (upper * half).astype(BF16)
        at[GP][:, part] = (half + upper * bell).astype(BF16)

    over_tiles(inner, inner // 2, up)
    save(ACT, GP)
    copies.ready(WD)
    at[FEED][...] = mm(at[ACT][...], at[WD][...], NN)

    def second_norm(rows):
        ffn = at[FEED][rows, :] + vec(bd)
        alive = at[LIVE][rows, 0:1]
        at[STATS][8:16, :] += fold8(ffn * ffn * alive)
        unit, rate = normed(at[WIDE][rows, :] + ffn)
        result = unit * vec(g2) + vec(s2)
        at[STATS][16:24, :] += fold8(result * result * alive)
        at[N2][rows, :] = unit.astype(BF16)
        at[R2][rows, :] = jnp.broadcast_to(rate, (ROW_BLOCK, LANES))
        at[Y][rows, :] = result.astype(BF16)

    over_rows(second_norm)
    save(Y, STATS, N2, R2)


def forward_kernel(section, row, x_row, n_in, n_old, n_out, *refs):
    ins, outs, refs = split_refs(n_in, n_old, n_out, refs)
    out = dict(zip(SAVED + (Y, STATS), outs))
    at = dict(zip(FORWARD_HELD, refs))

    @pl.when(lax.axis_index(LAYER) == section)
    def _():
        copies = Copies(at, refs[-1])

        def save(*names):
            for name in names:
                copies.store(at[name], out[name])

        source = ins[0].at[pl.ds(x_row * SEQ, SEQ), :]
        run_forward(at, copies, save, row, source, ins[1:4], ins[4:])
        copies.finish()


def forward(section, row, x, x_row, ids, params, kept):
    width, inner = params[9].shape[1:]
    shapes = shapes_of(width, inner)
    inputs = [(x, ANY)] + [(array, WHOLE) for array in ids]
    inputs += [(array, ANY if array.ndim == 3 else WHOLE) for array in params]
    made = call(
        partial(forward_kernel, section, row, x_row),
        "forward",
        inputs,
        {} if kept is None else {i: kept[name] for i, name in enumerate(SAVED)},
        [shapes[name] for name in SAVED + (Y, STATS)],
        [shapes[name] for name in FORWARD_HELD],
        32,
    )
    return dict(zip(SAVED, made)), made[-2], made[-1]


def norm_back(grad, unit, rate, gain):
    scaled = grad * gain
    mean = jnp.mean(scaled, axis=-1, keepdims=True)
    along = jnp.mean(scaled * unit, axis=-1, keepdims=True)
    return (scaled - mean - unit * along) * rate


def add_sum(ref, place, value):
    ref[place : place + 8, 0 : value.shape[-1]] += fold8(value)


def second_norm_back(at, gain2, target, base):
    def step(rows):
        grad = at[G][rows, :].astype(F32)
        unit = at[N2][rows, :].astype(F32)
        add_sum(at[SUMS_A], GAIN2, grad * unit)
        add_sum(at[SUMS_A], SHIFT2, grad)
        d_second = norm_back(grad, unit, at[R2][rows, 0:1], vec(gain2))
        at[WIDE][rows, :] = d_second
        low = d_second.astype(BF16)
        target[pl.ds(pl.multiple_of(rows.start + base, ROW_BLOCK), ROW_BLOCK), :] = low
        add_sum(at[SUMS_A], B_DOWN, low.astype(F32))

    over_rows(step)


def up_back(at, dffn, part):
    d_act = mm(dffn, at[WD][part, :], NT)
    low = (d_act * at[GP][:, part].astype(F32)).astype(BF16)
    at[SUMS_A][B_UP : B_UP + 8, part] += fold8(low.astype(F32))
    return low


def first_norm_back(at, gain1, target, base):
    def step(rows):
        grad = at[WIDE][rows, :]
        unit = at[N1][rows, :].astype(F32)
        add_sum(at[SUMS_B], GAIN1, grad * unit)
        add_sum(at[SUMS_B], SHIFT1, grad)
        d_first = norm_back(grad, unit, at[R1][rows, 0:1], vec(gain1))
        at[WIDE][rows, :] = d_first
        low = d_first.astype(BF16)
        target[pl.ds(pl.multiple_of(rows.start + base, ROW_BLOCK), ROW_BLOCK), :] = low
        add_sum(at[SUMS_B], B_OUT, low.astype(F32))

    over_rows(step)


def context_back(at, dbr, context):
    width = dbr.shape[1]
    d_context = mm(dbr, at[WO][...], NT).astype(BF16)
    at[DCTX][...] = d_context
    product = d_context.astype(F32) * context.astype(F32)
    high = product.astype(BF16)
    rest = (product - high.astype(F32)).astype(BF16)
    of_head = (
        lax.broadcasted_iota(jnp.int32, (16, width), 1) // HEAD_DIM
        == lax.broadcasted_iota(jnp.int32, (16, width), 0)
    )
    pick = jnp.where(of_head, 1.0, 0.0).astype(BF16)
    at[DELTA][...] = mm(pick, high, NT) + mm(pick, rest, NT)


def run_backward(at, copies, get, save, params, shared):
    gain1, gain2 = params[:2]
    width, inner = at[WU].shape
    get(G, N2, R2)
    for name in (SUMS_A, SUMS_B):
        at[name][...] = jnp.zeros(at[name].shape, F32)
    copies.ready(G, N2, R2)
    get(WD, GP)
    second_norm_back(at, gain2, at[DFFN], 0)
    save(DFFN)
    get(WU, N1, R1, WO, CTX)
    copies.ready(WD, GP)

    def up(part):
        at[DUP][:, part] = up_back(at, at[DFFN][...], part)

    over_tiles(inner, inner // 2, up)
    save(DUP, SUMS_A)
    get(QKV, KID, QID, LSE, WQKV)
    copies.ready(WU)
    at[WIDE][...] += mm(at[DUP][...], at[WU][...], NT)
    copies.ready(N1, R1)
    first_norm_back(at, gain1, at[DBR], 0)
    save(DBR, SUMS_B)
    copies.ready(WO, CTX)
    context_back(at, at[DBR][...], at[CTX][...])
    copies.ready(QKV, KID, QID, LSE)
    if shared is not None:
        shared.go()
    over_pairs(width, lambda j: attend_pair_back(j, width, at, at[DQKV], 0))
    save(DQKV, SUMS_C)
    copies.ready(WQKV)
    at[DX][...] = (at[WIDE][...] + mm(at[DQKV][...], at[WQKV][...], NT)).astype(BF16)
    save(DX)


BACK_READ = (N2, R2, GP, N1, R1, CTX, LSE, KID, QID, QKV)
SHARE_READ = (ACT, HID, X)
BACK_HELD = (G,) + BACK_READ + GRADS + (WIDE, DCTX, DELTA, DX, WQKV, WO, WU, WD)


def backward_kernel(section, g_row, n_in, n_old, n_out, *refs):
    ins, outs, refs = split_refs(n_in, n_old, n_out, refs)
    g_hbm, gain1, gain2, wq, wk, wv, wo, wu, wd = ins[:9]
    given = dict(zip(BACK_READ + SHARE_READ, ins[9:]))
    given.update({WO: wo.at[0], WU: wu.at[0], WD: wd.at[0]})
    given[G] = g_hbm.at[pl.ds(g_row * SEQ, SEQ), :]
    with_shares = section == 0
    out = dict(zip(GRADS + (DX,), outs))
    at = dict(zip(BACK_HELD + (SHARE_READ if with_shares else ()), refs))
    width, inner = at[WU].shape
    shared = Copies(at, refs[-1])
    shared.used = 40
    if with_shares:
        for name in SHARE_READ:
            shared.load(name, given[name], now=False)

        @pl.when(lax.axis_index(LAYER) != section)
        def _():
            others = Copies(at, refs[-1])
            others.used = 50
            for name in (DFFN, DUP, DBR, DQKV):
                others.load(name, out[name])
            others.load(CTX, given[CTX])
            shared.go()
            others.ready(DFFN, DUP, DBR, DQKV, CTX)

    @pl.when(lax.axis_index(LAYER) == section)
    def _():
        copies = Copies(at, refs[-1])

        def get(*names):
            for name in names:
                if name == WQKV:
                    load_qkv(copies, (wq, wk, wv), width)
                else:
                    copies.load(name, given[name])

        def save(*names):
            for name in names:
                copies.store(at[name], out[name])

        run_backward(at, copies, get, save, ins[1:3], shared if with_shares else None)
        copies.finish()

    if not with_shares:
        return
    down, up, rest = at[WD], at[WU], refs[-2]
    shared.ready(*SHARE_READ)

    def to_down(part):
        down[part, :] = mm(at[ACT][:, part], at[DFFN][...], TN).astype(BF16)

    over_tiles(inner, width, to_down)
    shared.store(down, outs[-3])

    def to_up(part):
        up[:, part] = mm(at[HID][...], at[DUP][:, part], TN).astype(BF16)

    over_tiles(inner, width, to_up)
    shared.store(up, outs[-2])
    rest[:, 0:width] = mm(at[CTX][...], at[DBR][...], TN).astype(BF16)

    def to_rest(i, carry):
        made = mm(at[X][...], at[DQKV][:, lanes_at(i * width - width, width)], TN)
        rest[:, lanes_at(i * width, width)] = made.astype(BF16)
        return carry

    lax.fori_loop(1, 4, to_rest, 0)
    shared.store(rest, outs[-1])
    shared.finish()


def backward(section, g, g_row, params, kept, old):
    wq, _, wk, wv, _, wo, _, gain1, _, wu, _, wd, _, gain2, _ = params
    shapes = shapes_of(*wu.shape[1:])
    inputs = [(g, ANY), (gain1, WHOLE), (gain2, WHOLE)]
    inputs += [(array, ANY) for array in (wq, wk, wv, wo, wu, wd)]
    inputs += [(kept[name], ANY) for name in BACK_READ]
    outs, held = list(GRADS + (DX,)), list(BACK_HELD)
    if section == 0:
        inputs += [(kept[name], ANY) for name in SHARE_READ]
        outs += [WD, WU, REST]
        held += SHARE_READ + (REST,)
    made = call(
        partial(backward_kernel, section, g_row),
        "backward",
        inputs,
        {} if old is None else {i: old[name] for i, name in enumerate(GRADS)},
        [shapes[name] for name in outs],
        [shapes[name] for name in held],
        56,
    )
    return dict(zip(GRADS, made)), made[len(GRADS) :]


KEPT = (X, CTX, HID, ACT)
BOTH_HELD = FORWARD_HELD + (G,) + GRADS + (DCTX, DELTA, DX)


def both_kernel(row, n_in, n_old, n_out, *refs):
    ins, outs, refs = split_refs(n_in, n_old, n_out, refs)
    out = dict(zip(KEPT + (Y, STATS) + GRADS + (DX,), outs))
    at = dict(zip(BOTH_HELD, refs))
    params = ins[5:]

    @pl.when(lax.axis_index(LAYER) == 1)
    def _():
        copies = Copies(at, refs[-1])

        def save(*names):
            for name in names:
                if name in out:
                    copies.store(at[name], out[name])

        def get(*names):
            pass

        def later():
            copies.load(G, ins[1].at[pl.ds(row * SEQ, SEQ), :])

        run_forward(at, copies, save, row, ins[0], ins[2:5], params, later)
        run_backward(at, copies, get, save, (params[7], params[13]), None)
        copies.finish()


def through_and_back(row, x, g, ids, params, kept):
    shapes = shapes_of(*params[9].shape[1:])
    inputs = [(x, ANY), (g, ANY)] + [(array, WHOLE) for array in ids]
    inputs += [(array, ANY if array.ndim == 3 else WHOLE) for array in params]
    names = KEPT + (Y, STATS) + GRADS + (DX,)
    made = call(
        partial(both_kernel, row),
        "both",
        inputs,
        {i: kept[name] for i, name in enumerate(KEPT)},
        [shapes[name] for name in names],
        [shapes[name] for name in BOTH_HELD],
        48,
    )
    made = dict(zip(names, made))
    kept = {**kept, **{name: made[name] for name in KEPT}}
    return kept, made[Y], made[STATS], {name: made[name] for name in GRADS}, made[DX]


N_TILES = 4


def gradient_shapes(*sizes):
    count = lax.axis_size(ROWS)
    if count != 16:
        shapes = [(size, BF16) for size in sizes]
        return shapes, shapes
    tall = sum(rows * columns for rows, columns in sizes) // (count * min(map(min, sizes)))
    width = min(map(min, sizes))
    return [((8, 2, tall, width), BF16)], [((8, tall, width), BF16)] * 2


class GradientOut:
    def __init__(self, ref, targets, sems, first_sem, tile, by_rows, base=0):
        self.ref, self.targets, self.sems, self.first_sem = ref, targets, sems, first_sem
        self.tile, self.by_rows, self.base = tile, by_rows, base
        self.plain = len(targets) == 1
        self.tall = tile // 4 if by_rows else tile // 16

    def at(self, i):
        start = i * self.tile
        if self.plain and self.by_rows:
            return (pl.ds(pl.multiple_of(start, 16), self.tile),)
        if self.plain:
            return (slice(None), lanes_at(start, self.tile))
        if self.by_rows:
            return (pl.ds(2 * i, 2), pl.ds(self.base, self.tall))
        return (slice(None), pl.ds(pl.multiple_of(self.base + i * self.tall, 16), self.tall))

    def moves(self, i):
        at = self.at(i)
        if self.plain:
            pairs = [(self.ref.at[at], self.targets[0].at[at])]
        else:
            core = lax.axis_index(ROWS) % 2
            pairs = [
                (self.ref.at[at[0], which, at[1]], target.at[at])
                for target, which in zip(self.targets, (core, 1 - core))
            ]
        base = self.first_sem + i * len(pairs)
        return [
            pltpu.make_async_copy(source, target, self.sems.at[base + k])
            for k, (source, target) in enumerate(pairs)
        ]

    def put(self, i, value):
        value = value.astype(BF16)
        at = self.at(i)
        if self.plain:
            self.ref[at] = value
        else:
            split = value.reshape(-1, 2, self.tall, value.shape[1])
            self.ref[at[0], :, at[1], :] = split
        for move in self.moves(i):
            move.start()

    def finish(self):
        for i in range(N_TILES):
            for move in self.moves(i):
                move.wait()


def loop_tiles(step):
    def body(i, carry):
        step(i)
        return carry

    lax.fori_loop(0, N_TILES, body, 0)


FEED_HELD = (G, N2, R2, WIDE, SUMS_A, ACT, DFFN, WD, GP, HID, DUP, FEED, REST)


def feed_kernel(n_in, n_old, n_out, *refs):
    ins, outs, refs = split_refs(n_in, n_old, n_out, refs)
    g_hbm, gain2, n2, r2, act_hbm, down_share, wd_hbm, gp_hbm, hid_hbm, up_share = ins
    dffn_out, dup_out, sums_out, wide_out = outs[:4]
    at = dict(zip(FEED_HELD, refs))
    totals, sems = refs[len(FEED_HELD) : -1], refs[-1]
    inner, width = at[WD].shape
    tile = inner // N_TILES
    if len(totals) == 1:
        ways = [(totals[0], outs[4:]), (totals[0], outs[4:])]
    else:
        ways = [(total, [target]) for total, target in zip(totals, outs[4:])]
    down_way = GradientOut(*ways[0], sems, 40, tile, True)
    up_way = GradientOut(*ways[1], sems, 50, tile, False, tile // 4)
    is_first = lax.axis_index(LAYER) == 0
    copies = Copies(at, sems)
    own = Copies(at, sems)
    own.used = 4
    for name, source in ((G, g_hbm), (N2, n2), (R2, r2)):
        own.load(name, source, now=False)
    targets = ((DFFN, dffn_out), (WIDE, wide_out), (SUMS_A, sums_out))
    stores = [own.store(at[name], target, now=False) for name, target in targets]
    other = Copies(at, sems)
    other.used = 12
    other.load(DFFN, dffn_out, now=False)
    other.load(DUP, dup_out, now=False)

    def fetch(i):
        part = lanes_at(i * tile, tile)
        pairs = (
            (up_share.at[:, part], at[REST].at[:, part]),
            (wd_hbm.at[0, part, :], at[WD].at[part, :]),
            (gp_hbm.at[:, part], at[GP].at[:, part]),
        )
        return [
            pltpu.make_async_copy(source, target, sems.at[16 + 3 * i + k])
            for k, (source, target) in enumerate(pairs)
        ]

    def fetch_start(i):
        fetch(i)[0].start()

        @pl.when(is_first)
        def _():
            for move in fetch(i)[1:]:
                move.start()

    def away(i):
        part = lanes_at(i * tile, tile)
        return pltpu.make_async_copy(at[DUP].at[:, part], dup_out.at[:, part], sems.at[32 + i])

    @pl.when(is_first)
    def _():
        own.go()

    copies.load(ACT, act_hbm)
    copies.load(FEED, down_share)

    @pl.when(is_first)
    def _():
        at[SUMS_A][...] = jnp.zeros(at[SUMS_A].shape, F32)
        own.ready(G, N2, R2)

    copies.load(HID, hid_hbm)
    fetch_start(0)

    @pl.when(is_first)
    def _():
        second_norm_back(at, gain2, at[DFFN], 0)
        for way in stores[:2]:
            way.start()

    @pl.when(jnp.logical_not(is_first))
    def _():
        other.go()
        other.ready(DFFN, DUP)

    copies.ready(ACT, FEED)
    fetch_start(1)

    def down_step(i):
        part = lanes_at(i * tile, tile)
        made = mm(at[ACT][:, part], at[DFFN][...], TN)
        down_way.put(i, made + at[FEED][part, :].astype(F32))

    loop_tiles(down_step)
    fetch_start(2)
    fetch_start(3)
    copies.ready(HID)

    def up_step(i):
        part = lanes_at(i * tile, tile)

        @pl.when(is_first)
        def _():
            for move in fetch(i)[1:]:
                move.wait()
            at[DUP][:, part] = up_back(at, at[DFFN][...], part)
            away(i).start()

        fetch(i)[0].wait()
        made = mm(at[HID][...], at[DUP][:, part], TN)
        up_way.put(i, made + at[REST][:, part].astype(F32))

    loop_tiles(up_step)
    down_way.finish()
    up_way.finish()

    @pl.when(is_first)
    def _():
        stores[2].start()
        for i in range(N_TILES):
            away(i).wait()
        own.finish()


def middle_kernel(n_in, n_old, n_out, *refs):
    ins, outs, refs = split_refs(n_in, n_old, n_out, refs)
    dup_hbm, wide_in, wu_hbm, gain1, n1, r1, wo_hbm, ctx_hbm = ins
    at = dict(zip((DUP, WIDE, WU, N1, R1, WO, CTX, DBR, DCTX, DELTA, SUMS_B), refs))

    @pl.when(lax.axis_index(LAYER) == 0)
    def _():
        copies = Copies(at, refs[-1])
        parts = [pl.ds(i * at[DUP].shape[1] // 2, at[DUP].shape[1] // 2) for i in range(2)]

        def get_half(i):
            copies.load(DUP, dup_hbm.at[:, parts[i]], at[DUP].at[:, parts[i]])
            copies.load(WU, wu_hbm.at[0, :, parts[i]], at[WU].at[:, parts[i]])

        get_half(0)
        copies.load(WIDE, wide_in)
        at[SUMS_B][...] = jnp.zeros(at[SUMS_B].shape, F32)
        copies.ready(DUP, WU, WIDE)
        get_half(1)
        copies.load(N1, n1)
        copies.load(R1, r1)
        copies.load(WO, wo_hbm.at[0])
        copies.load(CTX, ctx_hbm)
        at[WIDE][...] += mm(at[DUP][:, parts[0]], at[WU][:, parts[0]], NT)
        copies.ready(DUP, WU)
        at[WIDE][...] += mm(at[DUP][:, parts[1]], at[WU][:, parts[1]], NT)
        copies.ready(N1, R1)
        first_norm_back(at, gain1, at[DBR], 0)
        for name, target in ((DBR, outs[0]), (WIDE, outs[1]), (SUMS_B, outs[4])):
            copies.store(at[name], target)
        copies.ready(WO, CTX)
        context_back(at, at[DBR][...], at[CTX][...])
        copies.store(at[DCTX], outs[2])
        copies.store(at[DELTA], outs[3])
        copies.finish()


ATTEND_READ = (QKV, DCTX, KID, QID, LSE, DELTA)
ATTEND_HELD = ATTEND_READ + (X, CTX, DBR, REST, WIDE, WQKV, DQKV, SUMS_C, DX)


def attend_kernel(n_in, n_old, n_out, *refs):
    ins, outs, refs = split_refs(n_in, n_old, n_out, refs)
    x_hbm, ctx_hbm, dbr_hbm, share, wide_hbm, wq, wk, wv = ins[len(ATTEND_READ) :]
    dqkv_out, sums_out, dx_out = outs[:3]
    at = dict(zip(ATTEND_HELD, refs))
    total, sems = refs[-2:]
    width = at[X].shape[1]
    is_first = lax.axis_index(LAYER) == 0
    copies = Copies(at, sems)
    own = Copies(at, sems)
    own.used = 6
    for name, source in zip(ATTEND_READ, ins):
        own.load(name, source, now=False)
    targets = ((DQKV, dqkv_out), (SUMS_C, sums_out), (DX, dx_out))
    stores = [own.store(at[name], target, now=False) for name, target in targets]
    late = Copies(at, sems)
    late.used = 16
    late.load(WIDE, wide_hbm, now=False)
    for i, weight in enumerate((wq, wk, wv)):
        late.load(WQKV, weight.at[0], at[WQKV].at[:, pl.ds(i * width, width)], now=False)
    other = Copies(at, sems)
    other.used = 22
    other.load(DQKV, dqkv_out, now=False)

    @pl.when(is_first)
    def _():
        own.go()
        own.ready(*ATTEND_READ)

    for name, source in ((X, x_hbm), (CTX, ctx_hbm), (DBR, dbr_hbm), (REST, share)):
        copies.load(name, source)

    @pl.when(is_first)
    def _():
        late.go()
        over_pairs(width, lambda j: attend_pair_back(j, width, at, at[DQKV], 0))
        for way in stores[:2]:
            way.start()

    @pl.when(jnp.logical_not(is_first))
    def _():
        other.go()
        other.ready(DQKV)

    copies.ready(X, CTX, DBR, REST)
    way_out = GradientOut(total, outs[3:], sems, 24, width, False)
    way_out.put(0, mm(at[CTX][...], at[DBR][...], TN) + at[REST][:, 0:width].astype(F32))

    def step(i, carry):
        made = mm(at[X][...], at[DQKV][:, lanes_at((i - 1) * width, width)], TN)
        way_out.put(i, made + at[REST][:, lanes_at(i * width, width)].astype(F32))
        return carry

    lax.fori_loop(1, N_TILES, step, 0)

    @pl.when(is_first)
    def _():
        late.ready(WIDE, WQKV)
        at[DX][...] = (at[WIDE][...] + mm(at[DQKV][...], at[WQKV][...], NT)).astype(BF16)
        stores[2].start()
        own.finish()

    way_out.finish()


def swap(array, stride):
    count = lax.axis_size(ROWS)
    return lax.ppermute(array, ROWS, [(d, d ^ stride) for d in range(count)])


def halves_kernel(jobs, n_in, n_old, n_out, *refs):
    ins, outs, refs = split_refs(n_in, n_old, n_out, refs)
    copies = Copies({}, refs[-1])
    buffers = [refs[3 * i : 3 * i + 3] for i in range(len(jobs))]
    for i, job in enumerate(jobs):
        sources, stride, before, after, start, size, keep = job[:7]
        own = (lax.axis_index(ROWS) // stride) % 2
        which = own if keep else 1 - own
        for k in range(before):
            taken = pl.ds((2 * k + which) * after, after)
            for source, buffer in zip(sources, buffers[i]):
                target = buffer.at[pl.ds(k * after, after)]
                copies.load(i, ins[source].at[taken, :, pl.ds(start, size)], target)
    for i, job in enumerate(jobs):
        left, right, total = buffers[i]
        copies.ready(i)
        total[...] = (left[...].astype(F32) + right[...].astype(F32)).astype(BF16)
        place, start = job[7:]
        copies.store(total, outs[place].at[:, :, pl.ds(start, total.shape[-1])])
    copies.finish()


def halves(ways, arrays, n_outs, keep):
    tall = arrays[0].shape[1]
    jobs, scratch = [], []
    outs = [None] * n_outs
    for sources, stride, before, after, start, size, place, column in ways:
        jobs.append((sources, stride, before, after, start, size, keep, place, column))
        scratch += [((before * after, tall, size), BF16)] * 3
        outs[place] = ((before * after, tall, column + size), BF16)
    inputs = [(array, ANY) for array in arrays]
    return call(partial(halves_kernel, tuple(jobs)), "halves", inputs, {}, outs, scratch, 32)


class ScatterSum:
    def __init__(self, kept, came, sent=None):
        self.kept, self.came, self.sent = kept, came, sent

    @staticmethod
    def cores(blocks):
        return ScatterSum(blocks[0], swap(blocks[1], 1))

    @staticmethod
    def exchange(ways, arrays, n_outs, strides, first):
        arrays = lax.optimization_barrier((arrays, first))[0]
        sent = halves(ways, arrays, n_outs, 0)
        came = tuple(swap(part, stride) for part, stride in zip(sent, strides))
        kept = halves(ways, lax.optimization_barrier((arrays, sent))[0], n_outs, 1)
        return ScatterSum(tuple(kept), came, sent)

    def second(self, first):
        half = self.kept.shape[-1] // 2
        ways = (((0, 1), 2, 4, 1, 0, half, 0, 0), ((0, 1), 4, 2, 2, half, half, 1, 0))
        return self.exchange(ways, (self.kept, self.came), 2, (2, 4), first)

    def pairs(self):
        return (self.kept[0], self.came[0], self.kept[1], self.came[1])

    def third(self, first):
        half = self.kept[0].shape[-1]
        ways = (((0, 1), 4, 2, 1, 0, half, 0, 0), ((2, 3), 2, 2, 1, 0, half, 1, 0))
        return self.exchange(ways, self.pairs(), 2, (4, 2), first)

    def fourth(self, first):
        half = self.kept[0].shape[-1]
        ways = tuple(((2 * i, 2 * i + 1), 8, 1, 1, 0, half, 0, i * half) for i in range(2))
        made = self.exchange(ways, self.pairs(), 1, (8,), first)
        return ScatterSum(made.kept[0], made.came[0], made.sent)

    def finish(self):
        return (self.kept.astype(F32) + self.came.astype(F32))[0]


def whole_sum(partial_sum):
    return lax.psum_scatter(partial_sum, ROWS, scatter_dimension=0, tiled=True).astype(F32)


def small_sum(values, beside, after):
    if lax.axis_size(ROWS) != 16:
        return lax.psum(values, ROWS)
    for stride, first in zip((1, 2, 4, 8), (*beside, None)):
        values = values + swap(values, stride)
        if first is not None:
            values = after(values, first)
    return values


def on_device(tokens, cotangent, segment_ids, valid_mask, cluster_perm, *params):
    section = lax.axis_index(LAYER)
    is_first = section == 0
    wq, _, wk, wv, _, wo, _, gain1, _, wu, _, wd, _, gain2, _ = params
    width, inner = wu.shape[1:]
    ids = (cluster_perm, segment_ids, valid_mask)
    shapes = shapes_of(width, inner)

    def hop(array, source, target):
        return lax.ppermute(array, LAYER, [(source, target)])

    def after(array, first):
        return lax.optimization_barrier((array, first))[0]

    row0, y0, stats00 = forward(0, 0, tokens, 0, ids, params, None)
    in0 = hop(y0, 0, 1)
    row1, y1, stats01 = forward(0, 1, tokens, 1, ids, params, None)
    in1 = hop(y1, 0, 1)
    row0, out0, stats10, grads0, dx0 = through_and_back(0, in0, cotangent, ids, params, row0)
    cotangent = after(cotangent, dx0)
    g0 = hop(dx0, 1, 0)
    row1, out1, stats11, grads1, dx1 = through_and_back(1, in1, cotangent, ids, params, row1)
    g0 = after(g0, dx1)
    g1 = hop(dx1, 1, 0)
    grads0, (dx0, down_share, up_share, rest_share) = backward(0, g0, 0, params, row0, grads0)
    g1 = after(g1, dx0)

    def at_hbm(*arrays):
        return [(array, ANY) for array in arrays]

    def of(*names):
        return [shapes[name] for name in names]

    totals, parts = gradient_shapes((inner, width), (width, inner))
    plain = len(totals) == 2
    made = call(
        feed_kernel,
        "feed",
        at_hbm(g1)
        + [(gain2, WHOLE)]
        + at_hbm(row1[N2], row1[R2], row1[ACT], down_share, wd, row1[GP], row1[HID], up_share),
        {0: grads1[DFFN], 1: grads1[DUP], 2: grads1[SUMS_A]},
        of(DFFN, DUP, SUMS_A, WIDE) + parts,
        of(G, N2, R2, WIDE, SUMS_A, ACT, DFFN, WD, GP, HID, DUP, WD, WU) + totals,
        60,
    )
    _, dup1, sums_a1, wide = made[:4]
    feed_parts = made[4:]
    if not plain:
        feed_sum = ScatterSum.cores(feed_parts)

    made = call(
        middle_kernel,
        "middle",
        at_hbm(dup1, wide, wu) + [(gain1, WHOLE)] + at_hbm(row1[N1], row1[R1], wo, row1[CTX]),
        {0: grads1[DBR], 4: grads1[SUMS_B]},
        of(DBR, WIDE, DCTX, DELTA, SUMS_B),
        of(DUP, WIDE, WU, N1, R1, WO, CTX, DBR, DCTX, DELTA, SUMS_B),
        20,
    )
    dbr1, wide, dctx, delta, sums_b1 = made
    if not plain:
        feed_sum = feed_sum.second(dctx)
        dctx = after(dctx, feed_sum.kept)

    totals, parts = gradient_shapes((width, 4 * width))
    made = call(
        attend_kernel,
        "attend",
        at_hbm(row1[QKV], dctx, *(row1[name] for name in (KID, QID, LSE)), delta)
        + at_hbm(row1[X], row1[CTX], dbr1, rest_share, wide, wq, wk, wv),
        {0: grads1[DQKV], 1: grads1[SUMS_C]},
        of(DQKV, SUMS_C, DX) + parts,
        of(*ATTEND_HELD) + totals,
        40,
    )
    _, sums_c1, dx1 = made[:3]
    came = []
    if plain:
        w_down, w_up, w_rest = (whole_sum(part) for part in (*feed_parts, made[3]))
        w_out, w_query, w_key, w_value = jnp.split(w_rest, 4, axis=1)
    else:
        feed_sum = feed_sum.third(dx1)
        rest_sum = ScatterSum.cores(after(tuple(made[3:]), feed_sum.sent))
        came.append(rest_sum.came)
        rest_sum = rest_sum.second(feed_sum.sent)
        dx1 = after(dx1, rest_sum.sent)
        came.append(rest_sum.came)
        feed_sum = feed_sum.fourth(rest_sum.sent)
        rest_sum = rest_sum.third(feed_sum.sent)
        came.append(rest_sum.came)
        rest_sum = rest_sum.fourth(rest_sum.sent)
        w_feed, w_rest = feed_sum.finish(), rest_sum.finish()
        tall = inner // 16
        w_down = w_feed[:tall]
        w_up = jnp.concatenate(jnp.split(w_feed[tall:], N_TILES, axis=0), axis=1)
        w_out, w_query, w_key, w_value = jnp.split(w_rest, 4, axis=0)

    sums_a1, sums_b1, sums_c1 = (after(array, dx1) for array in (sums_a1, sums_b1, sums_c1))
    stats10 = after(stats10, dx1)
    sum_a = (grads0[SUMS_A] + sums_a1).reshape(4, 8, inner).sum(axis=1)
    sum_b = (grads0[SUMS_B] + sums_b1).reshape(3, 8, width).sum(axis=1)
    sum_c = (grads0[SUMS_C] + sums_c1).reshape(2, 8, width).sum(axis=1)
    stats = jnp.where(is_first, stats00 + stats01, stats10 + stats11)
    stats = stats.reshape(3, 8 * width).sum(axis=1)
    count = jnp.sum(valid_mask.astype(F32))
    pieces = [sum_a[:3, :width].reshape(-1), sum_b.reshape(-1), sum_c.reshape(-1), sum_a[3]]
    base = 8 * width + inner
    spare = -(base + 4) % (8 * LANES)
    tail = jnp.concatenate([stats, jnp.broadcast_to(count, (1,)), jnp.zeros((spare,), F32)])
    small = jnp.concatenate(pieces + [tail]).reshape(-1, LANES)
    small = small_sum(small, came, after).reshape(-1)
    shares = lax.axis_size(ROWS)
    me = lax.axis_index(ROWS)

    def small_part(place, size):
        own = size // shares
        return lax.dynamic_slice_in_dim(small, place * width + me * own, own, 0)[None]

    gain2_sum, shift2_sum, down_bias, gain1_sum, shift1_sum, out_bias, query_bias, value_bias = (
        small_part(i, width) for i in range(8)
    )
    up_bias = small_part(8, inner)
    root_means = jnp.sqrt(small[base : base + 3] / (small[base + 3] * width))[None, :]

    half = width // 2
    dx0, out0, out1 = (after(array, dx1) for array in (dx0, out0, out1))
    outgoing = jnp.concatenate(
        [
            jnp.where(is_first, grad[:, half:], made[:, :half])
            for grad, made in ((dx0, out0), (dx1, out1))
        ]
    )
    arrived = lax.ppermute(outgoing, LAYER, [(0, 1), (1, 0)])
    block_own = jnp.concatenate([out0[:, half:], out1[:, half:]])
    grad_own = jnp.concatenate([dx0[:, :half], dx1[:, :half]])
    block_part = jnp.where(is_first, arrived, block_own)
    grad_part = jnp.where(is_first, grad_own, arrived)
    return (
        block_part,
        grad_part,
        w_query[None],
        query_bias,
        w_key[None],
        w_value[None],
        value_bias,
        w_out[None],
        out_bias,
        gain1_sum,
        shift1_sum,
        w_up[None],
        up_bias,
        w_down[None],
        down_bias,
        gain2_sum,
        shift2_sum,
        root_means,
    )


def solution(mesh):
    by_layer = P(LAYER, None)
    matrix = P(LAYER, None, None)
    share = P(LAYER, ROWS)
    matrix_share = P(LAYER, ROWS, None)
    rows = P(ROWS, None)
    vectors = {1, 4, 6, 7, 8, 10, 12, 13, 14}
    matrices = {2, 4, 5, 7, 11, 13}
    return jax.shard_map(
        on_device,
        mesh=mesh,
        in_specs=(rows, rows, rows, rows, P(LAYER, ROWS, None, None))
        + tuple(by_layer if i in vectors else matrix for i in range(15)),
        out_specs=(P(ROWS, LAYER), P(ROWS, LAYER))
        + tuple(matrix_share if i in matrices else share for i in range(2, 17))
        + (P(LAYER, None),),
        check_vma=False,
    )
```

```python
from functools import partial

import jax
import jax.numpy as jnp
from jax import lax
from jax.experimental import pallas as pl
from jax.experimental.pallas import tpu as pltpu
from jax.sharding import PartitionSpec as P

HEAD_DIM = 64
CLUSTER = 128
SEQ = 512
LANES = 128
ROW_BLOCK = 512
PAIR_UNROLL = 3
MIB = 1024 * 1024

BF16 = jnp.bfloat16
F32 = jnp.float32
LOG2E = 1.4426950408889634
SCALE = HEAD_DIM**-0.5
SCORE_SCALE = SCALE * LOG2E

NN = ((1,), (0,))
NT = ((1,), (1,))
TN = ((0,), (0,))

ROWS = "dp"
LAYER = "section"
ANY = pl.BlockSpec(memory_space=pltpu.HBM)
FREE = pl.BlockSpec(memory_space=pl.ANY)
WHOLE = pl.BlockSpec(memory_space=pltpu.VMEM)
SHORT = pl.CostEstimate(flops=1, bytes_accessed=1, transcendentals=0)

X, QKV, CTX, LSE, KID, QID, N1, R1, HID, ACT, GP, N2, R2 = range(13)
G, DFFN, DUP, DBR, DQKV, SUMS_A, SUMS_B, SUMS_C, WIDE, DCTX, DELTA, DX, FEED, LIVE = range(13, 27)
BIAS, WQKV, Y, STATS, WO, WU, WD, REST = range(27, 35)
SAVED = (X, QKV, CTX, LSE, KID, QID, N1, R1, HID, ACT, GP, N2, R2)
GRADS = (DFFN, DUP, DBR, DQKV, SUMS_A, SUMS_B, SUMS_C)
GAIN2, SHIFT2, B_DOWN, B_UP = 0, 8, 16, 24
GAIN1, SHIFT1, B_OUT = 0, 8, 16
B_QUERY, B_VALUE = 0, 8


def shapes_of(width, inner):
    token, token32, narrow = ((SEQ, width), BF16), ((SEQ, width), F32), ((SEQ, LANES), F32)
    heads = ((16, SEQ), F32)
    shapes = {name: token for name in (X, CTX, N1, HID, N2, G, DFFN, DBR, DCTX, DX, Y)}
    shapes.update({name: token32 for name in (KID, WIDE, FEED)})
    shapes.update({name: narrow for name in (R1, R2, LIVE)})
    shapes.update({name: heads for name in (LSE, QID, DELTA)})
    shapes.update({name: ((SEQ, inner), BF16) for name in (ACT, GP, DUP)})
    shapes.update({name: ((SEQ, 3 * width), BF16) for name in (QKV, DQKV)})
    shapes.update({SUMS_A: ((32, inner), F32), SUMS_B: ((24, width), F32)})
    shapes.update({SUMS_C: ((16, width), F32), STATS: ((24, width), F32), BIAS: ((8, width), F32)})
    shapes.update({WQKV: ((width, 3 * width), BF16), WO: ((width, width), BF16)})
    shapes.update({WU: ((width, inner), BF16), WD: ((inner, width), BF16)})
    shapes[REST] = ((width, 4 * width), BF16)
    return shapes


def mm(left, right, dims):
    return lax.dot_general(left, right, (dims, ((), ())), preferred_element_type=F32)


def vec(ref):
    return ref[0:1, :].astype(F32)


def lanes_at(start, size=LANES):
    return pl.ds(pl.multiple_of(start, LANES), size)


def fold8(block):
    return jnp.sum(block.reshape(-1, 8, block.shape[-1]), axis=0)


def over_rows(step):
    def body(i, carry):
        step(pl.ds(pl.multiple_of(i * ROW_BLOCK, ROW_BLOCK), ROW_BLOCK))
        return carry

    lax.fori_loop(0, SEQ // ROW_BLOCK, body, 0)


def over_tiles(size, tile, step):
    def body(i, carry):
        step(pl.ds(pl.multiple_of(i * tile, tile), tile))
        return carry

    lax.fori_loop(0, size // tile, body, 0)


class Copies:
    def __init__(self, at, sems):
        self.at, self.sems = at, sems
        self.used = 0
        self.loads = {}
        self.stores = []

    def plan(self, source, target):
        self.used += 1
        return pltpu.make_async_copy(source, target, self.sems.at[self.used - 1])

    def load(self, name, source, target=None, now=True):
        target = self.at[name] if target is None else target
        copy = self.plan(source, target)
        self.loads.setdefault(name, []).append(copy)
        if now:
            copy.start()

    def go(self):
        for copies in self.loads.values():
            for copy in copies:
                copy.start()

    def ready(self, *names):
        for name in names:
            for copy in self.loads.pop(name, ()):
                copy.wait()

    def store(self, source, target, now=True):
        copy = self.plan(source, target)
        self.stores.append(copy)
        if now:
            copy.start()
        return copy

    def finish(self):
        for copy in self.stores:
            copy.wait()


def load_qkv(copies, weights, width):
    for i, weight in enumerate(weights):
        copies.load(WQKV, weight.at[0], copies.at[WQKV].at[:, pl.ds(i * width, width)])


def call(body, name, inputs, old, outs, scratch, n_sems, vmem=58):
    arrays = [array for array, _ in inputs]
    n_in = len(arrays)
    return pl.pallas_call(
        partial(body, n_in, len(old), len(outs)),
        out_shape=[jax.ShapeDtypeStruct(*shape) for shape in outs],
        in_specs=[spec for _, spec in inputs] + [ANY] * len(old),
        out_specs=[ANY] * len(outs),
        input_output_aliases={n_in + i: place for i, place in enumerate(old)},
        scratch_shapes=[pltpu.VMEM(*shape) for shape in scratch]
        + [pltpu.SemaphoreType.DMA((n_sems,))],
        compiler_params=pltpu.CompilerParams(vmem_limit_bytes=vmem * MIB),
        cost_estimate=SHORT,
        name=name,
    )(*arrays, *old.values())


def split_refs(n_in, n_old, n_out, refs):
    return refs[:n_in], refs[n_in + n_old : n_in + n_old + n_out], refs[n_in + n_old + n_out :]


def low_lanes():
    return lax.broadcasted_iota(jnp.int32, (SEQ, LANES), 1) < HEAD_DIM


def masked(scores, kid_column, qid_row):
    shape = (CLUSTER, CLUSTER)
    same = lax.broadcasted_iota(jnp.int32, shape, 0) == lax.broadcasted_iota(jnp.int32, shape, 1)
    count = SEQ // CLUSTER
    parts = [slice(i * CLUSTER, (i + 1) * CLUSTER) for i in range(count)]
    rows = []
    for i in range(count):
        tiles = []
        for j in range(count):
            ok = kid_column[parts[i]] == qid_row[:, parts[j]]
            if i == j:
                ok = ok | same
            tiles.append(jnp.where(ok, scores[parts[i], parts[j]], -1e30))
        rows.append(jnp.concatenate(tiles, axis=1))
    return jnp.concatenate(rows, axis=0)


def attend_pair(j, width, at):
    low = low_lanes()
    lanes = lanes_at(j * LANES)
    query = at[QKV][:, lanes]
    key = at[QKV][:, lanes_at(width + j * LANES)]
    value = at[QKV][:, lanes_at(2 * width + j * LANES)]
    kid_pair = at[KID][:, lanes]
    mixed, tops = [], []
    for half in (0, 1):
        own = low if half == 0 else ~low
        own_query = jnp.where(own, query, jnp.zeros_like(query))
        value_ones = jnp.where(own, value, jnp.ones_like(value))
        kid_column = kid_pair[:, half * HEAD_DIM : half * HEAD_DIM + 1]
        scores = mm(key, own_query, NT) * SCORE_SCALE
        scores = masked(scores, kid_column, at[QID][pl.ds(2 * j + half, 1), :])
        top = jnp.max(scores, axis=0, keepdims=True)
        tops.append(top)
        mixed.append(mm(jnp.exp2(scores - top).astype(BF16), value_ones, TN))
    sums = [pltpu.roll(part, HEAD_DIM, 1) for part in mixed]
    total = jnp.where(low, sums[0], sums[1])
    at[CTX][:, lanes] = (jnp.where(low, mixed[0], mixed[1]) / total).astype(BF16)
    turned = total.T
    for half in (0, 1):
        row = turned[half * HEAD_DIM : half * HEAD_DIM + 1, :]
        at[LSE][pl.ds(2 * j + half, 1), :] = tops[half] + jnp.log2(row)


def attend_pair_back(j, width, at, target, base):
    low = low_lanes()
    lanes = [lanes_at(i * width + j * LANES) for i in range(3)]
    query, key, value = (at[QKV][:, part] for part in lanes)
    d_out = at[DCTX][:, lanes[0]]
    kid_pair = at[KID][:, lanes[0]]
    d_query, d_key, d_value = [], [], []
    for half in (0, 1):
        h = pl.ds(2 * j + half, 1)
        own = low if half == 0 else ~low
        own_query = jnp.where(own, query, jnp.zeros_like(query))
        own_out = jnp.where(own, d_out, jnp.zeros_like(d_out))
        kid_column = kid_pair[:, half * HEAD_DIM : half * HEAD_DIM + 1]
        scores = mm(key, own_query, NT) * SCORE_SCALE - at[LSE][h, :]
        weights = jnp.exp2(masked(scores, kid_column, at[QID][h, :]))
        d_weights = mm(value, own_out, NT)
        d_scores = (weights * (d_weights - at[DELTA][h, :])).astype(BF16)
        d_value.append(mm(weights.astype(BF16), own_out, NN))
        d_key.append(mm(d_scores, own_query, NN))
        d_query.append(mm(d_scores, key, TN))
    made = (
        jnp.where(low, d_query[0], d_query[1]) * SCALE,
        (d_key[0] + d_key[1]) * SCALE,
        d_value[0] + d_value[1],
    )
    rows = pl.ds(base, SEQ)
    for i, place in ((0, B_QUERY), (1, None), (2, B_VALUE)):
        rounded = made[i].astype(BF16)
        target[rows, lanes[i]] = rounded
        if place is not None:
            at[SUMS_C][place : place + 8, lanes[0]] = fold8(rounded.astype(F32))


def over_pairs(width, step):
    def body(j, carry):
        step(j)
        return carry

    lax.fori_loop(0, width // LANES, body, 0, unroll=PAIR_UNROLL)


def token_ids(row, heads, perm_ref, seg_ref, valid_ref, kid_ref, qid_ref):
    token = lax.broadcasted_iota(jnp.int32, (SEQ, LANES), 0)
    lane = lax.broadcasted_iota(jnp.int32, (SEQ, LANES), 1)
    seg_row = seg_ref[row : row + 1, :].astype(F32)
    valid_row = valid_ref[row : row + 1, :].astype(F32)
    at = lax.broadcasted_iota(jnp.int32, (LANES, SEQ), 0)
    both = jnp.where(at == 0, seg_row, jnp.where(at == 1, valid_row, 0.0)).T
    segment, live = both[:, 0:1], both[:, 1:2]

    def column(h):
        places = perm_ref[0, row, pl.ds(h, 1), :]
        mine = jnp.zeros((SEQ, LANES), F32)
        for c in range(1, SEQ // CLUSTER):
            part = places[:, c * CLUSTER : (c + 1) * CLUSTER]
            mine = jnp.where(token == part, float(c), mine)
        return jnp.sum(mine, axis=1, keepdims=True) * 4.0 + segment

    def pair(j, ids):
        left, right = column(2 * j), column(2 * j + 1)
        own = jnp.where(lane < HEAD_DIM, left, right)
        kid_ref[:, lanes_at(j * LANES)] = jnp.where(live > 0.5, own, -1.0)
        ids = jnp.where(lane == 2 * j, left, ids)
        return jnp.where(lane == 2 * j + 1, right, ids)

    qid = lax.fori_loop(0, heads // 2, pair, jnp.zeros((SEQ, LANES), F32))
    qid_ref[...] = qid.T[0:16, :]
    return live


def normed(total):
    centre = total - jnp.mean(total, axis=-1, keepdims=True)
    spread = jnp.mean(centre * centre, axis=-1, keepdims=True)
    rate = lax.rsqrt(spread + 1e-05)
    return centre * rate, rate


FORWARD_HELD = SAVED + (WQKV, WO, WU, WD, WIDE, FEED, Y, STATS, LIVE, BIAS)


def run_forward(at, copies, save, row, source, ids, params, later=None):
    perm_ref, seg_ref, valid_ref = ids
    wq, bq, wk, wv, bv, wo, bo, g1, s1, wu, bu, wd, bd, g2, s2 = params
    width, inner = at[WU].shape
    heads = width // HEAD_DIM
    copies.load(X, source)
    first = copies.used
    load_qkv(copies, (wq, wk, wv), width)
    live = token_ids(row, heads, perm_ref, seg_ref, valid_ref, at[KID], at[QID])
    at[LIVE][...] = jnp.broadcast_to(live, (SEQ, LANES))
    at[LSE][...] = jnp.zeros((16, SEQ), F32)
    at[STATS][...] = jnp.zeros((24, width), F32)
    at[BIAS][0:1, :] = vec(bq)
    at[BIAS][1:2, :] = jnp.zeros((1, width), F32)
    at[BIAS][2:3, :] = vec(bv)
    copies.ready(X)

    def to_qkv(i, carry):
        part = pl.ds(pl.multiple_of(i * width, LANES), width)
        weight = at[WQKV].at[:, part]
        pltpu.make_async_copy(weight, weight, copies.sems.at[first + i]).wait()
        made = mm(at[X][...], at[WQKV][:, part], NN) + at[BIAS][pl.ds(i, 1), :]
        at[QKV][:, part] = made.astype(BF16)
        return carry

    lax.fori_loop(0, 3, to_qkv, 0)
    copies.loads.pop(WQKV)
    copies.load(WO, wo.at[0])
    copies.load(WU, wu.at[0])
    copies.load(WD, wd.at[0])
    if later is not None:
        later()
    save(KID, QID, X, QKV)
    over_pairs(width, lambda j: attend_pair(j, width, at))
    save(LSE, CTX)
    copies.ready(WO)
    at[WIDE][...] = mm(at[CTX][...], at[WO][...], NN)

    def first_norm(rows):
        branch = at[WIDE][rows, :] + vec(bo)
        alive = at[LIVE][rows, 0:1]
        at[STATS][0:8, :] += fold8(branch * branch * alive)
        unit, rate = normed(at[X][rows, :].astype(F32) + branch)
        hidden = unit * vec(g1) + vec(s1)
        at[N1][rows, :] = unit.astype(BF16)
        at[R1][rows, :] = jnp.broadcast_to(rate, (ROW_BLOCK, LANES))
        at[HID][rows, :] = hidden.astype(BF16)
        at[WIDE][rows, :] = hidden

    over_rows(first_norm)
    save(N1, R1, HID)
    copies.ready(WU)

    def up(part):
        upper = mm(at[HID][...], at[WU][:, part], NN) + bu[0:1, part].astype(F32)
        half = 0.5 + 0.5 * lax.erf(upper * 0.5**0.5)
        bell = jnp.exp2(upper * upper * (-0.5 * LOG2E)) * 0.3989422804014327
        at[ACT][:, part] = (upper * half).astype(BF16)
        at[GP][:, part] = (half + upper * bell).astype(BF16)

    over_tiles(inner, inner // 2, up)
    save(ACT, GP)
    copies.ready(WD)
    at[FEED][...] = mm(at[ACT][...], at[WD][...], NN)

    def second_norm(rows):
        ffn = at[FEED][rows, :] + vec(bd)
        alive = at[LIVE][rows, 0:1]
        at[STATS][8:16, :] += fold8(ffn * ffn * alive)
        unit, rate = normed(at[WIDE][rows, :] + ffn)
        result = unit * vec(g2) + vec(s2)
        at[STATS][16:24, :] += fold8(result * result * alive)
        at[N2][rows, :] = unit.astype(BF16)
        at[R2][rows, :] = jnp.broadcast_to(rate, (ROW_BLOCK, LANES))
        at[Y][rows, :] = result.astype(BF16)

    over_rows(second_norm)
    save(Y, STATS, N2, R2)


def forward_kernel(section, row, x_row, n_in, n_old, n_out, *refs):
    ins, outs, refs = split_refs(n_in, n_old, n_out, refs)
    out = dict(zip(SAVED + (Y, STATS), outs))
    at = dict(zip(FORWARD_HELD, refs))

    @pl.when(lax.axis_index(LAYER) == section)
    def _():
        copies = Copies(at, refs[-1])

        def save(*names):
            for name in names:
                copies.store(at[name], out[name])

        source = ins[0].at[pl.ds(x_row * SEQ, SEQ), :]
        run_forward(at, copies, save, row, source, ins[1:4], ins[4:])
        copies.finish()


def forward(section, row, x, x_row, ids, params, kept):
    width, inner = params[9].shape[1:]
    shapes = shapes_of(width, inner)
    inputs = [(x, ANY)] + [(array, WHOLE) for array in ids]
    inputs += [(array, ANY if array.ndim == 3 else WHOLE) for array in params]
    made = call(
        partial(forward_kernel, section, row, x_row),
        "forward",
        inputs,
        {} if kept is None else {i: kept[name] for i, name in enumerate(SAVED)},
        [shapes[name] for name in SAVED + (Y, STATS)],
        [shapes[name] for name in FORWARD_HELD],
        32,
    )
    return dict(zip(SAVED, made)), made[-2], made[-1]


def norm_back(grad, unit, rate, gain):
    scaled = grad * gain
    mean = jnp.mean(scaled, axis=-1, keepdims=True)
    along = jnp.mean(scaled * unit, axis=-1, keepdims=True)
    return (scaled - mean - unit * along) * rate


def add_sum(ref, place, value):
    ref[place : place + 8, 0 : value.shape[-1]] += fold8(value)


def second_norm_back(at, gain2, target, base):
    def step(rows):
        grad = at[G][rows, :].astype(F32)
        unit = at[N2][rows, :].astype(F32)
        add_sum(at[SUMS_A], GAIN2, grad * unit)
        add_sum(at[SUMS_A], SHIFT2, grad)
        d_second = norm_back(grad, unit, at[R2][rows, 0:1], vec(gain2))
        at[WIDE][rows, :] = d_second
        low = d_second.astype(BF16)
        target[pl.ds(pl.multiple_of(rows.start + base, ROW_BLOCK), ROW_BLOCK), :] = low
        add_sum(at[SUMS_A], B_DOWN, low.astype(F32))

    over_rows(step)


def up_back(at, dffn, part):
    d_act = mm(dffn, at[WD][part, :], NT)
    low = (d_act * at[GP][:, part].astype(F32)).astype(BF16)
    at[SUMS_A][B_UP : B_UP + 8, part] += fold8(low.astype(F32))
    return low


def first_norm_back(at, gain1, target, base):
    def step(rows):
        grad = at[WIDE][rows, :]
        unit = at[N1][rows, :].astype(F32)
        add_sum(at[SUMS_B], GAIN1, grad * unit)
        add_sum(at[SUMS_B], SHIFT1, grad)
        d_first = norm_back(grad, unit, at[R1][rows, 0:1], vec(gain1))
        at[WIDE][rows, :] = d_first
        low = d_first.astype(BF16)
        target[pl.ds(pl.multiple_of(rows.start + base, ROW_BLOCK), ROW_BLOCK), :] = low
        add_sum(at[SUMS_B], B_OUT, low.astype(F32))

    over_rows(step)


def context_back(at, dbr, context):
    width = dbr.shape[1]
    d_context = mm(dbr, at[WO][...], NT).astype(BF16)
    at[DCTX][...] = d_context
    product = d_context.astype(F32) * context.astype(F32)
    high = product.astype(BF16)
    rest = (product - high.astype(F32)).astype(BF16)
    of_head = (
        lax.broadcasted_iota(jnp.int32, (16, width), 1) // HEAD_DIM
        == lax.broadcasted_iota(jnp.int32, (16, width), 0)
    )
    pick = jnp.where(of_head, 1.0, 0.0).astype(BF16)
    at[DELTA][...] = mm(pick, high, NT) + mm(pick, rest, NT)


def run_backward(at, copies, get, save, params, shared):
    gain1, gain2 = params[:2]
    width, inner = at[WU].shape
    get(G, N2, R2)
    for name in (SUMS_A, SUMS_B):
        at[name][...] = jnp.zeros(at[name].shape, F32)
    copies.ready(G, N2, R2)
    get(WD, GP)
    second_norm_back(at, gain2, at[DFFN], 0)
    save(DFFN)
    get(WU, N1, R1, WO, CTX)
    copies.ready(WD, GP)

    def up(part):
        at[DUP][:, part] = up_back(at, at[DFFN][...], part)

    over_tiles(inner, inner // 2, up)
    save(DUP, SUMS_A)
    get(QKV, KID, QID, LSE, WQKV)
    copies.ready(WU)
    at[WIDE][...] += mm(at[DUP][...], at[WU][...], NT)
    copies.ready(N1, R1)
    first_norm_back(at, gain1, at[DBR], 0)
    save(DBR, SUMS_B)
    copies.ready(WO, CTX)
    context_back(at, at[DBR][...], at[CTX][...])
    copies.ready(QKV, KID, QID, LSE)
    if shared is not None:
        shared.go()
    over_pairs(width, lambda j: attend_pair_back(j, width, at, at[DQKV], 0))
    save(DQKV, SUMS_C)
    copies.ready(WQKV)
    at[DX][...] = (at[WIDE][...] + mm(at[DQKV][...], at[WQKV][...], NT)).astype(BF16)
    save(DX)


BACK_READ = (N2, R2, GP, N1, R1, CTX, LSE, KID, QID, QKV)
SHARE_READ = (ACT, HID, X)
BACK_HELD = (G,) + BACK_READ + GRADS + (WIDE, DCTX, DELTA, DX, WQKV, WO, WU, WD)


def backward_kernel(section, g_row, n_in, n_old, n_out, *refs):
    ins, outs, refs = split_refs(n_in, n_old, n_out, refs)
    g_hbm, gain1, gain2, wq, wk, wv, wo, wu, wd = ins[:9]
    given = dict(zip(BACK_READ + SHARE_READ, ins[9:]))
    given.update({WO: wo.at[0], WU: wu.at[0], WD: wd.at[0]})
    given[G] = g_hbm.at[pl.ds(g_row * SEQ, SEQ), :]
    with_shares = section == 0
    out = dict(zip(GRADS + (DX,), outs))
    at = dict(zip(BACK_HELD + (SHARE_READ if with_shares else ()), refs))
    width, inner = at[WU].shape
    shared = Copies(at, refs[-1])
    shared.used = 40
    if with_shares:
        for name in SHARE_READ:
            shared.load(name, given[name], now=False)

        @pl.when(lax.axis_index(LAYER) != section)
        def _():
            others = Copies(at, refs[-1])
            others.used = 50
            for name in (DFFN, DUP, DBR, DQKV):
                others.load(name, out[name])
            others.load(CTX, given[CTX])
            shared.go()
            others.ready(DFFN, DUP, DBR, DQKV, CTX)

    @pl.when(lax.axis_index(LAYER) == section)
    def _():
        copies = Copies(at, refs[-1])

        def get(*names):
            for name in names:
                if name == WQKV:
                    load_qkv(copies, (wq, wk, wv), width)
                else:
                    copies.load(name, given[name])

        def save(*names):
            for name in names:
                copies.store(at[name], out[name])

        run_backward(at, copies, get, save, ins[1:3], shared if with_shares else None)
        copies.finish()

    if not with_shares:
        return
    down, up, rest = at[WD], at[WU], refs[-2]
    shared.ready(*SHARE_READ)

    def to_down(part):
        down[part, :] = mm(at[ACT][:, part], at[DFFN][...], TN).astype(BF16)

    over_tiles(inner, width, to_down)
    shared.store(down, outs[-3])

    def to_up(part):
        up[:, part] = mm(at[HID][...], at[DUP][:, part], TN).astype(BF16)

    over_tiles(inner, width, to_up)
    shared.store(up, outs[-2])
    rest[:, 0:width] = mm(at[CTX][...], at[DBR][...], TN).astype(BF16)

    def to_rest(i, carry):
        made = mm(at[X][...], at[DQKV][:, lanes_at(i * width - width, width)], TN)
        rest[:, lanes_at(i * width, width)] = made.astype(BF16)
        return carry

    lax.fori_loop(1, 4, to_rest, 0)
    shared.store(rest, outs[-1])
    shared.finish()


def backward(section, g, g_row, params, kept, old):
    wq, _, wk, wv, _, wo, _, gain1, _, wu, _, wd, _, gain2, _ = params
    shapes = shapes_of(*wu.shape[1:])
    inputs = [(g, ANY), (gain1, WHOLE), (gain2, WHOLE)]
    inputs += [(array, ANY) for array in (wq, wk, wv, wo, wu, wd)]
    inputs += [(kept[name], ANY) for name in BACK_READ]
    outs, held = list(GRADS + (DX,)), list(BACK_HELD)
    if section == 0:
        inputs += [(kept[name], ANY) for name in SHARE_READ]
        outs += [WD, WU, REST]
        held += SHARE_READ + (REST,)
    made = call(
        partial(backward_kernel, section, g_row),
        "backward",
        inputs,
        {} if old is None else {i: old[name] for i, name in enumerate(GRADS)},
        [shapes[name] for name in outs],
        [shapes[name] for name in held],
        56,
    )
    return dict(zip(GRADS, made)), made[len(GRADS) :]


KEPT = (X, CTX, HID, ACT)
BOTH_HELD = FORWARD_HELD + (G,) + GRADS + (DCTX, DELTA, DX)


def both_kernel(row, n_in, n_old, n_out, *refs):
    ins, outs, refs = split_refs(n_in, n_old, n_out, refs)
    out = dict(zip(KEPT + (Y, STATS) + GRADS + (DX,), outs))
    at = dict(zip(BOTH_HELD, refs))
    params = ins[5:]

    @pl.when(lax.axis_index(LAYER) == 1)
    def _():
        copies = Copies(at, refs[-1])

        def save(*names):
            for name in names:
                if name in out:
                    copies.store(at[name], out[name])

        def get(*names):
            pass

        def later():
            copies.load(G, ins[1].at[pl.ds(row * SEQ, SEQ), :])

        run_forward(at, copies, save, row, ins[0], ins[2:5], params, later)
        run_backward(at, copies, get, save, (params[7], params[13]), None)
        copies.finish()


def through_and_back(row, x, g, ids, params, kept):
    shapes = shapes_of(*params[9].shape[1:])
    inputs = [(x, ANY), (g, ANY)] + [(array, WHOLE) for array in ids]
    inputs += [(array, ANY if array.ndim == 3 else WHOLE) for array in params]
    names = KEPT + (Y, STATS) + GRADS + (DX,)
    made = call(
        partial(both_kernel, row),
        "both",
        inputs,
        {i: kept[name] for i, name in enumerate(KEPT)},
        [shapes[name] for name in names],
        [shapes[name] for name in BOTH_HELD],
        48,
    )
    made = dict(zip(names, made))
    kept = {**kept, **{name: made[name] for name in KEPT}}
    return kept, made[Y], made[STATS], {name: made[name] for name in GRADS}, made[DX]


N_TILES = 4


def gradient_shapes(*sizes):
    count = lax.axis_size(ROWS)
    if count != 16:
        shapes = [(size, BF16) for size in sizes]
        return shapes, shapes
    tall = sum(rows * columns for rows, columns in sizes) // (count * min(map(min, sizes)))
    width = min(map(min, sizes))
    return [((8, 2, tall, width), BF16)], [((8, tall, width), BF16)] * 2


class GradientOut:
    def __init__(self, ref, targets, sems, first_sem, tile, by_rows, base=0):
        self.ref, self.targets, self.sems, self.first_sem = ref, targets, sems, first_sem
        self.tile, self.by_rows, self.base = tile, by_rows, base
        self.plain = len(targets) == 1
        self.tall = tile // 4 if by_rows else tile // 16

    def at(self, i):
        start = i * self.tile
        if self.plain and self.by_rows:
            return (pl.ds(pl.multiple_of(start, 16), self.tile),)
        if self.plain:
            return (slice(None), lanes_at(start, self.tile))
        if self.by_rows:
            return (pl.ds(2 * i, 2), pl.ds(self.base, self.tall))
        return (slice(None), pl.ds(pl.multiple_of(self.base + i * self.tall, 16), self.tall))

    def moves(self, i):
        at = self.at(i)
        if self.plain:
            pairs = [(self.ref.at[at], self.targets[0].at[at])]
        else:
            core = lax.axis_index(ROWS) % 2
            pairs = [
                (self.ref.at[at[0], which, at[1]], target.at[at])
                for target, which in zip(self.targets, (core, 1 - core))
            ]
        base = self.first_sem + i * len(pairs)
        return [
            pltpu.make_async_copy(source, target, self.sems.at[base + k])
            for k, (source, target) in enumerate(pairs)
        ]

    def put(self, i, value):
        value = value.astype(BF16)
        at = self.at(i)
        if self.plain:
            self.ref[at] = value
        else:
            split = value.reshape(-1, 2, self.tall, value.shape[1])
            self.ref[at[0], :, at[1], :] = split
        for move in self.moves(i):
            move.start()

    def finish(self):
        for i in range(N_TILES):
            for move in self.moves(i):
                move.wait()


def loop_tiles(step):
    def body(i, carry):
        step(i)
        return carry

    lax.fori_loop(0, N_TILES, body, 0)


FEED_HELD = (G, N2, R2, WIDE, SUMS_A, ACT, DFFN, WD, GP, HID, DUP, FEED, REST)


def feed_kernel(n_in, n_old, n_out, *refs):
    ins, outs, refs = split_refs(n_in, n_old, n_out, refs)
    g_hbm, gain2, n2, r2, act_hbm, down_share, wd_hbm, gp_hbm, hid_hbm, up_share = ins
    dffn_out, dup_out, sums_out, wide_out = outs[:4]
    at = dict(zip(FEED_HELD, refs))
    totals, sems = refs[len(FEED_HELD) : -1], refs[-1]
    inner, width = at[WD].shape
    tile = inner // N_TILES
    if len(totals) == 1:
        ways = [(totals[0], outs[4:]), (totals[0], outs[4:])]
    else:
        ways = [(total, [target]) for total, target in zip(totals, outs[4:])]
    down_way = GradientOut(*ways[0], sems, 40, tile, True)
    up_way = GradientOut(*ways[1], sems, 50, tile, False, tile // 4)
    is_first = lax.axis_index(LAYER) == 0
    copies = Copies(at, sems)
    own = Copies(at, sems)
    own.used = 4
    for name, source in ((G, g_hbm), (N2, n2), (R2, r2)):
        own.load(name, source, now=False)
    targets = ((DFFN, dffn_out), (WIDE, wide_out), (SUMS_A, sums_out))
    stores = [own.store(at[name], target, now=False) for name, target in targets]
    other = Copies(at, sems)
    other.used = 12
    other.load(DFFN, dffn_out, now=False)
    other.load(DUP, dup_out, now=False)

    def fetch(i):
        part = lanes_at(i * tile, tile)
        pairs = (
            (up_share.at[:, part], at[REST].at[:, part]),
            (wd_hbm.at[0, part, :], at[WD].at[part, :]),
            (gp_hbm.at[:, part], at[GP].at[:, part]),
        )
        return [
            pltpu.make_async_copy(source, target, sems.at[16 + 3 * i + k])
            for k, (source, target) in enumerate(pairs)
        ]

    def fetch_start(i):
        fetch(i)[0].start()

        @pl.when(is_first)
        def _():
            for move in fetch(i)[1:]:
                move.start()

    def away(i):
        part = lanes_at(i * tile, tile)
        return pltpu.make_async_copy(at[DUP].at[:, part], dup_out.at[:, part], sems.at[32 + i])

    @pl.when(is_first)
    def _():
        own.go()

    copies.load(ACT, act_hbm)
    copies.load(FEED, down_share)

    @pl.when(is_first)
    def _():
        at[SUMS_A][...] = jnp.zeros(at[SUMS_A].shape, F32)
        own.ready(G, N2, R2)

    copies.load(HID, hid_hbm)
    fetch_start(0)

    @pl.when(is_first)
    def _():
        second_norm_back(at, gain2, at[DFFN], 0)
        for way in stores[:2]:
            way.start()

    @pl.when(jnp.logical_not(is_first))
    def _():
        other.go()
        other.ready(DFFN, DUP)

    copies.ready(ACT, FEED)
    fetch_start(1)

    def down_step(i):
        part = lanes_at(i * tile, tile)
        made = mm(at[ACT][:, part], at[DFFN][...], TN)
        down_way.put(i, made + at[FEED][part, :].astype(F32))

    loop_tiles(down_step)
    fetch_start(2)
    fetch_start(3)
    copies.ready(HID)

    def up_step(i):
        part = lanes_at(i * tile, tile)

        @pl.when(is_first)
        def _():
            for move in fetch(i)[1:]:
                move.wait()
            at[DUP][:, part] = up_back(at, at[DFFN][...], part)
            away(i).start()

        fetch(i)[0].wait()
        made = mm(at[HID][...], at[DUP][:, part], TN)
        up_way.put(i, made + at[REST][:, part].astype(F32))

    loop_tiles(up_step)
    down_way.finish()
    up_way.finish()

    @pl.when(is_first)
    def _():
        stores[2].start()
        for i in range(N_TILES):
            away(i).wait()
        own.finish()


def middle_kernel(n_in, n_old, n_out, *refs):
    ins, outs, refs = split_refs(n_in, n_old, n_out, refs)
    dup_hbm, wide_in, wu_hbm, gain1, n1, r1, wo_hbm, ctx_hbm = ins
    at = dict(zip((DUP, WIDE, WU, N1, R1, WO, CTX, DBR, DCTX, DELTA, SUMS_B), refs))

    @pl.when(lax.axis_index(LAYER) == 0)
    def _():
        copies = Copies(at, refs[-1])
        parts = [pl.ds(i * at[DUP].shape[1] // 2, at[DUP].shape[1] // 2) for i in range(2)]

        def get_half(i):
            copies.load(DUP, dup_hbm.at[:, parts[i]], at[DUP].at[:, parts[i]])
            copies.load(WU, wu_hbm.at[0, :, parts[i]], at[WU].at[:, parts[i]])

        get_half(0)
        copies.load(WIDE, wide_in)
        at[SUMS_B][...] = jnp.zeros(at[SUMS_B].shape, F32)
        copies.ready(DUP, WU, WIDE)
        get_half(1)
        copies.load(N1, n1)
        copies.load(R1, r1)
        copies.load(WO, wo_hbm.at[0])
        copies.load(CTX, ctx_hbm)
        at[WIDE][...] += mm(at[DUP][:, parts[0]], at[WU][:, parts[0]], NT)
        copies.ready(DUP, WU)
        at[WIDE][...] += mm(at[DUP][:, parts[1]], at[WU][:, parts[1]], NT)
        copies.ready(N1, R1)
        first_norm_back(at, gain1, at[DBR], 0)
        for name, target in ((DBR, outs[0]), (WIDE, outs[1]), (SUMS_B, outs[4])):
            copies.store(at[name], target)
        copies.ready(WO, CTX)
        context_back(at, at[DBR][...], at[CTX][...])
        copies.store(at[DCTX], outs[2])
        copies.store(at[DELTA], outs[3])
        copies.finish()


ATTEND_READ = (QKV, DCTX, KID, QID, LSE, DELTA)
ATTEND_HELD = ATTEND_READ + (X, CTX, DBR, REST, WIDE, WQKV, DQKV, SUMS_C, DX)


def attend_kernel(n_in, n_old, n_out, *refs):
    ins, outs, refs = split_refs(n_in, n_old, n_out, refs)
    x_hbm, ctx_hbm, dbr_hbm, share, wide_hbm, wq, wk, wv = ins[len(ATTEND_READ) :]
    dqkv_out, sums_out, dx_out = outs[:3]
    at = dict(zip(ATTEND_HELD, refs))
    total, sems = refs[-2:]
    width = at[X].shape[1]
    is_first = lax.axis_index(LAYER) == 0
    copies = Copies(at, sems)
    own = Copies(at, sems)
    own.used = 6
    for name, source in zip(ATTEND_READ, ins):
        own.load(name, source, now=False)
    targets = ((DQKV, dqkv_out), (SUMS_C, sums_out), (DX, dx_out))
    stores = [own.store(at[name], target, now=False) for name, target in targets]
    late = Copies(at, sems)
    late.used = 16
    late.load(WIDE, wide_hbm, now=False)
    for i, weight in enumerate((wq, wk, wv)):
        late.load(WQKV, weight.at[0], at[WQKV].at[:, pl.ds(i * width, width)], now=False)
    other = Copies(at, sems)
    other.used = 22
    other.load(DQKV, dqkv_out, now=False)

    @pl.when(is_first)
    def _():
        own.go()
        own.ready(*ATTEND_READ)

    for name, source in ((X, x_hbm), (CTX, ctx_hbm), (DBR, dbr_hbm), (REST, share)):
        copies.load(name, source)

    @pl.when(is_first)
    def _():
        late.go()
        over_pairs(width, lambda j: attend_pair_back(j, width, at, at[DQKV], 0))
        for way in stores[:2]:
            way.start()

    @pl.when(jnp.logical_not(is_first))
    def _():
        other.go()
        other.ready(DQKV)

    copies.ready(X, CTX, DBR, REST)
    way_out = GradientOut(total, outs[3:], sems, 24, width, False)
    way_out.put(0, mm(at[CTX][...], at[DBR][...], TN) + at[REST][:, 0:width].astype(F32))

    def step(i, carry):
        made = mm(at[X][...], at[DQKV][:, lanes_at((i - 1) * width, width)], TN)
        way_out.put(i, made + at[REST][:, lanes_at(i * width, width)].astype(F32))
        return carry

    lax.fori_loop(1, N_TILES, step, 0)

    @pl.when(is_first)
    def _():
        late.ready(WIDE, WQKV)
        at[DX][...] = (at[WIDE][...] + mm(at[DQKV][...], at[WQKV][...], NT)).astype(BF16)
        stores[2].start()
        own.finish()

    way_out.finish()


def swap(array, stride):
    count = lax.axis_size(ROWS)
    return lax.ppermute(array, ROWS, [(d, d ^ stride) for d in range(count)])


def halves_kernel(jobs, n_in, n_old, n_out, *refs):
    ins, outs, refs = split_refs(n_in, n_old, n_out, refs)
    copies = Copies({}, refs[-1])
    buffers = [refs[3 * i : 3 * i + 3] for i in range(len(jobs))]
    for i, job in enumerate(jobs):
        sources, stride, before, after, start, size, keep = job[:7]
        own = (lax.axis_index(ROWS) // stride) % 2
        which = own if keep else 1 - own
        for k in range(before):
            taken = pl.ds((2 * k + which) * after, after)
            for source, buffer in zip(sources, buffers[i]):
                target = buffer.at[pl.ds(k * after, after)]
                copies.load(i, ins[source].at[taken, :, pl.ds(start, size)], target)
    for i, job in enumerate(jobs):
        left, right, total = buffers[i]
        copies.ready(i)
        total[...] = (left[...].astype(F32) + right[...].astype(F32)).astype(BF16)
        place, start = job[7:]
        copies.store(total, outs[place].at[:, :, pl.ds(start, total.shape[-1])])
    copies.finish()


def halves(ways, arrays, n_outs, keep, free=False):
    tall = arrays[0].shape[1]
    jobs, scratch = [], []
    outs = [None] * n_outs
    for sources, stride, before, after, start, size, place, column in ways:
        jobs.append((sources, stride, before, after, start, size, keep, place, column))
        scratch += [((before * after, tall, size), BF16)] * 3
        outs[place] = ((before * after, tall, column + size), BF16)
    inputs = [(array, FREE if free else ANY) for array in arrays]
    body = partial(halves_kernel, tuple(jobs))
    return call(body, "halves", inputs, {}, outs, scratch, 32, 24 if free else 58)


class ScatterSum:
    def __init__(self, kept, came, sent=None):
        self.kept, self.came, self.sent = kept, came, sent

    @staticmethod
    def cores(blocks):
        return ScatterSum(blocks[0], swap(blocks[1], 1))

    @staticmethod
    def exchange(ways, arrays, n_outs, strides, first, free=False):
        arrays = lax.optimization_barrier((arrays, first))[0]
        sent = halves(ways, arrays, n_outs, 0, free)
        came = tuple(swap(part, stride) for part, stride in zip(sent, strides))
        kept = halves(ways, lax.optimization_barrier((arrays, sent))[0], n_outs, 1, free)
        return ScatterSum(tuple(kept), came, sent)

    def second(self, first, free=False):
        half = self.kept.shape[-1] // 2
        ways = (((0, 1), 2, 4, 1, 0, half, 0, 0), ((0, 1), 4, 2, 2, half, half, 1, 0))
        return self.exchange(ways, (self.kept, self.came), 2, (2, 4), first, free)

    def pairs(self):
        return (self.kept[0], self.came[0], self.kept[1], self.came[1])

    def third(self, first):
        half = self.kept[0].shape[-1]
        ways = (((0, 1), 4, 2, 1, 0, half, 0, 0), ((2, 3), 2, 2, 1, 0, half, 1, 0))
        return self.exchange(ways, self.pairs(), 2, (4, 2), first)

    def fourth(self, first):
        half = self.kept[0].shape[-1]
        ways = tuple(((2 * i, 2 * i + 1), 8, 1, 1, 0, half, 0, i * half) for i in range(2))
        made = self.exchange(ways, self.pairs(), 1, (8,), first)
        return ScatterSum(made.kept[0], made.came[0], made.sent)

    def finish(self):
        return (self.kept.astype(F32) + self.came.astype(F32))[0]


def whole_sum(partial_sum):
    return lax.psum_scatter(partial_sum, ROWS, scatter_dimension=0, tiled=True).astype(F32)


def small_sum(values, beside, after):
    if lax.axis_size(ROWS) != 16:
        return lax.psum(values, ROWS)
    for stride, first in zip((1, 2, 4, 8), (*beside, None)):
        values = values + swap(values, stride)
        if first is not None:
            values = after(values, first)
    return values


def on_device(tokens, cotangent, segment_ids, valid_mask, cluster_perm, *params):
    section = lax.axis_index(LAYER)
    is_first = section == 0
    wq, _, wk, wv, _, wo, _, gain1, _, wu, _, wd, _, gain2, _ = params
    width, inner = wu.shape[1:]
    ids = (cluster_perm, segment_ids, valid_mask)
    shapes = shapes_of(width, inner)

    def hop(array, source, target):
        return lax.ppermute(array, LAYER, [(source, target)])

    def after(array, first):
        return lax.optimization_barrier((array, first))[0]

    row0, y0, stats00 = forward(0, 0, tokens, 0, ids, params, None)
    in0 = hop(y0, 0, 1)
    row1, y1, stats01 = forward(0, 1, tokens, 1, ids, params, None)
    in1 = hop(y1, 0, 1)
    row0, out0, stats10, grads0, dx0 = through_and_back(0, in0, cotangent, ids, params, row0)
    cotangent = after(cotangent, dx0)
    g0 = hop(dx0, 1, 0)
    row1, out1, stats11, grads1, dx1 = through_and_back(1, in1, cotangent, ids, params, row1)
    g0 = after(g0, dx1)
    g1 = hop(dx1, 1, 0)
    grads0, (dx0, down_share, up_share, rest_share) = backward(0, g0, 0, params, row0, grads0)
    g1 = after(g1, dx0)

    def at_hbm(*arrays):
        return [(array, ANY) for array in arrays]

    def of(*names):
        return [shapes[name] for name in names]

    totals, parts = gradient_shapes((inner, width), (width, inner))
    plain = len(totals) == 2
    made = call(
        feed_kernel,
        "feed",
        at_hbm(g1)
        + [(gain2, WHOLE)]
        + at_hbm(row1[N2], row1[R2], row1[ACT], down_share, wd, row1[GP], row1[HID], up_share),
        {0: grads1[DFFN], 1: grads1[DUP], 2: grads1[SUMS_A]},
        of(DFFN, DUP, SUMS_A, WIDE) + parts,
        of(G, N2, R2, WIDE, SUMS_A, ACT, DFFN, WD, GP, HID, DUP, WD, WU) + totals,
        60,
    )
    _, dup1, sums_a1, wide = made[:4]
    feed_parts = made[4:]
    if not plain:
        feed_sum = ScatterSum.cores(feed_parts)

    made = call(
        middle_kernel,
        "middle",
        at_hbm(dup1, wide, wu) + [(gain1, WHOLE)] + at_hbm(row1[N1], row1[R1], wo, row1[CTX]),
        {0: grads1[DBR], 4: grads1[SUMS_B]},
        of(DBR, WIDE, DCTX, DELTA, SUMS_B),
        of(DUP, WIDE, WU, N1, R1, WO, CTX, DBR, DCTX, DELTA, SUMS_B),
        20,
    )
    dbr1, wide, dctx, delta, sums_b1 = made
    if not plain:
        feed_sum = feed_sum.second(dctx, True)
        dctx = after(dctx, feed_sum.kept)

    totals, parts = gradient_shapes((width, 4 * width))
    made = call(
        attend_kernel,
        "attend",
        at_hbm(row1[QKV], dctx, *(row1[name] for name in (KID, QID, LSE)), delta)
        + at_hbm(row1[X], row1[CTX], dbr1, rest_share, wide, wq, wk, wv),
        {0: grads1[DQKV], 1: grads1[SUMS_C]},
        of(DQKV, SUMS_C, DX) + parts,
        of(*ATTEND_HELD) + totals,
        40,
    )
    _, sums_c1, dx1 = made[:3]
    came = []
    if plain:
        w_down, w_up, w_rest = (whole_sum(part) for part in (*feed_parts, made[3]))
        w_out, w_query, w_key, w_value = jnp.split(w_rest, 4, axis=1)
    else:
        feed_sum = feed_sum.third(dx1)
        rest_sum = ScatterSum.cores(after(tuple(made[3:]), feed_sum.sent))
        came.append(rest_sum.came)
        rest_sum = rest_sum.second(feed_sum.sent)
        dx1 = after(dx1, rest_sum.sent)
        came.append(rest_sum.came)
        feed_sum = feed_sum.fourth(rest_sum.sent)
        rest_sum = rest_sum.third(feed_sum.sent)
        came.append(rest_sum.came)
        rest_sum = rest_sum.fourth(rest_sum.sent)
        w_feed, w_rest = feed_sum.finish(), rest_sum.finish()
        tall = inner // 16
        w_down = w_feed[:tall]
        w_up = jnp.concatenate(jnp.split(w_feed[tall:], N_TILES, axis=0), axis=1)
        w_out, w_query, w_key, w_value = jnp.split(w_rest, 4, axis=0)

    sums_a1, sums_b1, sums_c1 = (after(array, dx1) for array in (sums_a1, sums_b1, sums_c1))
    stats10 = after(stats10, dx1)
    sum_a = (grads0[SUMS_A] + sums_a1).reshape(4, 8, inner).sum(axis=1)
    sum_b = (grads0[SUMS_B] + sums_b1).reshape(3, 8, width).sum(axis=1)
    sum_c = (grads0[SUMS_C] + sums_c1).reshape(2, 8, width).sum(axis=1)
    stats = jnp.where(is_first, stats00 + stats01, stats10 + stats11)
    stats = stats.reshape(3, 8 * width).sum(axis=1)
    count = jnp.sum(valid_mask.astype(F32))
    pieces = [sum_a[:3, :width].reshape(-1), sum_b.reshape(-1), sum_c.reshape(-1), sum_a[3]]
    base = 8 * width + inner
    spare = -(base + 4) % (8 * LANES)
    tail = jnp.concatenate([stats, jnp.broadcast_to(count, (1,)), jnp.zeros((spare,), F32)])
    small = jnp.concatenate(pieces + [tail]).reshape(-1, LANES)
    small = small_sum(small, came, after).reshape(-1)
    shares = lax.axis_size(ROWS)
    me = lax.axis_index(ROWS)

    def small_part(place, size):
        own = size // shares
        return lax.dynamic_slice_in_dim(small, place * width + me * own, own, 0)[None]

    gain2_sum, shift2_sum, down_bias, gain1_sum, shift1_sum, out_bias, query_bias, value_bias = (
        small_part(i, width) for i in range(8)
    )
    up_bias = small_part(8, inner)
    root_means = jnp.sqrt(small[base : base + 3] / (small[base + 3] * width))[None, :]

    half = width // 2
    dx0, out0, out1 = (after(array, dx1) for array in (dx0, out0, out1))
    outgoing = jnp.concatenate(
        [
            jnp.where(is_first, grad[:, half:], made[:, :half])
            for grad, made in ((dx0, out0), (dx1, out1))
        ]
    )
    arrived = lax.ppermute(outgoing, LAYER, [(0, 1), (1, 0)])
    block_own = jnp.concatenate([out0[:, half:], out1[:, half:]])
    grad_own = jnp.concatenate([dx0[:, :half], dx1[:, :half]])
    block_part = jnp.where(is_first, arrived, block_own)
    grad_part = jnp.where(is_first, grad_own, arrived)
    return (
        block_part,
        grad_part,
        w_query[None],
        query_bias,
        w_key[None],
        w_value[None],
        value_bias,
        w_out[None],
        out_bias,
        gain1_sum,
        shift1_sum,
        w_up[None],
        up_bias,
        w_down[None],
        down_bias,
        gain2_sum,
        shift2_sum,
        root_means,
    )


def solution(mesh):
    by_layer = P(LAYER, None)
    matrix = P(LAYER, None, None)
    share = P(LAYER, ROWS)
    matrix_share = P(LAYER, ROWS, None)
    rows = P(ROWS, None)
    vectors = {1, 4, 6, 7, 8, 10, 12, 13, 14}
    matrices = {2, 4, 5, 7, 11, 13}
    return jax.shard_map(
        on_device,
        mesh=mesh,
        in_specs=(rows, rows, rows, rows, P(LAYER, ROWS, None, None))
        + tuple(by_layer if i in vectors else matrix for i in range(15)),
        out_specs=(P(ROWS, LAYER), P(ROWS, LAYER))
        + tuple(matrix_share if i in matrices else share for i in range(2, 17))
        + (P(LAYER, None),),
        check_vma=False,
    )
```

```python
from functools import partial

import jax
import jax.numpy as jnp
from jax import lax
from jax.experimental import pallas as pl
from jax.experimental.pallas import tpu as pltpu
from jax.sharding import PartitionSpec as P

HEAD_DIM = 64
CLUSTER = 128
SEQ = 512
LANES = 128
ROW_BLOCK = 512
PAIR_UNROLL = 3
MIB = 1024 * 1024

BF16 = jnp.bfloat16
F32 = jnp.float32
LOG2E = 1.4426950408889634
SCALE = HEAD_DIM**-0.5
SCORE_SCALE = SCALE * LOG2E

NN = ((1,), (0,))
NT = ((1,), (1,))
TN = ((0,), (0,))

ROWS = "dp"
LAYER = "section"
ANY = pl.BlockSpec(memory_space=pltpu.HBM)
FREE = pl.BlockSpec(memory_space=pl.ANY)
WHOLE = pl.BlockSpec(memory_space=pltpu.VMEM)
SHORT = pl.CostEstimate(flops=1, bytes_accessed=1, transcendentals=0)

X, QKV, CTX, LSE, KID, QID, N1, R1, HID, ACT, GP, N2, R2 = range(13)
G, DFFN, DUP, DBR, DQKV, SUMS_A, SUMS_B, SUMS_C, WIDE, DCTX, DELTA, DX, FEED, LIVE = range(13, 27)
BIAS, WQKV, Y, STATS, WO, WU, WD, REST = range(27, 35)
SAVED = (X, QKV, CTX, LSE, KID, QID, N1, R1, HID, ACT, GP, N2, R2)
GRADS = (DFFN, DUP, DBR, DQKV, SUMS_A, SUMS_B, SUMS_C)
GAIN2, SHIFT2, B_DOWN, B_UP = 0, 8, 16, 24
GAIN1, SHIFT1, B_OUT = 0, 8, 16
B_QUERY, B_VALUE = 0, 8


def shapes_of(width, inner):
    token, token32, narrow = ((SEQ, width), BF16), ((SEQ, width), F32), ((SEQ, LANES), F32)
    heads = ((16, SEQ), F32)
    shapes = {name: token for name in (X, CTX, N1, HID, N2, G, DFFN, DBR, DCTX, DX, Y)}
    shapes.update({name: token32 for name in (KID, WIDE, FEED)})
    shapes.update({name: narrow for name in (R1, R2, LIVE)})
    shapes.update({name: heads for name in (LSE, QID, DELTA)})
    shapes.update({name: ((SEQ, inner), BF16) for name in (ACT, GP, DUP)})
    shapes.update({name: ((SEQ, 3 * width), BF16) for name in (QKV, DQKV)})
    shapes.update({SUMS_A: ((32, inner), F32), SUMS_B: ((24, width), F32)})
    shapes.update({SUMS_C: ((16, width), F32), STATS: ((24, width), F32), BIAS: ((8, width), F32)})
    shapes.update({WQKV: ((width, 3 * width), BF16), WO: ((width, width), BF16)})
    shapes.update({WU: ((width, inner), BF16), WD: ((inner, width), BF16)})
    shapes[REST] = ((width, 4 * width), BF16)
    return shapes


def mm(left, right, dims):
    return lax.dot_general(left, right, (dims, ((), ())), preferred_element_type=F32)


def vec(ref):
    return ref[0:1, :].astype(F32)


def lanes_at(start, size=LANES):
    return pl.ds(pl.multiple_of(start, LANES), size)


def fold8(block):
    return jnp.sum(block.reshape(-1, 8, block.shape[-1]), axis=0)


def over_rows(step):
    def body(i, carry):
        step(pl.ds(pl.multiple_of(i * ROW_BLOCK, ROW_BLOCK), ROW_BLOCK))
        return carry

    lax.fori_loop(0, SEQ // ROW_BLOCK, body, 0)


def over_tiles(size, tile, step):
    def body(i, carry):
        step(pl.ds(pl.multiple_of(i * tile, tile), tile))
        return carry

    lax.fori_loop(0, size // tile, body, 0)


class Copies:
    def __init__(self, at, sems):
        self.at, self.sems = at, sems
        self.used = 0
        self.loads = {}
        self.stores = []

    def plan(self, source, target):
        self.used += 1
        return pltpu.make_async_copy(source, target, self.sems.at[self.used - 1])

    def load(self, name, source, target=None, now=True):
        target = self.at[name] if target is None else target
        copy = self.plan(source, target)
        self.loads.setdefault(name, []).append(copy)
        if now:
            copy.start()

    def go(self):
        for copies in self.loads.values():
            for copy in copies:
                copy.start()

    def ready(self, *names):
        for name in names:
            for copy in self.loads.pop(name, ()):
                copy.wait()

    def store(self, source, target, now=True):
        copy = self.plan(source, target)
        self.stores.append(copy)
        if now:
            copy.start()
        return copy

    def finish(self):
        for copy in self.stores:
            copy.wait()


def load_qkv(copies, weights, width):
    for i, weight in enumerate(weights):
        copies.load(WQKV, weight.at[0], copies.at[WQKV].at[:, pl.ds(i * width, width)])


def call(body, name, inputs, old, outs, scratch, n_sems, vmem=58):
    arrays = [array for array, _ in inputs]
    n_in = len(arrays)
    return pl.pallas_call(
        partial(body, n_in, len(old), len(outs)),
        out_shape=[jax.ShapeDtypeStruct(*shape) for shape in outs],
        in_specs=[spec for _, spec in inputs] + [ANY] * len(old),
        out_specs=[ANY] * len(outs),
        input_output_aliases={n_in + i: place for i, place in enumerate(old)},
        scratch_shapes=[pltpu.VMEM(*shape) for shape in scratch]
        + [pltpu.SemaphoreType.DMA((n_sems,))],
        compiler_params=pltpu.CompilerParams(vmem_limit_bytes=vmem * MIB),
        cost_estimate=SHORT,
        name=name,
    )(*arrays, *old.values())


def split_refs(n_in, n_old, n_out, refs):
    return refs[:n_in], refs[n_in + n_old : n_in + n_old + n_out], refs[n_in + n_old + n_out :]


def low_lanes():
    return lax.broadcasted_iota(jnp.int32, (SEQ, LANES), 1) < HEAD_DIM


def masked(scores, kid_column, qid_row):
    shape = (CLUSTER, CLUSTER)
    same = lax.broadcasted_iota(jnp.int32, shape, 0) == lax.broadcasted_iota(jnp.int32, shape, 1)
    count = SEQ // CLUSTER
    parts = [slice(i * CLUSTER, (i + 1) * CLUSTER) for i in range(count)]
    rows = []
    for i in range(count):
        tiles = []
        for j in range(count):
            ok = kid_column[parts[i]] == qid_row[:, parts[j]]
            if i == j:
                ok = ok | same
            tiles.append(jnp.where(ok, scores[parts[i], parts[j]], -1e30))
        rows.append(jnp.concatenate(tiles, axis=1))
    return jnp.concatenate(rows, axis=0)


def attend_pair(j, width, at):
    low = low_lanes()
    lanes = lanes_at(j * LANES)
    query = at[QKV][:, lanes]
    key = at[QKV][:, lanes_at(width + j * LANES)]
    value = at[QKV][:, lanes_at(2 * width + j * LANES)]
    kid_pair = at[KID][:, lanes]
    mixed, tops = [], []
    for half in (0, 1):
        own = low if half == 0 else ~low
        own_query = jnp.where(own, query, jnp.zeros_like(query))
        value_ones = jnp.where(own, value, jnp.ones_like(value))
        kid_column = kid_pair[:, half * HEAD_DIM : half * HEAD_DIM + 1]
        scores = mm(key, own_query, NT) * SCORE_SCALE
        scores = masked(scores, kid_column, at[QID][pl.ds(2 * j + half, 1), :])
        top = jnp.max(scores, axis=0, keepdims=True)
        tops.append(top)
        mixed.append(mm(jnp.exp2(scores - top).astype(BF16), value_ones, TN))
    sums = [pltpu.roll(part, HEAD_DIM, 1) for part in mixed]
    total = jnp.where(low, sums[0], sums[1])
    at[CTX][:, lanes] = (jnp.where(low, mixed[0], mixed[1]) / total).astype(BF16)
    turned = total.T
    for half in (0, 1):
        row = turned[half * HEAD_DIM : half * HEAD_DIM + 1, :]
        at[LSE][pl.ds(2 * j + half, 1), :] = tops[half] + jnp.log2(row)


def attend_pair_back(j, width, at, target, base):
    low = low_lanes()
    lanes = [lanes_at(i * width + j * LANES) for i in range(3)]
    query, key, value = (at[QKV][:, part] for part in lanes)
    d_out = at[DCTX][:, lanes[0]]
    kid_pair = at[KID][:, lanes[0]]
    d_query, d_key, d_value = [], [], []
    for half in (0, 1):
        h = pl.ds(2 * j + half, 1)
        own = low if half == 0 else ~low
        own_query = jnp.where(own, query, jnp.zeros_like(query))
        own_out = jnp.where(own, d_out, jnp.zeros_like(d_out))
        kid_column = kid_pair[:, half * HEAD_DIM : half * HEAD_DIM + 1]
        scores = mm(key, own_query, NT) * SCORE_SCALE - at[LSE][h, :]
        weights = jnp.exp2(masked(scores, kid_column, at[QID][h, :]))
        d_weights = mm(value, own_out, NT)
        d_scores = (weights * (d_weights - at[DELTA][h, :])).astype(BF16)
        d_value.append(mm(weights.astype(BF16), own_out, NN))
        d_key.append(mm(d_scores, own_query, NN))
        d_query.append(mm(d_scores, key, TN))
    made = (
        jnp.where(low, d_query[0], d_query[1]) * SCALE,
        (d_key[0] + d_key[1]) * SCALE,
        d_value[0] + d_value[1],
    )
    rows = pl.ds(base, SEQ)
    for i, place in ((0, B_QUERY), (1, None), (2, B_VALUE)):
        rounded = made[i].astype(BF16)
        target[rows, lanes[i]] = rounded
        if place is not None:
            at[SUMS_C][place : place + 8, lanes[0]] = fold8(rounded.astype(F32))


def over_pairs(width, step):
    def body(j, carry):
        step(j)
        return carry

    lax.fori_loop(0, width // LANES, body, 0, unroll=PAIR_UNROLL)


def token_ids(row, heads, perm_ref, seg_ref, valid_ref, kid_ref, qid_ref):
    token = lax.broadcasted_iota(jnp.int32, (SEQ, LANES), 0)
    lane = lax.broadcasted_iota(jnp.int32, (SEQ, LANES), 1)
    seg_row = seg_ref[row : row + 1, :].astype(F32)
    valid_row = valid_ref[row : row + 1, :].astype(F32)
    at = lax.broadcasted_iota(jnp.int32, (LANES, SEQ), 0)
    both = jnp.where(at == 0, seg_row, jnp.where(at == 1, valid_row, 0.0)).T
    segment, live = both[:, 0:1], both[:, 1:2]

    def column(h):
        places = perm_ref[0, row, pl.ds(h, 1), :]
        mine = jnp.zeros((SEQ, LANES), F32)
        for c in range(1, SEQ // CLUSTER):
            part = places[:, c * CLUSTER : (c + 1) * CLUSTER]
            mine = jnp.where(token == part, float(c), mine)
        return jnp.sum(mine, axis=1, keepdims=True) * 4.0 + segment

    def pair(j, ids):
        left, right = column(2 * j), column(2 * j + 1)
        own = jnp.where(lane < HEAD_DIM, left, right)
        kid_ref[:, lanes_at(j * LANES)] = jnp.where(live > 0.5, own, -1.0)
        ids = jnp.where(lane == 2 * j, left, ids)
        return jnp.where(lane == 2 * j + 1, right, ids)

    qid = lax.fori_loop(0, heads // 2, pair, jnp.zeros((SEQ, LANES), F32))
    qid_ref[...] = qid.T[0:16, :]
    return live


def normed(total):
    centre = total - jnp.mean(total, axis=-1, keepdims=True)
    spread = jnp.mean(centre * centre, axis=-1, keepdims=True)
    rate = lax.rsqrt(spread + 1e-05)
    return centre * rate, rate


FORWARD_HELD = SAVED + (WQKV, WO, WU, WD, WIDE, FEED, Y, STATS, LIVE, BIAS)


def run_forward(at, copies, save, row, source, ids, params, later=None):
    perm_ref, seg_ref, valid_ref = ids
    wq, bq, wk, wv, bv, wo, bo, g1, s1, wu, bu, wd, bd, g2, s2 = params
    width, inner = at[WU].shape
    heads = width // HEAD_DIM
    copies.load(X, source)
    first = copies.used
    load_qkv(copies, (wq, wk, wv), width)
    live = token_ids(row, heads, perm_ref, seg_ref, valid_ref, at[KID], at[QID])
    at[LIVE][...] = jnp.broadcast_to(live, (SEQ, LANES))
    at[LSE][...] = jnp.zeros((16, SEQ), F32)
    at[STATS][...] = jnp.zeros((24, width), F32)
    at[BIAS][0:1, :] = vec(bq)
    at[BIAS][1:2, :] = jnp.zeros((1, width), F32)
    at[BIAS][2:3, :] = vec(bv)
    copies.ready(X)

    def to_qkv(i, carry):
        part = pl.ds(pl.multiple_of(i * width, LANES), width)
        weight = at[WQKV].at[:, part]
        pltpu.make_async_copy(weight, weight, copies.sems.at[first + i]).wait()
        made = mm(at[X][...], at[WQKV][:, part], NN) + at[BIAS][pl.ds(i, 1), :]
        at[QKV][:, part] = made.astype(BF16)
        return carry

    lax.fori_loop(0, 3, to_qkv, 0)
    copies.loads.pop(WQKV)
    copies.load(WO, wo.at[0])
    copies.load(WU, wu.at[0])
    copies.load(WD, wd.at[0])
    if later is not None:
        later()
    save(KID, QID, X, QKV)
    over_pairs(width, lambda j: attend_pair(j, width, at))
    save(LSE, CTX)
    copies.ready(WO)
    at[WIDE][...] = mm(at[CTX][...], at[WO][...], NN)

    def first_norm(rows):
        branch = at[WIDE][rows, :] + vec(bo)
        alive = at[LIVE][rows, 0:1]
        at[STATS][0:8, :] += fold8(branch * branch * alive)
        unit, rate = normed(at[X][rows, :].astype(F32) + branch)
        hidden = unit * vec(g1) + vec(s1)
        at[N1][rows, :] = unit.astype(BF16)
        at[R1][rows, :] = jnp.broadcast_to(rate, (ROW_BLOCK, LANES))
        at[HID][rows, :] = hidden.astype(BF16)
        at[WIDE][rows, :] = hidden

    over_rows(first_norm)
    save(N1, R1, HID)
    copies.ready(WU)

    def up(part):
        upper = mm(at[HID][...], at[WU][:, part], NN) + bu[0:1, part].astype(F32)
        half = 0.5 + 0.5 * lax.erf(upper * 0.5**0.5)
        bell = jnp.exp2(upper * upper * (-0.5 * LOG2E)) * 0.3989422804014327
        at[ACT][:, part] = (upper * half).astype(BF16)
        at[GP][:, part] = (half + upper * bell).astype(BF16)

    over_tiles(inner, inner // 2, up)
    save(ACT, GP)
    copies.ready(WD)
    at[FEED][...] = mm(at[ACT][...], at[WD][...], NN)

    def second_norm(rows):
        ffn = at[FEED][rows, :] + vec(bd)
        alive = at[LIVE][rows, 0:1]
        at[STATS][8:16, :] += fold8(ffn * ffn * alive)
        unit, rate = normed(at[WIDE][rows, :] + ffn)
        result = unit * vec(g2) + vec(s2)
        at[STATS][16:24, :] += fold8(result * result * alive)
        at[N2][rows, :] = unit.astype(BF16)
        at[R2][rows, :] = jnp.broadcast_to(rate, (ROW_BLOCK, LANES))
        at[Y][rows, :] = result.astype(BF16)

    over_rows(second_norm)
    save(Y, STATS, N2, R2)


def forward_kernel(section, row, x_row, n_in, n_old, n_out, *refs):
    ins, outs, refs = split_refs(n_in, n_old, n_out, refs)
    out = dict(zip(SAVED + (Y, STATS), outs))
    at = dict(zip(FORWARD_HELD, refs))

    @pl.when(lax.axis_index(LAYER) == section)
    def _():
        copies = Copies(at, refs[-1])

        def save(*names):
            for name in names:
                copies.store(at[name], out[name])

        source = ins[0].at[pl.ds(x_row * SEQ, SEQ), :]
        run_forward(at, copies, save, row, source, ins[1:4], ins[4:])
        copies.finish()


def forward(section, row, x, x_row, ids, params, kept):
    width, inner = params[9].shape[1:]
    shapes = shapes_of(width, inner)
    inputs = [(x, ANY)] + [(array, WHOLE) for array in ids]
    inputs += [(array, ANY if array.ndim == 3 else WHOLE) for array in params]
    made = call(
        partial(forward_kernel, section, row, x_row),
        "forward",
        inputs,
        {} if kept is None else {i: kept[name] for i, name in enumerate(SAVED)},
        [shapes[name] for name in SAVED + (Y, STATS)],
        [shapes[name] for name in FORWARD_HELD],
        32,
    )
    return dict(zip(SAVED, made)), made[-2], made[-1]


def norm_back(grad, unit, rate, gain):
    scaled = grad * gain
    mean = jnp.mean(scaled, axis=-1, keepdims=True)
    along = jnp.mean(scaled * unit, axis=-1, keepdims=True)
    return (scaled - mean - unit * along) * rate


def add_sum(ref, place, value):
    ref[place : place + 8, 0 : value.shape[-1]] += fold8(value)


def second_norm_back(at, gain2, target, base):
    def step(rows):
        grad = at[G][rows, :].astype(F32)
        unit = at[N2][rows, :].astype(F32)
        add_sum(at[SUMS_A], GAIN2, grad * unit)
        add_sum(at[SUMS_A], SHIFT2, grad)
        d_second = norm_back(grad, unit, at[R2][rows, 0:1], vec(gain2))
        at[WIDE][rows, :] = d_second
        low = d_second.astype(BF16)
        target[pl.ds(pl.multiple_of(rows.start + base, ROW_BLOCK), ROW_BLOCK), :] = low
        add_sum(at[SUMS_A], B_DOWN, low.astype(F32))

    over_rows(step)


def up_back(at, dffn, part):
    d_act = mm(dffn, at[WD][part, :], NT)
    low = (d_act * at[GP][:, part].astype(F32)).astype(BF16)
    at[SUMS_A][B_UP : B_UP + 8, part] += fold8(low.astype(F32))
    return low


def first_norm_back(at, gain1, target, base):
    def step(rows):
        grad = at[WIDE][rows, :]
        unit = at[N1][rows, :].astype(F32)
        add_sum(at[SUMS_B], GAIN1, grad * unit)
        add_sum(at[SUMS_B], SHIFT1, grad)
        d_first = norm_back(grad, unit, at[R1][rows, 0:1], vec(gain1))
        at[WIDE][rows, :] = d_first
        low = d_first.astype(BF16)
        target[pl.ds(pl.multiple_of(rows.start + base, ROW_BLOCK), ROW_BLOCK), :] = low
        add_sum(at[SUMS_B], B_OUT, low.astype(F32))

    over_rows(step)


def context_back(at, dbr, context):
    width = dbr.shape[1]
    d_context = mm(dbr, at[WO][...], NT).astype(BF16)
    at[DCTX][...] = d_context
    product = d_context.astype(F32) * context.astype(F32)
    high = product.astype(BF16)
    rest = (product - high.astype(F32)).astype(BF16)
    of_head = (
        lax.broadcasted_iota(jnp.int32, (16, width), 1) // HEAD_DIM
        == lax.broadcasted_iota(jnp.int32, (16, width), 0)
    )
    pick = jnp.where(of_head, 1.0, 0.0).astype(BF16)
    at[DELTA][...] = mm(pick, high, NT) + mm(pick, rest, NT)


def run_backward(at, copies, get, save, params, shared):
    gain1, gain2 = params[:2]
    width, inner = at[WU].shape
    get(G, N2, R2)
    for name in (SUMS_A, SUMS_B):
        at[name][...] = jnp.zeros(at[name].shape, F32)
    copies.ready(G, N2, R2)
    get(WD, GP)
    second_norm_back(at, gain2, at[DFFN], 0)
    save(DFFN)
    get(WU, N1, R1, WO, CTX)
    copies.ready(WD, GP)

    def up(part):
        at[DUP][:, part] = up_back(at, at[DFFN][...], part)

    over_tiles(inner, inner // 2, up)
    save(DUP, SUMS_A)
    get(QKV, KID, QID, LSE, WQKV)
    copies.ready(WU)
    at[WIDE][...] += mm(at[DUP][...], at[WU][...], NT)
    copies.ready(N1, R1)
    first_norm_back(at, gain1, at[DBR], 0)
    save(DBR, SUMS_B)
    copies.ready(WO, CTX)
    context_back(at, at[DBR][...], at[CTX][...])
    copies.ready(QKV, KID, QID, LSE)
    if shared is not None:
        shared.go()
    over_pairs(width, lambda j: attend_pair_back(j, width, at, at[DQKV], 0))
    save(DQKV, SUMS_C)
    copies.ready(WQKV)
    at[DX][...] = (at[WIDE][...] + mm(at[DQKV][...], at[WQKV][...], NT)).astype(BF16)
    save(DX)


BACK_READ = (N2, R2, GP, N1, R1, CTX, LSE, KID, QID, QKV)
SHARE_READ = (ACT, HID, X)
BACK_HELD = (G,) + BACK_READ + GRADS + (WIDE, DCTX, DELTA, DX, WQKV, WO, WU, WD)


def backward_kernel(section, g_row, n_in, n_old, n_out, *refs):
    ins, outs, refs = split_refs(n_in, n_old, n_out, refs)
    g_hbm, gain1, gain2, wq, wk, wv, wo, wu, wd = ins[:9]
    given = dict(zip(BACK_READ + SHARE_READ, ins[9:]))
    given.update({WO: wo.at[0], WU: wu.at[0], WD: wd.at[0]})
    given[G] = g_hbm.at[pl.ds(g_row * SEQ, SEQ), :]
    with_shares = section == 0
    out = dict(zip(GRADS + (DX,), outs))
    at = dict(zip(BACK_HELD + (SHARE_READ if with_shares else ()), refs))
    width, inner = at[WU].shape
    shared = Copies(at, refs[-1])
    shared.used = 40
    if with_shares:
        for name in SHARE_READ:
            shared.load(name, given[name], now=False)

        @pl.when(lax.axis_index(LAYER) != section)
        def _():
            others = Copies(at, refs[-1])
            others.used = 50
            for name in (DFFN, DUP, DBR, DQKV):
                others.load(name, out[name])
            others.load(CTX, given[CTX])
            shared.go()
            others.ready(DFFN, DUP, DBR, DQKV, CTX)

    @pl.when(lax.axis_index(LAYER) == section)
    def _():
        copies = Copies(at, refs[-1])

        def get(*names):
            for name in names:
                if name == WQKV:
                    load_qkv(copies, (wq, wk, wv), width)
                else:
                    copies.load(name, given[name])

        def save(*names):
            for name in names:
                copies.store(at[name], out[name])

        run_backward(at, copies, get, save, ins[1:3], shared if with_shares else None)
        copies.finish()

    if not with_shares:
        return
    down, up, rest = at[WD], at[WU], refs[-2]
    shared.ready(*SHARE_READ)

    def to_down(part):
        down[part, :] = mm(at[ACT][:, part], at[DFFN][...], TN).astype(BF16)

    over_tiles(inner, width, to_down)
    shared.store(down, outs[-3])

    def to_up(part):
        up[:, part] = mm(at[HID][...], at[DUP][:, part], TN).astype(BF16)

    over_tiles(inner, width, to_up)
    shared.store(up, outs[-2])
    rest[:, 0:width] = mm(at[CTX][...], at[DBR][...], TN).astype(BF16)

    def to_rest(i, carry):
        made = mm(at[X][...], at[DQKV][:, lanes_at(i * width - width, width)], TN)
        rest[:, lanes_at(i * width, width)] = made.astype(BF16)
        return carry

    lax.fori_loop(1, 4, to_rest, 0)
    shared.store(rest, outs[-1])
    shared.finish()


def backward(section, g, g_row, params, kept, old):
    wq, _, wk, wv, _, wo, _, gain1, _, wu, _, wd, _, gain2, _ = params
    shapes = shapes_of(*wu.shape[1:])
    inputs = [(g, ANY), (gain1, WHOLE), (gain2, WHOLE)]
    inputs += [(array, ANY) for array in (wq, wk, wv, wo, wu, wd)]
    inputs += [(kept[name], ANY) for name in BACK_READ]
    outs, held = list(GRADS + (DX,)), list(BACK_HELD)
    if section == 0:
        inputs += [(kept[name], ANY) for name in SHARE_READ]
        outs += [WD, WU, REST]
        held += SHARE_READ + (REST,)
    made = call(
        partial(backward_kernel, section, g_row),
        "backward",
        inputs,
        {} if old is None else {i: old[name] for i, name in enumerate(GRADS)},
        [shapes[name] for name in outs],
        [shapes[name] for name in held],
        56,
    )
    return dict(zip(GRADS, made)), made[len(GRADS) :]


KEPT = (X, CTX, HID, ACT)
BOTH_HELD = FORWARD_HELD + (G,) + GRADS + (DCTX, DELTA, DX)


def both_kernel(row, n_in, n_old, n_out, *refs):
    ins, outs, refs = split_refs(n_in, n_old, n_out, refs)
    out = dict(zip(KEPT + (Y, STATS) + GRADS + (DX,), outs))
    at = dict(zip(BOTH_HELD, refs))
    params = ins[5:]

    @pl.when(lax.axis_index(LAYER) == 1)
    def _():
        copies = Copies(at, refs[-1])

        def save(*names):
            for name in names:
                if name in out:
                    copies.store(at[name], out[name])

        def get(*names):
            pass

        def later():
            copies.load(G, ins[1].at[pl.ds(row * SEQ, SEQ), :])

        run_forward(at, copies, save, row, ins[0], ins[2:5], params, later)
        run_backward(at, copies, get, save, (params[7], params[13]), None)
        copies.finish()


def through_and_back(row, x, g, ids, params, kept):
    shapes = shapes_of(*params[9].shape[1:])
    inputs = [(x, ANY), (g, ANY)] + [(array, WHOLE) for array in ids]
    inputs += [(array, ANY if array.ndim == 3 else WHOLE) for array in params]
    names = KEPT + (Y, STATS) + GRADS + (DX,)
    made = call(
        partial(both_kernel, row),
        "both",
        inputs,
        {i: kept[name] for i, name in enumerate(KEPT)},
        [shapes[name] for name in names],
        [shapes[name] for name in BOTH_HELD],
        48,
    )
    made = dict(zip(names, made))
    kept = {**kept, **{name: made[name] for name in KEPT}}
    return kept, made[Y], made[STATS], {name: made[name] for name in GRADS}, made[DX]


N_TILES = 4


def gradient_shapes(*sizes):
    count = lax.axis_size(ROWS)
    if count != 16:
        shapes = [(size, BF16) for size in sizes]
        return shapes, shapes
    tall = sum(rows * columns for rows, columns in sizes) // (count * min(map(min, sizes)))
    width = min(map(min, sizes))
    return [((8, 2, tall, width), BF16)], [((8, tall, width), BF16)] * 2


class GradientOut:
    def __init__(self, ref, targets, sems, first_sem, tile, by_rows, base=0):
        self.ref, self.targets, self.sems, self.first_sem = ref, targets, sems, first_sem
        self.tile, self.by_rows, self.base = tile, by_rows, base
        self.plain = len(targets) == 1
        self.tall = tile // 4 if by_rows else tile // 16

    def at(self, i):
        start = i * self.tile
        if self.plain and self.by_rows:
            return (pl.ds(pl.multiple_of(start, 16), self.tile),)
        if self.plain:
            return (slice(None), lanes_at(start, self.tile))
        if self.by_rows:
            return (pl.ds(2 * i, 2), pl.ds(self.base, self.tall))
        return (slice(None), pl.ds(pl.multiple_of(self.base + i * self.tall, 16), self.tall))

    def moves(self, i):
        at = self.at(i)
        if self.plain:
            pairs = [(self.ref.at[at], self.targets[0].at[at])]
        else:
            core = lax.axis_index(ROWS) % 2
            pairs = [
                (self.ref.at[at[0], which, at[1]], target.at[at])
                for target, which in zip(self.targets, (core, 1 - core))
            ]
        base = self.first_sem + i * len(pairs)
        return [
            pltpu.make_async_copy(source, target, self.sems.at[base + k])
            for k, (source, target) in enumerate(pairs)
        ]

    def put(self, i, value):
        value = value.astype(BF16)
        at = self.at(i)
        if self.plain:
            self.ref[at] = value
        else:
            split = value.reshape(-1, 2, self.tall, value.shape[1])
            self.ref[at[0], :, at[1], :] = split
        for move in self.moves(i):
            move.start()

    def finish(self):
        for i in range(N_TILES):
            for move in self.moves(i):
                move.wait()


def loop_tiles(step):
    def body(i, carry):
        step(i)
        return carry

    lax.fori_loop(0, N_TILES, body, 0)


FEED_HELD = (G, N2, R2, WIDE, SUMS_A, ACT, DFFN, WD, GP, HID, DUP, FEED, REST)


def feed_kernel(n_in, n_old, n_out, *refs):
    ins, outs, refs = split_refs(n_in, n_old, n_out, refs)
    g_hbm, gain2, n2, r2, act_hbm, down_share, wd_hbm, gp_hbm, hid_hbm, up_share = ins
    dffn_out, dup_out, sums_out, wide_out = outs[:4]
    at = dict(zip(FEED_HELD, refs))
    totals, sems = refs[len(FEED_HELD) : -1], refs[-1]
    inner, width = at[WD].shape
    tile = inner // N_TILES
    if len(totals) == 1:
        ways = [(totals[0], outs[4:]), (totals[0], outs[4:])]
    else:
        ways = [(total, [target]) for total, target in zip(totals, outs[4:])]
    down_way = GradientOut(*ways[0], sems, 40, tile, True)
    up_way = GradientOut(*ways[1], sems, 50, tile, False, tile // 4)
    is_first = lax.axis_index(LAYER) == 0
    copies = Copies(at, sems)
    own = Copies(at, sems)
    own.used = 4
    for name, source in ((G, g_hbm), (N2, n2), (R2, r2)):
        own.load(name, source, now=False)
    targets = ((DFFN, dffn_out), (WIDE, wide_out), (SUMS_A, sums_out))
    stores = [own.store(at[name], target, now=False) for name, target in targets]
    other = Copies(at, sems)
    other.used = 12
    other.load(DFFN, dffn_out, now=False)
    other.load(DUP, dup_out, now=False)

    def fetch(i):
        part = lanes_at(i * tile, tile)
        pairs = (
            (up_share.at[:, part], at[REST].at[:, part]),
            (wd_hbm.at[0, part, :], at[WD].at[part, :]),
            (gp_hbm.at[:, part], at[GP].at[:, part]),
        )
        return [
            pltpu.make_async_copy(source, target, sems.at[16 + 3 * i + k])
            for k, (source, target) in enumerate(pairs)
        ]

    def fetch_start(i):
        fetch(i)[0].start()

        @pl.when(is_first)
        def _():
            for move in fetch(i)[1:]:
                move.start()

    def away(i):
        part = lanes_at(i * tile, tile)
        return pltpu.make_async_copy(at[DUP].at[:, part], dup_out.at[:, part], sems.at[32 + i])

    @pl.when(is_first)
    def _():
        own.go()

    copies.load(ACT, act_hbm)
    copies.load(FEED, down_share)

    @pl.when(is_first)
    def _():
        at[SUMS_A][...] = jnp.zeros(at[SUMS_A].shape, F32)
        own.ready(G, N2, R2)

    copies.load(HID, hid_hbm)
    fetch_start(0)

    @pl.when(is_first)
    def _():
        second_norm_back(at, gain2, at[DFFN], 0)
        for way in stores[:2]:
            way.start()

    @pl.when(jnp.logical_not(is_first))
    def _():
        other.go()
        other.ready(DFFN, DUP)

    copies.ready(ACT, FEED)
    fetch_start(1)

    def down_step(i):
        part = lanes_at(i * tile, tile)
        made = mm(at[ACT][:, part], at[DFFN][...], TN)
        down_way.put(i, made + at[FEED][part, :].astype(F32))

    loop_tiles(down_step)
    fetch_start(2)
    fetch_start(3)
    copies.ready(HID)

    def up_step(i):
        part = lanes_at(i * tile, tile)

        @pl.when(is_first)
        def _():
            for move in fetch(i)[1:]:
                move.wait()
            at[DUP][:, part] = up_back(at, at[DFFN][...], part)
            away(i).start()

        fetch(i)[0].wait()
        made = mm(at[HID][...], at[DUP][:, part], TN)
        up_way.put(i, made + at[REST][:, part].astype(F32))

    loop_tiles(up_step)
    down_way.finish()
    up_way.finish()

    @pl.when(is_first)
    def _():
        stores[2].start()
        for i in range(N_TILES):
            away(i).wait()
        own.finish()


def middle_kernel(n_in, n_old, n_out, *refs):
    ins, outs, refs = split_refs(n_in, n_old, n_out, refs)
    dup_hbm, wide_in, wu_hbm, gain1, n1, r1, wo_hbm, ctx_hbm = ins
    at = dict(zip((DUP, WIDE, WU, N1, R1, WO, CTX, DBR, DCTX, DELTA, SUMS_B), refs))

    @pl.when(lax.axis_index(LAYER) == 0)
    def _():
        copies = Copies(at, refs[-1])
        parts = [pl.ds(i * at[DUP].shape[1] // 2, at[DUP].shape[1] // 2) for i in range(2)]

        def get_half(i):
            copies.load(DUP, dup_hbm.at[:, parts[i]], at[DUP].at[:, parts[i]])
            copies.load(WU, wu_hbm.at[0, :, parts[i]], at[WU].at[:, parts[i]])

        get_half(0)
        copies.load(WIDE, wide_in)
        at[SUMS_B][...] = jnp.zeros(at[SUMS_B].shape, F32)
        copies.ready(DUP, WU, WIDE)
        get_half(1)
        copies.load(N1, n1)
        copies.load(R1, r1)
        copies.load(WO, wo_hbm.at[0])
        copies.load(CTX, ctx_hbm)
        at[WIDE][...] += mm(at[DUP][:, parts[0]], at[WU][:, parts[0]], NT)
        copies.ready(DUP, WU)
        at[WIDE][...] += mm(at[DUP][:, parts[1]], at[WU][:, parts[1]], NT)
        copies.ready(N1, R1)
        first_norm_back(at, gain1, at[DBR], 0)
        for name, target in ((DBR, outs[0]), (WIDE, outs[1]), (SUMS_B, outs[4])):
            copies.store(at[name], target)
        copies.ready(WO, CTX)
        context_back(at, at[DBR][...], at[CTX][...])
        copies.store(at[DCTX], outs[2])
        copies.store(at[DELTA], outs[3])
        copies.finish()


ATTEND_READ = (QKV, DCTX, KID, QID, LSE, DELTA)
ATTEND_HELD = ATTEND_READ + (X, CTX, DBR, REST, WIDE, WQKV, DQKV, SUMS_C, DX)


def attend_kernel(n_in, n_old, n_out, *refs):
    ins, outs, refs = split_refs(n_in, n_old, n_out, refs)
    x_hbm, ctx_hbm, dbr_hbm, share, wide_hbm, wq, wk, wv = ins[len(ATTEND_READ) :]
    dqkv_out, sums_out, dx_out = outs[:3]
    at = dict(zip(ATTEND_HELD, refs))
    total, sems = refs[-2:]
    width = at[X].shape[1]
    is_first = lax.axis_index(LAYER) == 0
    copies = Copies(at, sems)
    own = Copies(at, sems)
    own.used = 6
    for name, source in zip(ATTEND_READ, ins):
        own.load(name, source, now=False)
    targets = ((DQKV, dqkv_out), (SUMS_C, sums_out), (DX, dx_out))
    stores = [own.store(at[name], target, now=False) for name, target in targets]
    late = Copies(at, sems)
    late.used = 16
    late.load(WIDE, wide_hbm, now=False)
    for i, weight in enumerate((wq, wk, wv)):
        late.load(WQKV, weight.at[0], at[WQKV].at[:, pl.ds(i * width, width)], now=False)
    other = Copies(at, sems)
    other.used = 22
    other.load(DQKV, dqkv_out, now=False)

    @pl.when(is_first)
    def _():
        own.go()
        own.ready(*ATTEND_READ)

    for name, source in ((X, x_hbm), (CTX, ctx_hbm), (DBR, dbr_hbm), (REST, share)):
        copies.load(name, source)

    @pl.when(is_first)
    def _():
        late.go()
        over_pairs(width, lambda j: attend_pair_back(j, width, at, at[DQKV], 0))
        for way in stores[:2]:
            way.start()

    @pl.when(jnp.logical_not(is_first))
    def _():
        other.go()
        other.ready(DQKV)

    copies.ready(X, CTX, DBR, REST)
    way_out = GradientOut(total, outs[3:], sems, 24, width, False)
    way_out.put(0, mm(at[CTX][...], at[DBR][...], TN) + at[REST][:, 0:width].astype(F32))

    def step(i, carry):
        made = mm(at[X][...], at[DQKV][:, lanes_at((i - 1) * width, width)], TN)
        way_out.put(i, made + at[REST][:, lanes_at(i * width, width)].astype(F32))
        return carry

    lax.fori_loop(1, N_TILES, step, 0)

    @pl.when(is_first)
    def _():
        late.ready(WIDE, WQKV)
        at[DX][...] = (at[WIDE][...] + mm(at[DQKV][...], at[WQKV][...], NT)).astype(BF16)
        stores[2].start()
        own.finish()

    way_out.finish()


def swap(array, stride):
    count = lax.axis_size(ROWS)
    return lax.ppermute(array, ROWS, [(d, d ^ stride) for d in range(count)])


def halves_kernel(jobs, n_in, n_old, n_out, *refs):
    ins, outs, refs = split_refs(n_in, n_old, n_out, refs)
    copies = Copies({}, refs[-1])
    buffers = [refs[3 * i : 3 * i + 3] for i in range(len(jobs))]
    for i, job in enumerate(jobs):
        sources, stride, before, after, start, size, keep = job[:7]
        own = (lax.axis_index(ROWS) // stride) % 2
        which = own if keep else 1 - own
        for k in range(before):
            taken = pl.ds((2 * k + which) * after, after)
            for source, buffer in zip(sources, buffers[i]):
                target = buffer.at[pl.ds(k * after, after)]
                copies.load(i, ins[source].at[taken, :, pl.ds(start, size)], target)
    for i, job in enumerate(jobs):
        left, right, total = buffers[i]
        copies.ready(i)
        total[...] = (left[...].astype(F32) + right[...].astype(F32)).astype(BF16)
        place, start = job[7:]
        copies.store(total, outs[place].at[:, :, pl.ds(start, total.shape[-1])])
    copies.finish()


def halves(ways, arrays, n_outs, keep, free=False):
    tall = arrays[0].shape[1]
    jobs, scratch = [], []
    outs = [None] * n_outs
    for sources, stride, before, after, start, size, place, column in ways:
        jobs.append((sources, stride, before, after, start, size, keep, place, column))
        scratch += [((before * after, tall, size), BF16)] * 3
        outs[place] = ((before * after, tall, column + size), BF16)
    inputs = [(array, FREE if free else ANY) for array in arrays]
    body = partial(halves_kernel, tuple(jobs))
    return call(body, "halves", inputs, {}, outs, scratch, 32, 24 if free else 58)


class ScatterSum:
    def __init__(self, kept, came, sent=None):
        self.kept, self.came, self.sent = kept, came, sent

    @staticmethod
    def cores(blocks):
        return ScatterSum(blocks[0], swap(blocks[1], 1))

    @staticmethod
    def exchange(ways, arrays, n_outs, strides, first, free=False):
        arrays = lax.optimization_barrier((arrays, first))[0]
        sent = halves(ways, arrays, n_outs, 0, free)
        came = tuple(swap(part, stride) for part, stride in zip(sent, strides))
        kept = halves(ways, lax.optimization_barrier((arrays, sent))[0], n_outs, 1, free)
        return ScatterSum(tuple(kept), came, sent)

    def second(self, first, free=False):
        half = self.kept.shape[-1] // 2
        ways = (((0, 1), 2, 4, 1, 0, half, 0, 0), ((0, 1), 4, 2, 2, half, half, 1, 0))
        return self.exchange(ways, (self.kept, self.came), 2, (2, 4), first, free)

    def pairs(self):
        return (self.kept[0], self.came[0], self.kept[1], self.came[1])

    def third(self, first):
        half = self.kept[0].shape[-1]
        ways = (((0, 1), 4, 2, 1, 0, half, 0, 0), ((2, 3), 2, 2, 1, 0, half, 1, 0))
        return self.exchange(ways, self.pairs(), 2, (4, 2), first)

    def fourth(self, first, free=False):
        half = self.kept[0].shape[-1]
        ways = tuple(((2 * i, 2 * i + 1), 8, 1, 1, 0, half, 0, i * half) for i in range(2))
        made = self.exchange(ways, self.pairs(), 1, (8,), first, free)
        return ScatterSum(made.kept[0], made.came[0], made.sent)

    def finish(self):
        return (self.kept.astype(F32) + self.came.astype(F32))[0]


def whole_sum(partial_sum):
    return lax.psum_scatter(partial_sum, ROWS, scatter_dimension=0, tiled=True).astype(F32)


def small_sum(values, beside, after):
    if lax.axis_size(ROWS) != 16:
        return lax.psum(values, ROWS)
    for stride, first in zip((1, 2, 4, 8), (*beside, None)):
        values = values + swap(values, stride)
        if first is not None:
            values = after(values, first)
    return values


def on_device(tokens, cotangent, segment_ids, valid_mask, cluster_perm, *params):
    section = lax.axis_index(LAYER)
    is_first = section == 0
    wq, _, wk, wv, _, wo, _, gain1, _, wu, _, wd, _, gain2, _ = params
    width, inner = wu.shape[1:]
    ids = (cluster_perm, segment_ids, valid_mask)
    shapes = shapes_of(width, inner)

    def hop(array, source, target):
        return lax.ppermute(array, LAYER, [(source, target)])

    def after(array, first):
        return lax.optimization_barrier((array, first))[0]

    row0, y0, stats00 = forward(0, 0, tokens, 0, ids, params, None)
    in0 = hop(y0, 0, 1)
    row1, y1, stats01 = forward(0, 1, tokens, 1, ids, params, None)
    in1 = hop(y1, 0, 1)
    row0, out0, stats10, grads0, dx0 = through_and_back(0, in0, cotangent, ids, params, row0)
    cotangent = after(cotangent, dx0)
    g0 = hop(dx0, 1, 0)
    row1, out1, stats11, grads1, dx1 = through_and_back(1, in1, cotangent, ids, params, row1)
    g0 = after(g0, dx1)
    g1 = hop(dx1, 1, 0)
    grads0, (dx0, down_share, up_share, rest_share) = backward(0, g0, 0, params, row0, grads0)
    g1 = after(g1, dx0)

    def at_hbm(*arrays):
        return [(array, ANY) for array in arrays]

    def of(*names):
        return [shapes[name] for name in names]

    totals, parts = gradient_shapes((inner, width), (width, inner))
    plain = len(totals) == 2
    made = call(
        feed_kernel,
        "feed",
        at_hbm(g1)
        + [(gain2, WHOLE)]
        + at_hbm(row1[N2], row1[R2], row1[ACT], down_share, wd, row1[GP], row1[HID], up_share),
        {0: grads1[DFFN], 1: grads1[DUP], 2: grads1[SUMS_A]},
        of(DFFN, DUP, SUMS_A, WIDE) + parts,
        of(G, N2, R2, WIDE, SUMS_A, ACT, DFFN, WD, GP, HID, DUP, WD, WU) + totals,
        60,
    )
    _, dup1, sums_a1, wide = made[:4]
    feed_parts = made[4:]
    if not plain:
        feed_sum = ScatterSum.cores(feed_parts)

    made = call(
        middle_kernel,
        "middle",
        at_hbm(dup1, wide, wu) + [(gain1, WHOLE)] + at_hbm(row1[N1], row1[R1], wo, row1[CTX]),
        {0: grads1[DBR], 4: grads1[SUMS_B]},
        of(DBR, WIDE, DCTX, DELTA, SUMS_B),
        of(DUP, WIDE, WU, N1, R1, WO, CTX, DBR, DCTX, DELTA, SUMS_B),
        20,
    )
    dbr1, wide, dctx, delta, sums_b1 = made
    if not plain:
        feed_sum = feed_sum.second(dctx, True)
        dctx = after(dctx, feed_sum.kept)

    totals, parts = gradient_shapes((width, 4 * width))
    made = call(
        attend_kernel,
        "attend",
        at_hbm(row1[QKV], dctx, *(row1[name] for name in (KID, QID, LSE)), delta)
        + at_hbm(row1[X], row1[CTX], dbr1, rest_share, wide, wq, wk, wv),
        {0: grads1[DQKV], 1: grads1[SUMS_C]},
        of(DQKV, SUMS_C, DX) + parts,
        of(*ATTEND_HELD) + totals,
        40,
    )
    _, sums_c1, dx1 = made[:3]
    came = []
    if plain:
        w_down, w_up, w_rest = (whole_sum(part) for part in (*feed_parts, made[3]))
        w_out, w_query, w_key, w_value = jnp.split(w_rest, 4, axis=1)
    else:
        feed_sum = feed_sum.third(dx1)
        rest_sum = ScatterSum.cores(after(tuple(made[3:]), feed_sum.sent))
        came.append(rest_sum.came)
        rest_sum = rest_sum.second(feed_sum.sent)
        dx1 = after(dx1, rest_sum.sent)
        came.append(rest_sum.came)
        feed_sum = feed_sum.fourth(rest_sum.sent)
        rest_sum = rest_sum.third(feed_sum.sent)
        came.append(rest_sum.came)
        rest_sum = rest_sum.fourth(rest_sum.sent, True)
        w_feed, w_rest = feed_sum.finish(), rest_sum.finish()
        tall = inner // 16
        w_down = w_feed[:tall]
        w_up = jnp.concatenate(jnp.split(w_feed[tall:], N_TILES, axis=0), axis=1)
        w_out, w_query, w_key, w_value = jnp.split(w_rest, 4, axis=0)

    sums_a1, sums_b1, sums_c1 = (after(array, dx1) for array in (sums_a1, sums_b1, sums_c1))
    stats10 = after(stats10, dx1)
    sum_a = (grads0[SUMS_A] + sums_a1).reshape(4, 8, inner).sum(axis=1)
    sum_b = (grads0[SUMS_B] + sums_b1).reshape(3, 8, width).sum(axis=1)
    sum_c = (grads0[SUMS_C] + sums_c1).reshape(2, 8, width).sum(axis=1)
    stats = jnp.where(is_first, stats00 + stats01, stats10 + stats11)
    stats = stats.reshape(3, 8 * width).sum(axis=1)
    count = jnp.sum(valid_mask.astype(F32))
    pieces = [sum_a[:3, :width].reshape(-1), sum_b.reshape(-1), sum_c.reshape(-1), sum_a[3]]
    base = 8 * width + inner
    spare = -(base + 4) % (8 * LANES)
    tail = jnp.concatenate([stats, jnp.broadcast_to(count, (1,)), jnp.zeros((spare,), F32)])
    small = jnp.concatenate(pieces + [tail]).reshape(-1, LANES)
    small = small_sum(small, came, after).reshape(-1)
    shares = lax.axis_size(ROWS)
    me = lax.axis_index(ROWS)

    def small_part(place, size):
        own = size // shares
        return lax.dynamic_slice_in_dim(small, place * width + me * own, own, 0)[None]

    gain2_sum, shift2_sum, down_bias, gain1_sum, shift1_sum, out_bias, query_bias, value_bias = (
        small_part(i, width) for i in range(8)
    )
    up_bias = small_part(8, inner)
    root_means = jnp.sqrt(small[base : base + 3] / (small[base + 3] * width))[None, :]

    half = width // 2
    dx0, out0, out1 = (after(array, dx1) for array in (dx0, out0, out1))
    outgoing = jnp.concatenate(
        [
            jnp.where(is_first, grad[:, half:], made[:, :half])
            for grad, made in ((dx0, out0), (dx1, out1))
        ]
    )
    arrived = lax.ppermute(outgoing, LAYER, [(0, 1), (1, 0)])
    if not plain:
        arrived = after(arrived, rest_sum.sent)
    block_own = jnp.concatenate([out0[:, half:], out1[:, half:]])
    grad_own = jnp.concatenate([dx0[:, :half], dx1[:, :half]])
    block_part = jnp.where(is_first, arrived, block_own)
    grad_part = jnp.where(is_first, grad_own, arrived)
    return (
        block_part,
        grad_part,
        w_query[None],
        query_bias,
        w_key[None],
        w_value[None],
        value_bias,
        w_out[None],
        out_bias,
        gain1_sum,
        shift1_sum,
        w_up[None],
        up_bias,
        w_down[None],
        down_bias,
        gain2_sum,
        shift2_sum,
        root_means,
    )


def solution(mesh):
    by_layer = P(LAYER, None)
    matrix = P(LAYER, None, None)
    share = P(LAYER, ROWS)
    matrix_share = P(LAYER, ROWS, None)
    rows = P(ROWS, None)
    vectors = {1, 4, 6, 7, 8, 10, 12, 13, 14}
    matrices = {2, 4, 5, 7, 11, 13}
    return jax.shard_map(
        on_device,
        mesh=mesh,
        in_specs=(rows, rows, rows, rows, P(LAYER, ROWS, None, None))
        + tuple(by_layer if i in vectors else matrix for i in range(15)),
        out_specs=(P(ROWS, LAYER), P(ROWS, LAYER))
        + tuple(matrix_share if i in matrices else share for i in range(2, 17))
        + (P(LAYER, None),),
        check_vma=False,
    )
```
